32 devices in a mesh: fsdp: 8 (over z, y), tensor: 4 (over x, core).
Axes of the slice: x: 2, y: 2, z: 4, core: 2. Of those that a mesh axis runs over, the one named last changes fastest.
Arguments:
- context: bfloat16 [2048, 4096], P('fsdp', 'tensor'), may hold values from -6 to 6
- cotangent: bfloat16 [2048, 8192], P('fsdp', 'tensor'), may hold values from -0.125 to 0.125
- block_table: int32 [4, 128], P('tensor'), may hold values from 0 to 127, each once within a row
- left_stat: float32 [4, 128, 256, 256], P('tensor', 'fsdp'), may hold values from -1 to 5, as said below
- right_stat: float32 [4, 128, 256, 256], P('tensor', 'fsdp'), may hold values from -1 to 5, as said below
- root_left: float32 [4, 128, 256, 256], P('tensor', 'fsdp'), may hold values from -1 to 5, as said below
- root_right: float32 [4, 128, 256, 256], P('tensor', 'fsdp'), may hold values from -1 to 5, as said below
- second_moment: float32 [4, 128, 256, 256], P('tensor', 'fsdp'), may hold values from 0.3 to 3
Outputs:
- left_new: float32 [4, 128, 256, 256], P('tensor', 'fsdp')
- right_new: float32 [4, 128, 256, 256], P('tensor', 'fsdp')
- second_new: float32 [4, 128, 256, 256], P('tensor', 'fsdp')
- search_direction: bfloat16 [4, 1024, 8192], P('tensor', 'fsdp')
The draws below stay inside these ranges and needn't reach their ends.
Inputs may be any that keep to these rules, and one draw needn't show every extreme that they name: Each row of block_table names every block 0 to 127 once. `left_stat`: symmetric, with positive diagonal. `right_stat`: symmetric, with positive diagonal. `root_left`: symmetric, with positive diagonal. `root_right`: symmetric, with positive diagonal.
All inputs are finite; a program needn't handle non-finite values.
Results may differ from the reference program's by a relative error of at most 0.017.
Values may be sent and summed in bfloat16 or wider, within the bound.
No kernel may reach another device: no remote copies, remote signals or barrier semaphores. Data moves between devices by JAX's collectives and lax.ppermute only.
A program may use at most 128 MiB of HBM per device.

```python
import math
import jax
import jax.numpy as jnp
from jax import lax

D = 8192
BLOCK = 256
TOK_DEV = 256
HD = 4096
TOKENS = 2048
BAND = 1024
COLB = 32
NBT = 128
N_FSDP = 8
N_TENSOR = 4


def symmetric_blocks(base_key, spread):
    first_key, second_key = jax.random.split(base_key)
    full_shape = (N_TENSOR, NBT, BLOCK, BLOCK)
    jitter = jnp.clip(jax.random.normal(first_key, full_shape, jnp.float32), -3.0, 3.0)
    jitter = (jitter + jnp.swapaxes(jitter, -1, -2)) * (spread / math.sqrt(2.0 * BLOCK))
    log_diag = jax.random.uniform(second_key, full_shape[:-1], jnp.float32, math.log(0.5), math.log(4.0))
    identity = jnp.eye(BLOCK, dtype=jnp.float32)
    return jitter + jnp.exp(log_diag)[..., None] * identity


def draw_left_stat(key, part):
    return symmetric_blocks(jax.random.fold_in(key, 11), 0.5)


def draw_right_stat(key, part):
    return symmetric_blocks(jax.random.fold_in(key, 23), 0.5)


def draw_root_left(key, part):
    return symmetric_blocks(jax.random.fold_in(key, 37), 0.6)


def draw_root_right(key, part):
    return symmetric_blocks(jax.random.fold_in(key, 41), 0.6)


def block_scale(stream_key, shape, cuts, smallest, top_value):
    factor_of = 1.0
    for axis_at, shards_of in cuts:
        heights = jax.random.uniform(jax.random.fold_in(jax.random.fold_in(stream_key, 6), axis_at), (shards_of,), jnp.float32, smallest / len(cuts), top_value / len(cuts))
        factor_of = factor_of * jnp.repeat(jnp.exp(heights), shape[axis_at] // shards_of).reshape((-1,) + (1,) * (len(shape) - 1 - axis_at))
    return factor_of


def scatter_about(own_key, shape, width, bound, shards=(), kind=jnp.bfloat16):
    factor_of = block_scale(own_key, shape, shards, -0.22, 0.18) if shards else 1.0
    result = jax.random.normal(own_key, shape, jnp.float32) * width * factor_of
    return jnp.minimum(jnp.maximum(result, -bound), bound).astype(kind)


def setup_inputs(seed: int = 0) -> dict:
    keys = jax.random.split(jax.random.key(seed), 9)
    context = scatter_about(keys[0], (TOKENS, HD), 1.0, 6.0, ((0, 8), (1, 4)))
    cotangent = scatter_about(keys[1], (TOKENS, D), TOKENS ** -0.5, 0.125, ((0, 8), (1, 4)))
    block_table = jax.vmap(lambda own: jax.random.permutation(own, NBT))(jax.random.split(keys[2], N_TENSOR)).reshape((N_TENSOR, NBT)).astype(jnp.int32)
    left_stat = draw_left_stat(jax.random.fold_in(keys[8], 71), 0)
    right_stat = draw_right_stat(jax.random.fold_in(keys[8], 71), 0)
    root_left = draw_root_left(jax.random.fold_in(keys[8], 71), 0)
    root_right = draw_root_right(jax.random.fold_in(keys[8], 71), 0)
    second_moment = jnp.clip(jnp.exp(math.log(3.0) - 2.3025851 * jax.random.uniform(keys[7], (N_TENSOR, NBT, BLOCK, BLOCK), jnp.float32) ** block_scale(keys[7], (N_TENSOR, NBT, BLOCK, BLOCK), ((0, 4), (1, 8)), -0.2, 0.2)), 0.3, 3.0)
    return {"context": context, "cotangent": cotangent, "block_table": block_table, "left_stat": left_stat, "right_stat": right_stat, "root_left": root_left, "root_right": root_right, "second_moment": second_moment}


decay_rate = 0.95

def reference(context, cotangent, block_table, left_stat, right_stat, root_left, root_right, second_moment):
    ctx_groups = context.reshape(N_FSDP, TOK_DEV, HD)
    cot_groups = cotangent.reshape(N_FSDP, TOK_DEV, D)

    def add_group(running, inputs):
        partial_sum = jnp.dot(inputs[0].T, inputs[1], preferred_element_type=jnp.float32).astype(jnp.bfloat16)
        partial_sum = lax.optimization_barrier(partial_sum)
        return (running + partial_sum.astype(jnp.float32), None)
    gradient, _ = lax.scan(add_group, jnp.zeros((HD, D), jnp.float32), (ctx_groups, cot_groups))
    natural = gradient.reshape(N_TENSOR, BAND // BLOCK, BLOCK, COLB, BLOCK)
    natural = natural.transpose(0, 1, 3, 2, 4).reshape(N_TENSOR, NBT, BLOCK, BLOCK)
    grads = jnp.take_along_axis(natural, block_table.astype(jnp.int32)[:, :, None, None], axis=1)
    highest = lax.Precision.HIGHEST
    gram_left = jnp.einsum('tsij,tskj->tsik', grads, grads, precision=highest)
    gram_right = jnp.einsum('tsji,tsjk->tsik', grads, grads, precision=highest)
    left_new = decay_rate * left_stat + (1.0 - decay_rate) * gram_left / BLOCK
    right_new = decay_rate * right_stat + (1.0 - decay_rate) * gram_right / BLOCK
    second_new = decay_rate * second_moment + (1.0 - decay_rate) * grads * grads
    adam_step = grads / (jnp.sqrt(second_new) + 1e-08)
    shaped = jnp.einsum('tsij,tsjk->tsik', root_left, grads, precision=highest)
    shaped = jnp.einsum('tsij,tsjk->tsik', shaped, root_right, precision=highest)
    graft_ratio = jnp.sqrt(lax.optimization_barrier(jnp.sum(adam_step * adam_step, axis=(2, 3)))) / jnp.sqrt(lax.optimization_barrier(jnp.sum(shaped * shaped, axis=(2, 3))) + 1e-06)
    direction = (shaped * graft_ratio[:, :, None, None]).astype(jnp.bfloat16)
    band_index = jnp.arange(N_TENSOR).astype(jnp.int32)[:, None]
    placed = jnp.zeros((N_TENSOR, NBT, BLOCK, BLOCK), jnp.bfloat16)
    placed = placed.at[band_index, block_table.astype(jnp.int32)].set(direction)
    placed = placed.reshape(N_TENSOR, BAND // BLOCK, COLB, BLOCK, BLOCK).transpose(0, 1, 3, 2, 4)
    search_direction = placed.reshape(N_TENSOR, BAND, D)
    return (left_new, right_new, second_new, search_direction)
```

```python
import functools

import jax
import jax.numpy as jnp
from jax import lax
from jax.experimental import pallas as pl
from jax.experimental.pallas import tpu as pltpu
from jax.sharding import PartitionSpec as P

decay_rate = 0.95
MIB = 1024 * 1024


def general_plan(
    context, cotangent, block_table, left_stat, right_stat, root_left, root_right, second_moment
):
    full_cot = lax.all_gather(cotangent, "tensor", axis=1, tiled=True)
    tokens_here, band_rows = context.shape
    model_width = full_cot.shape[1]
    block_size = left_stat.shape[-1]
    slot_count = left_stat.shape[1]
    groups = lax.axis_size("fsdp")
    position = lax.axis_index("fsdp")
    owner_table = block_table[0]
    col_bands = model_width // block_size
    strip_rows = band_rows // groups
    per_band = block_size // strip_rows
    my_blocks = lax.dynamic_slice_in_dim(owner_table, position * slot_count, slot_count)
    ctx_bands = context.reshape(tokens_here, band_rows // block_size, block_size)
    cot_bands = full_cot.reshape(tokens_here, col_bands, block_size)
    left_part = jnp.take(ctx_bands, owner_table // col_bands, axis=1)
    right_part = jnp.take(cot_bands, owner_table % col_bands, axis=1)
    blocks = jnp.einsum("tnb,tnc->nbc", left_part, right_part, preferred_element_type=jnp.float32)
    gradient = lax.psum_scatter(
        blocks.reshape(slot_count * block_size * lax.axis_size("fsdp"), block_size).astype(
            jnp.bfloat16
        ),
        "fsdp",
        scatter_dimension=0,
        tiled=True,
    ).astype(jnp.float32)
    gradient = gradient.reshape(slot_count, block_size, block_size)
    highest = lax.Precision.HIGHEST
    gram_left = jnp.einsum("sij,skj->sik", gradient, gradient, precision=highest)
    gram_right = jnp.einsum("sji,sjk->sik", gradient, gradient, precision=highest)
    left_new = decay_rate * left_stat[0] + (1.0 - decay_rate) * gram_left / block_size
    right_new = decay_rate * right_stat[0] + (1.0 - decay_rate) * gram_right / block_size
    second_new = decay_rate * second_moment[0] + (1.0 - decay_rate) * gradient * gradient
    adam_step = gradient / (jnp.sqrt(second_new) + 1e-08)
    shaped = jnp.einsum("sij,sjk->sik", root_left[0], gradient, precision=highest)
    shaped = jnp.einsum("sij,sjk->sik", shaped, root_right[0], precision=highest)
    graft_ratio = jnp.sqrt(jnp.sum(adam_step * adam_step, axis=(1, 2))) / jnp.sqrt(
        jnp.sum(shaped * shaped, axis=(1, 2)) + 1e-06
    )
    direction = (shaped * graft_ratio[:, None, None]).astype(jnp.bfloat16)
    by_strip = direction.reshape(slot_count, per_band, strip_rows, block_size)
    targets = jnp.arange(groups, dtype=jnp.int32)
    chosen = jnp.take(by_strip, targets % per_band, axis=1)
    keep_mask = ((my_blocks // col_bands)[:, None] == (targets // per_band)[None, :]).astype(
        jnp.bfloat16
    )
    outgoing_rows = jnp.swapaxes(chosen * keep_mask[:, :, None, None], 0, 1)
    returned = lax.all_to_all(outgoing_rows, "fsdp", split_axis=0, concat_axis=0, tiled=True)
    wanted = position // per_band * col_bands + jnp.arange(col_bands, dtype=jnp.int32)
    slot_ids = jnp.arange(owner_table.shape[0], dtype=jnp.int32)
    located = jnp.sum(
        jnp.where(owner_table[None, :] == wanted[:, None], slot_ids[None, :], 0), axis=1
    )
    flat_pieces = returned.reshape(groups * slot_count, strip_rows, block_size)
    pieces = jnp.take(flat_pieces, located, axis=0)
    result = jnp.swapaxes(pieces, 0, 1).reshape(strip_rows, model_width)
    return (left_new[None], right_new[None], second_new[None], result[None])


def swap(value, axis, offset):
    count = lax.axis_size(axis)
    return lax.ppermute(value, axis, [(i, i ^ offset) for i in range(count)])


def strip_kernel(groups, strip, meta, cot_ref, *refs):
    outs, turned = refs[:groups], refs[groups]
    position = meta[0]
    turned[...] = cot_ref[...].T
    for k in range(groups):
        start = pl.multiple_of((position ^ k) * strip, strip)
        outs[k][0] = turned[pl.ds(start, strip), :]


def cot_strips(meta, cotangent, groups, block):
    tokens, width = cotangent.shape
    bands, strip = width // block, block // groups
    return pl.pallas_call(
        functools.partial(strip_kernel, groups, strip),
        grid_spec=pltpu.PrefetchScalarGridSpec(
            num_scalar_prefetch=1,
            grid=(bands,),
            in_specs=[pl.BlockSpec((tokens, block), lambda c, meta: (0, c))],
            out_specs=[pl.BlockSpec((1, strip, tokens), lambda c, meta: (c, 0, 0))] * groups,
            scratch_shapes=[pltpu.VMEM((block, tokens), jnp.bfloat16)],
        ),
        out_shape=[jax.ShapeDtypeStruct((bands, strip, tokens), jnp.bfloat16)] * groups,
        compiler_params=pltpu.CompilerParams(vmem_limit_bytes=16 * MIB),
        cost_estimate=pl.CostEstimate(
            flops=0, bytes_accessed=4 * tokens * width, transcendentals=0
        ),
        name="cot_strips",
    )(meta, cotangent)


def gradient_kernel(groups, ranks, slots, bands, strip, block, meta, *refs):
    cots, ctxs = refs[:ranks], refs[ranks : ranks + groups]
    outs = refs[ranks + groups : ranks + 2 * groups]
    lhs, rhs, strips, sems = refs[ranks + 2 * groups :]
    tokens = ctxs[0].shape[0]
    rows = lhs.shape[1]
    position, rank = meta[0], meta[1]
    copies = []
    for k in range(groups):
        copies.append(
            pltpu.make_async_copy(
                ctxs[k], rhs.at[pl.ds(k * tokens, tokens), :], sems.at[ranks * groups + k]
            )
        )
    for t in range(ranks):
        for k in range(groups):
            copies.append(
                pltpu.make_async_copy(
                    cots[t].at[k],
                    lhs.at[t, :, pl.ds(k * tokens, tokens)],
                    sems.at[t * groups + k],
                )
            )
    for copy in copies:
        copy.start()
    for copy in copies:
        copy.wait()
    for t in range(ranks):
        strips[pl.ds(t * rows, rows), :] = jnp.dot(
            lhs[t], rhs[...], preferred_element_type=jnp.float32
        ).astype(jnp.bfloat16)
    own_bands = bands // ranks

    def place(s, carry):
        for k in range(groups):
            block_id = meta[2 + (position ^ k) * slots + s]
            row_band, col_band = lax.div(block_id, bands), lax.rem(block_id, bands)
            piece = lax.div(col_band, own_bands) ^ rank
            start = piece * rows + lax.rem(col_band, own_bands) * strip
            outs[k][s] = strips[
                pl.ds(pl.multiple_of(start, strip), strip),
                pl.ds(pl.multiple_of(row_band * block, block), block),
            ]
        return carry

    lax.fori_loop(0, slots, place, 0)


def gradient_strips(meta, cots, ctxs, slots, bands, block):
    groups, ranks = len(ctxs), len(cots)
    tokens, band_rows = ctxs[0].shape
    rows, strip = cots[0].shape[1], block // groups
    flops = 2 * ranks * rows * groups * tokens * band_rows
    return pl.pallas_call(
        functools.partial(gradient_kernel, groups, ranks, slots, bands, strip, block),
        grid_spec=pltpu.PrefetchScalarGridSpec(
            num_scalar_prefetch=1,
            grid=(),
            in_specs=[pl.BlockSpec(memory_space=pl.ANY)] * (ranks + groups),
            out_specs=[pl.BlockSpec(memory_space=pltpu.VMEM)] * groups,
            scratch_shapes=[
                pltpu.VMEM((ranks, rows, groups * tokens), jnp.bfloat16),
                pltpu.VMEM((groups * tokens, band_rows), jnp.bfloat16),
                pltpu.VMEM((ranks * rows, band_rows), jnp.bfloat16),
                pltpu.SemaphoreType.DMA(((ranks + 1) * groups,)),
            ],
        ),
        out_shape=[jax.ShapeDtypeStruct((slots, strip, block), jnp.bfloat16)] * groups,
        compiler_params=pltpu.CompilerParams(vmem_limit_bytes=48 * MIB),
        cost_estimate=pl.CostEstimate(
            flops=flops,
            bytes_accessed=2 * groups * (ranks * rows * tokens + tokens * band_rows + slots * strip * block),
            transcendentals=0,
        ),
        name="gradient_strips",
    )(meta, *cots, *ctxs)


def gather_block(groups, strip, position, grads, turned):
    for k in range(groups):
        start = pl.multiple_of((position ^ k) * strip, strip)
        turned[pl.ds(start, strip), :] = grads[k][0]


def direction_kernel(groups, strip, sub, meta, second_ref, left_ref, right_ref, *refs):
    grads, outs, turned, rows = refs[:groups], refs[groups : 2 * groups], refs[-2], refs[-1]
    position = meta[0]
    gather_block(groups, strip, position, grads, turned)
    grad_bf16 = turned[...].T
    grad = grad_bf16.astype(jnp.float32)
    second = decay_rate * second_ref[0, 0] + (1.0 - decay_rate) * grad * grad
    adam = grad / (jnp.sqrt(second) + 1e-08)
    half = jnp.dot(
        left_ref[0, 0].astype(jnp.bfloat16), grad_bf16, preferred_element_type=jnp.float32
    )
    shaped = jnp.dot(
        half.astype(jnp.bfloat16),
        right_ref[0, 0].astype(jnp.bfloat16),
        preferred_element_type=jnp.float32,
    )
    adam_sum = jnp.sum(adam * adam, keepdims=True)
    shaped_sum = jnp.sum(shaped * shaped, keepdims=True)
    ratio = jnp.sqrt(adam_sum) / jnp.sqrt(shaped_sum + 1e-06)
    rows[...] = (shaped * ratio).astype(jnp.bfloat16)
    halves = outs[0].shape[1]
    for k in range(groups):
        for h in range(halves):
            start = pl.multiple_of(h * groups * sub + (position ^ k) * sub, sub)
            outs[k][0, h] = rows[pl.ds(start, sub), :]


def directions(meta, grads, second, root_left, root_right, halves, sub):
    groups = len(grads)
    slots, strip, block = grads[0].shape
    stat = pl.BlockSpec((1, 1, block, block), lambda s, meta: (0, s, 0, 0))
    return pl.pallas_call(
        functools.partial(direction_kernel, groups, strip, sub),
        grid_spec=pltpu.PrefetchScalarGridSpec(
            num_scalar_prefetch=1,
            grid=(slots,),
            in_specs=[stat] * 3
            + [pl.BlockSpec((1, strip, block), lambda s, meta: (s, 0, 0))] * groups,
            out_specs=[pl.BlockSpec((1, halves, sub, block), lambda s, meta: (s, 0, 0, 0))]
            * groups,
            scratch_shapes=[
                pltpu.VMEM((block, block), jnp.bfloat16),
                pltpu.VMEM((block, block), jnp.bfloat16),
            ],
        ),
        out_shape=[jax.ShapeDtypeStruct((slots, halves, sub, block), jnp.bfloat16)] * groups,
        compiler_params=pltpu.CompilerParams(vmem_limit_bytes=32 * MIB),
        cost_estimate=pl.CostEstimate(
            flops=4 * slots * block**3,
            bytes_accessed=16 * slots * block * block,
            transcendentals=0,
        ),
        name="directions",
    )(meta, second, root_left, root_right, *grads)


def statistics_kernel(groups, strip, meta, left_ref, right_ref, second_ref, *refs):
    grads = refs[:groups]
    left_out, right_out, second_out, turned = refs[groups:]
    gather_block(groups, strip, meta[0], grads, turned)
    block = turned.shape[0]
    grad_t = turned[...]
    grad_bf16 = grad_t.T
    grad = grad_bf16.astype(jnp.float32)
    gram_left = jnp.dot(grad_bf16, grad_t, preferred_element_type=jnp.float32)
    gram_right = jnp.dot(grad_t, grad_bf16, preferred_element_type=jnp.float32)
    left_out[0, 0] = decay_rate * left_ref[0, 0] + (1.0 - decay_rate) * gram_left / block
    right_out[0, 0] = decay_rate * right_ref[0, 0] + (1.0 - decay_rate) * gram_right / block
    second_out[0, 0] = decay_rate * second_ref[0, 0] + (1.0 - decay_rate) * grad * grad


def statistics(meta, grads, left_stat, right_stat, second):
    groups = len(grads)
    slots, strip, block = grads[0].shape
    stat = pl.BlockSpec((1, 1, block, block), lambda s, meta: (0, s, 0, 0))
    return pl.pallas_call(
        functools.partial(statistics_kernel, groups, strip),
        grid_spec=pltpu.PrefetchScalarGridSpec(
            num_scalar_prefetch=1,
            grid=(slots,),
            in_specs=[stat] * 3
            + [pl.BlockSpec((1, strip, block), lambda s, meta: (s, 0, 0))] * groups,
            out_specs=[stat] * 3,
            scratch_shapes=[pltpu.VMEM((block, block), jnp.bfloat16)],
        ),
        out_shape=[jax.ShapeDtypeStruct(left_stat.shape, jnp.float32)] * 3,
        compiler_params=pltpu.CompilerParams(vmem_limit_bytes=32 * MIB),
        cost_estimate=pl.CostEstimate(
            flops=4 * slots * block**3,
            bytes_accessed=26 * slots * block * block,
            transcendentals=0,
        ),
        name="statistics",
    )(meta, left_stat, right_stat, second, *grads)


def regroup_kernel(groups, slots, bands, halves, meta, *refs):
    pieces, outs, placed = refs[:groups], refs[groups : 2 * groups], refs[-1]
    block = pieces[0].shape[-1]
    position = meta[0]

    def place(s, carry):
        for k in range(groups):
            block_id = meta[2 + (position ^ k) * slots + s]
            row_band, col_band = lax.div(block_id, bands), lax.rem(block_id, bands)
            columns = pl.ds(pl.multiple_of(col_band * block, block), block)
            for h in range(halves):
                placed[(row_band * halves + h) ^ position, :, columns] = pieces[k][s, h]
        return carry

    lax.fori_loop(0, slots, place, 0)
    for k in range(groups):
        outs[k][...] = placed[k]


def regroup(meta, pieces, bands):
    groups = len(pieces)
    slots, halves, sub, block = pieces[0].shape
    return pl.pallas_call(
        functools.partial(regroup_kernel, groups, slots, bands, halves),
        grid_spec=pltpu.PrefetchScalarGridSpec(
            num_scalar_prefetch=1,
            grid=(),
            in_specs=[pl.BlockSpec(memory_space=pltpu.VMEM)] * groups,
            out_specs=[pl.BlockSpec(memory_space=pltpu.VMEM)] * groups,
            scratch_shapes=[pltpu.VMEM((groups, sub, bands * block), jnp.bfloat16)],
        ),
        out_shape=[jax.ShapeDtypeStruct((sub, bands * block), jnp.bfloat16)] * groups,
        compiler_params=pltpu.CompilerParams(vmem_limit_bytes=32 * MIB),
        cost_estimate=pl.CostEstimate(
            flops=0,
            bytes_accessed=4 * groups * sub * bands * block,
            transcendentals=0,
        ),
        name="regroup",
    )(meta, *pieces)


def stack_kernel(groups, meta, *refs):
    pieces, out, sems = refs[:groups], refs[groups], refs[groups + 1]
    sub = pieces[0].shape[0]
    copies = []
    for k in range(groups):
        start = pl.multiple_of((meta[0] ^ k) * sub, sub)
        copies.append(
            pltpu.make_async_copy(pieces[k], out.at[0, pl.ds(start, sub), :], sems.at[k])
        )
    for copy in copies:
        copy.start()
    for copy in copies:
        copy.wait()


def stack_rows(meta, pieces):
    groups = len(pieces)
    sub, width = pieces[0].shape
    return pl.pallas_call(
        functools.partial(stack_kernel, groups),
        grid_spec=pltpu.PrefetchScalarGridSpec(
            num_scalar_prefetch=1,
            grid=(),
            in_specs=[pl.BlockSpec(memory_space=pl.ANY)] * groups,
            out_specs=pl.BlockSpec(memory_space=pl.ANY),
            scratch_shapes=[pltpu.SemaphoreType.DMA((groups,))],
        ),
        out_shape=jax.ShapeDtypeStruct((1, groups * sub, width), jnp.bfloat16),
        cost_estimate=pl.CostEstimate(
            flops=0, bytes_accessed=4 * groups * sub * width, transcendentals=0
        ),
        name="stack_rows",
    )(meta, *pieces)


def exchange(pieces):
    return [pieces[0]] + [swap(pieces[k], "fsdp", k) for k in range(1, len(pieces))]


def strip_plan(
    context, cotangent, block_table, left_stat, right_stat, root_left, root_right, second_moment
):
    groups, ranks = lax.axis_size("fsdp"), lax.axis_size("tensor")
    band_rows = context.shape[1]
    block, slots = left_stat.shape[-1], left_stat.shape[1]
    bands = cotangent.shape[1] * ranks // block
    strip_rows = band_rows // groups
    place = jnp.stack([lax.axis_index("fsdp"), lax.axis_index("tensor")]).astype(jnp.int32)
    meta = jnp.concatenate([place, block_table[0]])

    strips = exchange(cot_strips(meta, cotangent, groups, block))
    ctxs = [context] + [None] * (groups - 1)
    for k in range(groups):
        if k % 2:
            ctxs[k] = swap(ctxs[k - 1], "fsdp", 1)
        elif k:
            ctxs[k] = swap(context, "fsdp", k)
    tokens = context.shape[0]
    cots = [jnp.stack(strips).reshape(groups, -1, tokens)]
    offset = ranks // 2
    by_offset = {0: cots[0]}
    while offset:
        for known in list(by_offset):
            by_offset[known ^ offset] = swap(by_offset[known], "tensor", offset)
        offset //= 2
    cots = [by_offset[t] for t in range(ranks)]

    grads = exchange(gradient_strips(meta, cots, ctxs, slots, bands, block))
    halves, sub = block // strip_rows, strip_rows // groups
    pieces = exchange(
        directions(meta, grads, second_moment, root_left, root_right, halves, sub)
    )
    left_new, right_new, second_new = statistics(
        meta, grads, left_stat, right_stat, second_moment
    )
    rows = exchange(regroup(meta, pieces, bands))
    return (left_new, right_new, second_new, stack_rows(meta, rows))


def per_device(context, cotangent, block_table, left_stat, *rest):
    groups, ranks = lax.axis_size("fsdp"), lax.axis_size("tensor")
    block = left_stat.shape[-1]
    strip_rows = context.shape[1] // groups
    powers = groups & (groups - 1) == 0 and ranks & (ranks - 1) == 0
    even = block % (16 * groups) == 0 and strip_rows % (16 * groups) == 0
    whole = block % strip_rows == 0 and cotangent.shape[1] % block == 0
    plan = strip_plan if powers and even and whole else general_plan
    return plan(context, cotangent, block_table, left_stat, *rest)


def solution(mesh):
    return jax.shard_map(
        per_device,
        mesh=mesh,
        in_specs=(
            P("fsdp", "tensor"),
            P("fsdp", "tensor"),
            P("tensor", None),
            P("tensor", "fsdp", None, None),
            P("tensor", "fsdp", None, None),
            P("tensor", "fsdp", None, None),
            P("tensor", "fsdp", None, None),
            P("tensor", "fsdp", None, None),
        ),
        out_specs=(
            P("tensor", "fsdp", None, None),
            P("tensor", "fsdp", None, None),
            P("tensor", "fsdp", None, None),
            P("tensor", "fsdp", None),
        ),
        check_vma=False,
    )
```

```python
import functools

import jax
import jax.numpy as jnp
from jax import lax
from jax.experimental import pallas as pl
from jax.experimental.pallas import tpu as pltpu
from jax.sharding import PartitionSpec as P

decay_rate = 0.95
MIB = 1024 * 1024


def general_plan(
    context, cotangent, block_table, left_stat, right_stat, root_left, root_right, second_moment
):
    full_cot = lax.all_gather(cotangent, "tensor", axis=1, tiled=True)
    tokens_here, band_rows = context.shape
    model_width = full_cot.shape[1]
    block_size = left_stat.shape[-1]
    slot_count = left_stat.shape[1]
    groups = lax.axis_size("fsdp")
    position = lax.axis_index("fsdp")
    owner_table = block_table[0]
    col_bands = model_width // block_size
    strip_rows = band_rows // groups
    per_band = block_size // strip_rows
    my_blocks = lax.dynamic_slice_in_dim(owner_table, position * slot_count, slot_count)
    ctx_bands = context.reshape(tokens_here, band_rows // block_size, block_size)
    cot_bands = full_cot.reshape(tokens_here, col_bands, block_size)
    left_part = jnp.take(ctx_bands, owner_table // col_bands, axis=1)
    right_part = jnp.take(cot_bands, owner_table % col_bands, axis=1)
    blocks = jnp.einsum("tnb,tnc->nbc", left_part, right_part, preferred_element_type=jnp.float32)
    gradient = lax.psum_scatter(
        blocks.reshape(slot_count * block_size * lax.axis_size("fsdp"), block_size).astype(
            jnp.bfloat16
        ),
        "fsdp",
        scatter_dimension=0,
        tiled=True,
    ).astype(jnp.float32)
    gradient = gradient.reshape(slot_count, block_size, block_size)
    highest = lax.Precision.HIGHEST
    gram_left = jnp.einsum("sij,skj->sik", gradient, gradient, precision=highest)
    gram_right = jnp.einsum("sji,sjk->sik", gradient, gradient, precision=highest)
    left_new = decay_rate * left_stat[0] + (1.0 - decay_rate) * gram_left / block_size
    right_new = decay_rate * right_stat[0] + (1.0 - decay_rate) * gram_right / block_size
    second_new = decay_rate * second_moment[0] + (1.0 - decay_rate) * gradient * gradient
    adam_step = gradient / (jnp.sqrt(second_new) + 1e-08)
    shaped = jnp.einsum("sij,sjk->sik", root_left[0], gradient, precision=highest)
    shaped = jnp.einsum("sij,sjk->sik", shaped, root_right[0], precision=highest)
    graft_ratio = jnp.sqrt(jnp.sum(adam_step * adam_step, axis=(1, 2))) / jnp.sqrt(
        jnp.sum(shaped * shaped, axis=(1, 2)) + 1e-06
    )
    direction = (shaped * graft_ratio[:, None, None]).astype(jnp.bfloat16)
    by_strip = direction.reshape(slot_count, per_band, strip_rows, block_size)
    targets = jnp.arange(groups, dtype=jnp.int32)
    chosen = jnp.take(by_strip, targets % per_band, axis=1)
    keep_mask = ((my_blocks // col_bands)[:, None] == (targets // per_band)[None, :]).astype(
        jnp.bfloat16
    )
    outgoing_rows = jnp.swapaxes(chosen * keep_mask[:, :, None, None], 0, 1)
    returned = lax.all_to_all(outgoing_rows, "fsdp", split_axis=0, concat_axis=0, tiled=True)
    wanted = position // per_band * col_bands + jnp.arange(col_bands, dtype=jnp.int32)
    slot_ids = jnp.arange(owner_table.shape[0], dtype=jnp.int32)
    located = jnp.sum(
        jnp.where(owner_table[None, :] == wanted[:, None], slot_ids[None, :], 0), axis=1
    )
    flat_pieces = returned.reshape(groups * slot_count, strip_rows, block_size)
    pieces = jnp.take(flat_pieces, located, axis=0)
    result = jnp.swapaxes(pieces, 0, 1).reshape(strip_rows, model_width)
    return (left_new[None], right_new[None], second_new[None], result[None])


def swap(value, axis, offset):
    count = lax.axis_size(axis)
    return lax.ppermute(value, axis, [(i, i ^ offset) for i in range(count)])


def strip_kernel(groups, strip, meta, cot_ref, *refs):
    outs, turned = refs[:groups], refs[groups]
    position = meta[0]
    turned[...] = cot_ref[...].T
    for k in range(groups):
        start = pl.multiple_of((position ^ k) * strip, strip)
        outs[k][0] = turned[pl.ds(start, strip), :]


def cot_strips(meta, cotangent, groups, block):
    tokens, width = cotangent.shape
    bands, strip = width // block, block // groups
    return pl.pallas_call(
        functools.partial(strip_kernel, groups, strip),
        grid_spec=pltpu.PrefetchScalarGridSpec(
            num_scalar_prefetch=1,
            grid=(bands,),
            in_specs=[pl.BlockSpec((tokens, block), lambda c, meta: (0, c))],
            out_specs=[pl.BlockSpec((1, strip, tokens), lambda c, meta: (c, 0, 0))] * groups,
            scratch_shapes=[pltpu.VMEM((block, tokens), jnp.bfloat16)],
        ),
        out_shape=[jax.ShapeDtypeStruct((bands, strip, tokens), jnp.bfloat16)] * groups,
        compiler_params=pltpu.CompilerParams(vmem_limit_bytes=16 * MIB),
        cost_estimate=pl.CostEstimate(
            flops=0, bytes_accessed=4 * tokens * width, transcendentals=0
        ),
        name="cot_strips",
    )(meta, cotangent)


def gradient_kernel(groups, ranks, slots, bands, strip, block, meta, *refs):
    cots, ctxs = refs[:ranks], refs[ranks : ranks + groups]
    outs = refs[ranks + groups : ranks + 2 * groups]
    lhs, rhs, strips, sems = refs[ranks + 2 * groups :]
    tokens = ctxs[0].shape[0]
    rows = lhs.shape[1]
    position, rank = meta[0], meta[1]
    copies = []
    for k in range(groups):
        copies.append(
            pltpu.make_async_copy(
                ctxs[k], rhs.at[pl.ds(k * tokens, tokens), :], sems.at[ranks * groups + k]
            )
        )
    for t in range(ranks):
        for k in range(groups):
            copies.append(
                pltpu.make_async_copy(
                    cots[t].at[k],
                    lhs.at[t, :, pl.ds(k * tokens, tokens)],
                    sems.at[t * groups + k],
                )
            )
    for copy in copies:
        copy.start()
    for copy in copies:
        copy.wait()
    for t in range(ranks):
        strips[pl.ds(t * rows, rows), :] = jnp.dot(
            lhs[t], rhs[...], preferred_element_type=jnp.float32
        ).astype(jnp.bfloat16)
    own_bands = bands // ranks

    def place(s, carry):
        for k in range(groups):
            block_id = meta[2 + (position ^ k) * slots + s]
            row_band, col_band = lax.div(block_id, bands), lax.rem(block_id, bands)
            piece = lax.div(col_band, own_bands) ^ rank
            start = piece * rows + lax.rem(col_band, own_bands) * strip
            outs[k][s] = strips[
                pl.ds(pl.multiple_of(start, strip), strip),
                pl.ds(pl.multiple_of(row_band * block, block), block),
            ]
        return carry

    lax.fori_loop(0, slots, place, 0)


def gradient_strips(meta, cots, ctxs, slots, bands, block):
    groups, ranks = len(ctxs), len(cots)
    tokens, band_rows = ctxs[0].shape
    rows, strip = cots[0].shape[1], block // groups
    flops = 2 * ranks * rows * groups * tokens * band_rows
    return pl.pallas_call(
        functools.partial(gradient_kernel, groups, ranks, slots, bands, strip, block),
        grid_spec=pltpu.PrefetchScalarGridSpec(
            num_scalar_prefetch=1,
            grid=(),
            in_specs=[pl.BlockSpec(memory_space=pl.ANY)] * (ranks + groups),
            out_specs=[pl.BlockSpec(memory_space=pltpu.VMEM)] * groups,
            scratch_shapes=[
                pltpu.VMEM((ranks, rows, groups * tokens), jnp.bfloat16),
                pltpu.VMEM((groups * tokens, band_rows), jnp.bfloat16),
                pltpu.VMEM((ranks * rows, band_rows), jnp.bfloat16),
                pltpu.SemaphoreType.DMA(((ranks + 1) * groups,)),
            ],
        ),
        out_shape=[jax.ShapeDtypeStruct((slots, strip, block), jnp.bfloat16)] * groups,
        compiler_params=pltpu.CompilerParams(vmem_limit_bytes=48 * MIB),
        cost_estimate=pl.CostEstimate(
            flops=flops,
            bytes_accessed=2 * groups * (ranks * rows * tokens + tokens * band_rows + slots * strip * block),
            transcendentals=0,
        ),
        name="gradient_strips",
    )(meta, *cots, *ctxs)


def gather_block(groups, strip, position, grads, turned):
    for k in range(groups):
        start = pl.multiple_of((position ^ k) * strip, strip)
        turned[pl.ds(start, strip), :] = grads[k][0]


def direction_kernel(groups, strip, halves, meta, second_ref, left_ref, right_ref, *refs):
    grads, outs, turned, rows = refs[:groups], refs[groups : 2 * groups], refs[-2], refs[-1]
    position = meta[0]
    gather_block(groups, strip, position, grads, turned)
    grad_bf16 = turned[...].T
    grad = grad_bf16.astype(jnp.float32)
    second = decay_rate * second_ref[0, 0] + (1.0 - decay_rate) * grad * grad
    adam = grad / (jnp.sqrt(second) + 1e-08)
    half = jnp.dot(
        left_ref[0, 0].astype(jnp.bfloat16), grad_bf16, preferred_element_type=jnp.float32
    )
    shaped = jnp.dot(
        half.astype(jnp.bfloat16),
        right_ref[0, 0].astype(jnp.bfloat16),
        preferred_element_type=jnp.float32,
    )
    adam_sum = jnp.sum(adam * adam, keepdims=True)
    shaped_sum = jnp.sum(shaped * shaped, keepdims=True)
    ratio = jnp.sqrt(adam_sum) / jnp.sqrt(shaped_sum + 1e-06)
    rows[...] = (shaped * ratio).astype(jnp.bfloat16)
    sub = outs[0].shape[1]
    for k in range(groups):
        middle = position ^ k
        half, quarter = lax.rem(middle, halves), lax.div(middle, halves)
        start = (half * (groups // halves) + quarter) * sub
        outs[k][0] = rows[pl.ds(pl.multiple_of(start, sub), sub), :]


def directions(meta, grads, second, root_left, root_right, halves, sub):
    groups = len(grads)
    slots, strip, block = grads[0].shape
    stat = pl.BlockSpec((1, 1, block, block), lambda s, meta: (0, s, 0, 0))
    return pl.pallas_call(
        functools.partial(direction_kernel, groups, strip, halves),
        grid_spec=pltpu.PrefetchScalarGridSpec(
            num_scalar_prefetch=1,
            grid=(slots,),
            in_specs=[stat] * 3
            + [pl.BlockSpec((1, strip, block), lambda s, meta: (s, 0, 0))] * groups,
            out_specs=[pl.BlockSpec((1, sub, block), lambda s, meta: (s, 0, 0))] * groups,
            scratch_shapes=[
                pltpu.VMEM((block, block), jnp.bfloat16),
                pltpu.VMEM((block, block), jnp.bfloat16),
            ],
        ),
        out_shape=[jax.ShapeDtypeStruct((slots, sub, block), jnp.bfloat16)] * groups,
        compiler_params=pltpu.CompilerParams(vmem_limit_bytes=32 * MIB),
        cost_estimate=pl.CostEstimate(
            flops=4 * slots * block**3,
            bytes_accessed=16 * slots * block * block,
            transcendentals=0,
        ),
        name="directions",
    )(meta, second, root_left, root_right, *grads)


def statistics_kernel(groups, strip, meta, left_ref, right_ref, second_ref, *refs):
    grads = refs[:groups]
    left_out, right_out, second_out, turned = refs[groups:]
    gather_block(groups, strip, meta[0], grads, turned)
    block = turned.shape[0]
    grad_t = turned[...]
    grad_bf16 = grad_t.T
    grad = grad_bf16.astype(jnp.float32)
    gram_left = jnp.dot(grad_bf16, grad_t, preferred_element_type=jnp.float32)
    gram_right = jnp.dot(grad_t, grad_bf16, preferred_element_type=jnp.float32)
    left_out[0, 0] = decay_rate * left_ref[0, 0] + (1.0 - decay_rate) * gram_left / block
    right_out[0, 0] = decay_rate * right_ref[0, 0] + (1.0 - decay_rate) * gram_right / block
    second_out[0, 0] = decay_rate * second_ref[0, 0] + (1.0 - decay_rate) * grad * grad


def statistics(meta, grads, left_stat, right_stat, second):
    groups = len(grads)
    slots, strip, block = grads[0].shape
    stat = pl.BlockSpec((1, 1, block, block), lambda s, meta: (0, s, 0, 0))
    return pl.pallas_call(
        functools.partial(statistics_kernel, groups, strip),
        grid_spec=pltpu.PrefetchScalarGridSpec(
            num_scalar_prefetch=1,
            grid=(slots,),
            in_specs=[stat] * 3
            + [pl.BlockSpec((1, strip, block), lambda s, meta: (s, 0, 0))] * groups,
            out_specs=[stat] * 3,
            scratch_shapes=[pltpu.VMEM((block, block), jnp.bfloat16)],
        ),
        out_shape=[jax.ShapeDtypeStruct(left_stat.shape, jnp.float32)] * 3,
        compiler_params=pltpu.CompilerParams(vmem_limit_bytes=32 * MIB),
        cost_estimate=pl.CostEstimate(
            flops=4 * slots * block**3,
            bytes_accessed=26 * slots * block * block,
            transcendentals=0,
        ),
        name="statistics",
    )(meta, left_stat, right_stat, second, *grads)


def regroup_kernel(groups, slots, bands, halves, meta, *refs):
    pieces, outs, placed = refs[:groups], refs[groups:-1], refs[-1]
    block = pieces[0].shape[-1]
    position = meta[0]
    own_band = lax.div(position, halves)

    def place(s, carry):
        for k in range(groups):
            block_id = meta[2 + (position ^ k) * slots + s]
            row_band, col_band = lax.div(block_id, bands), lax.rem(block_id, bands)
            columns = pl.ds(pl.multiple_of(col_band * block, block), block)
            placed[row_band ^ own_band, :, columns] = pieces[k][s]
        return carry

    lax.fori_loop(0, slots, place, 0)
    for k in range(len(outs)):
        outs[k][...] = placed[k]


def regroup(meta, pieces, bands, halves):
    groups = len(pieces)
    slots, sub, block = pieces[0].shape
    row_bands = groups // halves
    return pl.pallas_call(
        functools.partial(regroup_kernel, groups, slots, bands, halves),
        grid_spec=pltpu.PrefetchScalarGridSpec(
            num_scalar_prefetch=1,
            grid=(),
            in_specs=[pl.BlockSpec(memory_space=pltpu.VMEM)] * groups,
            out_specs=[pl.BlockSpec(memory_space=pltpu.VMEM)] * row_bands,
            scratch_shapes=[pltpu.VMEM((row_bands, sub, bands * block), jnp.bfloat16)],
        ),
        out_shape=[jax.ShapeDtypeStruct((sub, bands * block), jnp.bfloat16)] * row_bands,
        compiler_params=pltpu.CompilerParams(vmem_limit_bytes=32 * MIB),
        cost_estimate=pl.CostEstimate(
            flops=0,
            bytes_accessed=4 * row_bands * sub * bands * block,
            transcendentals=0,
        ),
        name="regroup",
    )(meta, *pieces)


def stack_kernel(halves, meta, *refs):
    pieces, out = refs[:-1], refs[-1]
    sub = pieces[0].shape[0]
    own_band = lax.div(meta[0], halves)
    for k in range(len(pieces)):
        start = pl.multiple_of((own_band ^ k) * sub, sub)
        out[0, pl.ds(start, sub), :] = pieces[k][...]


def stack_rows(meta, pieces, halves):
    count = len(pieces)
    sub, width = pieces[0].shape
    part = width // count
    return pl.pallas_call(
        functools.partial(stack_kernel, halves),
        grid_spec=pltpu.PrefetchScalarGridSpec(
            num_scalar_prefetch=1,
            grid=(count,),
            in_specs=[pl.BlockSpec((sub, part), lambda c, meta: (0, c))] * count,
            out_specs=pl.BlockSpec((1, count * sub, part), lambda c, meta: (0, 0, c)),
        ),
        out_shape=jax.ShapeDtypeStruct((1, count * sub, width), jnp.bfloat16),
        compiler_params=pltpu.CompilerParams(vmem_limit_bytes=16 * MIB),
        cost_estimate=pl.CostEstimate(
            flops=0, bytes_accessed=4 * count * sub * width, transcendentals=0
        ),
        name="stack_rows",
    )(meta, *pieces)


def exchange(pieces, stride=1):
    return [pieces[0]] + [swap(pieces[k], "fsdp", k * stride) for k in range(1, len(pieces))]


def gather_relayed(value):
    groups = lax.axis_size("fsdp")
    found = [value] + [None] * (groups - 1)
    far = groups // 2
    found[far] = swap(value, "fsdp", far)
    step = 1
    while step < far:
        found[step] = swap(value, "fsdp", step)
        for k in range(1, step):
            found[step + k] = swap(found[step], "fsdp", k)
        step *= 2
    step = 1
    while step < far:
        for k in range(step):
            found[far + step + k] = swap(found[far + k], "fsdp", step)
        step *= 2
    return found


def strip_plan(
    context, cotangent, block_table, left_stat, right_stat, root_left, root_right, second_moment
):
    groups, ranks = lax.axis_size("fsdp"), lax.axis_size("tensor")
    band_rows = context.shape[1]
    block, slots = left_stat.shape[-1], left_stat.shape[1]
    bands = cotangent.shape[1] * ranks // block
    strip_rows = band_rows // groups
    place = jnp.stack([lax.axis_index("fsdp"), lax.axis_index("tensor")]).astype(jnp.int32)
    meta = jnp.concatenate([place, block_table[0]])

    strips = exchange(cot_strips(meta, cotangent, groups, block))
    ctxs = gather_relayed(context)
    tokens = context.shape[0]
    cots = [jnp.stack(strips).reshape(groups, -1, tokens)]
    offset = ranks // 2
    by_offset = {0: cots[0]}
    while offset:
        for known in list(by_offset):
            by_offset[known ^ offset] = swap(by_offset[known], "tensor", offset)
        offset //= 2
    cots = [by_offset[t] for t in range(ranks)]

    grads = exchange(gradient_strips(meta, cots, ctxs, slots, bands, block))
    halves = block // strip_rows
    sub = strip_rows * halves // groups
    pieces = exchange(
        directions(meta, grads, second_moment, root_left, root_right, halves, sub)
    )
    left_new, right_new, second_new = statistics(
        meta, grads, left_stat, right_stat, second_moment
    )
    rows = exchange(regroup(meta, pieces, bands, halves), halves)
    return (left_new, right_new, second_new, stack_rows(meta, rows, halves))


def per_device(context, cotangent, block_table, left_stat, *rest):
    groups, ranks = lax.axis_size("fsdp"), lax.axis_size("tensor")
    block = left_stat.shape[-1]
    strip_rows = context.shape[1] // groups
    powers = groups & (groups - 1) == 0 and ranks & (ranks - 1) == 0
    whole = block % strip_rows == 0 and cotangent.shape[1] % block == 0
    even = block % (16 * groups) == 0
    plan = strip_plan if powers and even and whole else general_plan
    return plan(context, cotangent, block_table, left_stat, *rest)


def solution(mesh):
    return jax.shard_map(
        per_device,
        mesh=mesh,
        in_specs=(
            P("fsdp", "tensor"),
            P("fsdp", "tensor"),
            P("tensor", None),
            P("tensor", "fsdp", None, None),
            P("tensor", "fsdp", None, None),
            P("tensor", "fsdp", None, None),
            P("tensor", "fsdp", None, None),
            P("tensor", "fsdp", None, None),
        ),
        out_specs=(
            P("tensor", "fsdp", None, None),
            P("tensor", "fsdp", None, None),
            P("tensor", "fsdp", None, None),
            P("tensor", "fsdp", None),
        ),
        check_vma=False,
    )
```

```python
import functools

import jax
import jax.numpy as jnp
from jax import lax
from jax.experimental import pallas as pl
from jax.experimental.pallas import tpu as pltpu
from jax.sharding import PartitionSpec as P

decay_rate = 0.95
MIB = 1024 * 1024


def general_plan(
    context, cotangent, block_table, left_stat, right_stat, root_left, root_right, second_moment
):
    full_cot = lax.all_gather(cotangent, "tensor", axis=1, tiled=True)
    tokens_here, band_rows = context.shape
    model_width = full_cot.shape[1]
    block_size = left_stat.shape[-1]
    slot_count = left_stat.shape[1]
    groups = lax.axis_size("fsdp")
    position = lax.axis_index("fsdp")
    owner_table = block_table[0]
    col_bands = model_width // block_size
    strip_rows = band_rows // groups
    per_band = block_size // strip_rows
    my_blocks = lax.dynamic_slice_in_dim(owner_table, position * slot_count, slot_count)
    ctx_bands = context.reshape(tokens_here, band_rows // block_size, block_size)
    cot_bands = full_cot.reshape(tokens_here, col_bands, block_size)
    left_part = jnp.take(ctx_bands, owner_table // col_bands, axis=1)
    right_part = jnp.take(cot_bands, owner_table % col_bands, axis=1)
    blocks = jnp.einsum("tnb,tnc->nbc", left_part, right_part, preferred_element_type=jnp.float32)
    gradient = lax.psum_scatter(
        blocks.reshape(slot_count * block_size * lax.axis_size("fsdp"), block_size).astype(
            jnp.bfloat16
        ),
        "fsdp",
        scatter_dimension=0,
        tiled=True,
    ).astype(jnp.float32)
    gradient = gradient.reshape(slot_count, block_size, block_size)
    highest = lax.Precision.HIGHEST
    gram_left = jnp.einsum("sij,skj->sik", gradient, gradient, precision=highest)
    gram_right = jnp.einsum("sji,sjk->sik", gradient, gradient, precision=highest)
    left_new = decay_rate * left_stat[0] + (1.0 - decay_rate) * gram_left / block_size
    right_new = decay_rate * right_stat[0] + (1.0 - decay_rate) * gram_right / block_size
    second_new = decay_rate * second_moment[0] + (1.0 - decay_rate) * gradient * gradient
    adam_step = gradient / (jnp.sqrt(second_new) + 1e-08)
    shaped = jnp.einsum("sij,sjk->sik", root_left[0], gradient, precision=highest)
    shaped = jnp.einsum("sij,sjk->sik", shaped, root_right[0], precision=highest)
    graft_ratio = jnp.sqrt(jnp.sum(adam_step * adam_step, axis=(1, 2))) / jnp.sqrt(
        jnp.sum(shaped * shaped, axis=(1, 2)) + 1e-06
    )
    direction = (shaped * graft_ratio[:, None, None]).astype(jnp.bfloat16)
    by_strip = direction.reshape(slot_count, per_band, strip_rows, block_size)
    targets = jnp.arange(groups, dtype=jnp.int32)
    chosen = jnp.take(by_strip, targets % per_band, axis=1)
    keep_mask = ((my_blocks // col_bands)[:, None] == (targets // per_band)[None, :]).astype(
        jnp.bfloat16
    )
    outgoing_rows = jnp.swapaxes(chosen * keep_mask[:, :, None, None], 0, 1)
    returned = lax.all_to_all(outgoing_rows, "fsdp", split_axis=0, concat_axis=0, tiled=True)
    wanted = position // per_band * col_bands + jnp.arange(col_bands, dtype=jnp.int32)
    slot_ids = jnp.arange(owner_table.shape[0], dtype=jnp.int32)
    located = jnp.sum(
        jnp.where(owner_table[None, :] == wanted[:, None], slot_ids[None, :], 0), axis=1
    )
    flat_pieces = returned.reshape(groups * slot_count, strip_rows, block_size)
    pieces = jnp.take(flat_pieces, located, axis=0)
    result = jnp.swapaxes(pieces, 0, 1).reshape(strip_rows, model_width)
    return (left_new[None], right_new[None], second_new[None], result[None])


def swap(value, axis, offset):
    count = lax.axis_size(axis)
    return lax.ppermute(value, axis, [(i, i ^ offset) for i in range(count)])


def strip_kernel(groups, strip, meta, cot_ref, *refs):
    outs, turned = refs[:groups], refs[groups]
    position = meta[0]
    turned[...] = cot_ref[...].T
    for k in range(groups):
        start = pl.multiple_of((position ^ k) * strip, strip)
        outs[k][0] = turned[pl.ds(start, strip), :]


def cot_strips(meta, cotangent, groups, block):
    tokens, width = cotangent.shape
    bands, strip = width // block, block // groups
    return pl.pallas_call(
        functools.partial(strip_kernel, groups, strip),
        grid_spec=pltpu.PrefetchScalarGridSpec(
            num_scalar_prefetch=1,
            grid=(bands,),
            in_specs=[pl.BlockSpec((tokens, block), lambda c, meta: (0, c))],
            out_specs=[pl.BlockSpec((1, strip, tokens), lambda c, meta: (c, 0, 0))] * groups,
            scratch_shapes=[pltpu.VMEM((block, tokens), jnp.bfloat16)],
        ),
        out_shape=[jax.ShapeDtypeStruct((bands, strip, tokens), jnp.bfloat16)] * groups,
        compiler_params=pltpu.CompilerParams(vmem_limit_bytes=16 * MIB),
        cost_estimate=pl.CostEstimate(
            flops=0, bytes_accessed=4 * tokens * width, transcendentals=0
        ),
        name="cot_strips",
    )(meta, cotangent)


def gradient_kernel(groups, ranks, chunks, bands, strip, block, meta, *refs):
    cots, ctxs = refs[:ranks], refs[ranks : ranks + groups]
    outs = refs[ranks + groups : -4]
    lhs, rhs, strips, sems = refs[-4:]
    slots = sum(chunks)
    tokens = ctxs[0].shape[0]
    rows = lhs.shape[1]
    position, rank = meta[0], meta[1]
    copies = []
    for k in range(groups):
        copies.append(
            pltpu.make_async_copy(
                ctxs[k], rhs.at[pl.ds(k * tokens, tokens), :], sems.at[ranks * groups + k]
            )
        )
    for t in range(ranks):
        for k in range(groups):
            copies.append(
                pltpu.make_async_copy(
                    cots[t].at[k],
                    lhs.at[t, :, pl.ds(k * tokens, tokens)],
                    sems.at[t * groups + k],
                )
            )
    for copy in copies:
        copy.start()
    for copy in copies:
        copy.wait()
    for t in range(ranks):
        strips[pl.ds(t * rows, rows), :] = jnp.dot(
            lhs[t], rhs[...], preferred_element_type=jnp.float32
        ).astype(jnp.bfloat16)
    own_bands = bands // ranks

    def place(first, pieces, s, carry):
        for k in range(groups):
            block_id = meta[2 + (position ^ k) * slots + first + s]
            row_band, col_band = lax.div(block_id, bands), lax.rem(block_id, bands)
            piece = lax.div(col_band, own_bands) ^ rank
            start = piece * rows + lax.rem(col_band, own_bands) * strip
            pieces[k][s] = strips[
                pl.ds(pl.multiple_of(start, strip), strip),
                pl.ds(pl.multiple_of(row_band * block, block), block),
            ]
        return carry

    for i, count in enumerate(chunks):
        pieces = outs[i * groups : (i + 1) * groups]
        lax.fori_loop(0, count, functools.partial(place, sum(chunks[:i]), pieces), 0)


def gradient_strips(meta, cots, ctxs, chunks, bands, block):
    groups, ranks = len(ctxs), len(cots)
    tokens, band_rows = ctxs[0].shape
    rows, strip = cots[0].shape[1], block // groups
    flops = 2 * ranks * rows * groups * tokens * band_rows
    slots = sum(chunks)
    outs = pl.pallas_call(
        functools.partial(gradient_kernel, groups, ranks, chunks, bands, strip, block),
        grid_spec=pltpu.PrefetchScalarGridSpec(
            num_scalar_prefetch=1,
            grid=(),
            in_specs=[pl.BlockSpec(memory_space=pl.ANY)] * (ranks + groups),
            out_specs=[pl.BlockSpec(memory_space=pltpu.VMEM)] * (groups * len(chunks)),
            scratch_shapes=[
                pltpu.VMEM((ranks, rows, groups * tokens), jnp.bfloat16),
                pltpu.VMEM((groups * tokens, band_rows), jnp.bfloat16),
                pltpu.VMEM((ranks * rows, band_rows), jnp.bfloat16),
                pltpu.SemaphoreType.DMA(((ranks + 1) * groups,)),
            ],
        ),
        out_shape=[
            jax.ShapeDtypeStruct((count, strip, block), jnp.bfloat16)
            for count in chunks
            for _ in range(groups)
        ],
        compiler_params=pltpu.CompilerParams(vmem_limit_bytes=48 * MIB),
        cost_estimate=pl.CostEstimate(
            flops=flops,
            bytes_accessed=2 * groups * (ranks * rows * tokens + tokens * band_rows + slots * strip * block),
            transcendentals=0,
        ),
        name="gradient_strips",
    )(meta, *cots, *ctxs)
    return [outs[i * groups : (i + 1) * groups] for i in range(len(chunks))]


def gather_block(groups, strip, position, grads, turned):
    for k in range(groups):
        start = pl.multiple_of((position ^ k) * strip, strip)
        turned[pl.ds(start, strip), :] = grads[k][0]


def direction_kernel(groups, strip, halves, meta, second_ref, left_ref, right_ref, *refs):
    grads, outs, turned, rows = refs[:groups], refs[groups : 2 * groups], refs[-2], refs[-1]
    position = meta[0]
    gather_block(groups, strip, position, grads, turned)
    grad_bf16 = turned[...].T
    grad = grad_bf16.astype(jnp.float32)
    second = decay_rate * second_ref[0, 0] + (1.0 - decay_rate) * grad * grad
    adam = grad / (jnp.sqrt(second) + 1e-08)
    half = jnp.dot(
        left_ref[0, 0].astype(jnp.bfloat16), grad_bf16, preferred_element_type=jnp.float32
    )
    shaped = jnp.dot(
        half.astype(jnp.bfloat16),
        right_ref[0, 0].astype(jnp.bfloat16),
        preferred_element_type=jnp.float32,
    )
    adam_sum = jnp.sum(adam * adam, keepdims=True)
    shaped_sum = jnp.sum(shaped * shaped, keepdims=True)
    ratio = jnp.sqrt(adam_sum) / jnp.sqrt(shaped_sum + 1e-06)
    rows[...] = (shaped * ratio).astype(jnp.bfloat16)
    sub = outs[0].shape[1]
    for k in range(groups):
        middle = position ^ k
        half, quarter = lax.rem(middle, halves), lax.div(middle, halves)
        start = (half * (groups // halves) + quarter) * sub
        outs[k][0] = rows[pl.ds(pl.multiple_of(start, sub), sub), :]


def directions(meta, grads, first, second, root_left, root_right, halves, sub):
    groups = len(grads)
    slots, strip, block = grads[0].shape
    stat = pl.BlockSpec((1, 1, block, block), lambda s, meta: (0, first + s, 0, 0))
    return pl.pallas_call(
        functools.partial(direction_kernel, groups, strip, halves),
        grid_spec=pltpu.PrefetchScalarGridSpec(
            num_scalar_prefetch=1,
            grid=(slots,),
            in_specs=[stat] * 3
            + [pl.BlockSpec((1, strip, block), lambda s, meta: (s, 0, 0))] * groups,
            out_specs=[pl.BlockSpec((1, sub, block), lambda s, meta: (s, 0, 0))] * groups,
            scratch_shapes=[
                pltpu.VMEM((block, block), jnp.bfloat16),
                pltpu.VMEM((block, block), jnp.bfloat16),
            ],
        ),
        out_shape=[jax.ShapeDtypeStruct((slots, sub, block), jnp.bfloat16)] * groups,
        compiler_params=pltpu.CompilerParams(vmem_limit_bytes=32 * MIB),
        cost_estimate=pl.CostEstimate(
            flops=4 * slots * block**3,
            bytes_accessed=16 * slots * block * block,
            transcendentals=0,
        ),
        name="directions",
    )(meta, second, root_left, root_right, *grads)


def statistics_kernel(groups, strip, chunks, meta, left_ref, right_ref, second_ref, *refs):
    grads = refs[: groups * len(chunks)]
    left_out, right_out, second_out, turned = refs[groups * len(chunks) :]
    slot = pl.program_id(0)
    for i, count in enumerate(chunks):
        first = sum(chunks[:i])

        @pl.when(jnp.logical_and(slot >= first, slot < first + count))
        def _():
            gather_block(groups, strip, meta[0], grads[i * groups : (i + 1) * groups], turned)

    block = turned.shape[0]
    grad_t = turned[...]
    grad_bf16 = grad_t.T
    grad = grad_bf16.astype(jnp.float32)
    gram_left = jnp.dot(grad_bf16, grad_t, preferred_element_type=jnp.float32)
    gram_right = jnp.dot(grad_t, grad_bf16, preferred_element_type=jnp.float32)
    left_out[0, 0] = decay_rate * left_ref[0, 0] + (1.0 - decay_rate) * gram_left / block
    right_out[0, 0] = decay_rate * right_ref[0, 0] + (1.0 - decay_rate) * gram_right / block
    second_out[0, 0] = decay_rate * second_ref[0, 0] + (1.0 - decay_rate) * grad * grad


def statistics(meta, grads, left_stat, right_stat, second):
    groups, chunks = len(grads[0]), [chunk[0].shape[0] for chunk in grads]
    _, strip, block = grads[0][0].shape
    slots = sum(chunks)
    stat = pl.BlockSpec((1, 1, block, block), lambda s, meta: (0, s, 0, 0))

    def strip_spec(first, count):
        return pl.BlockSpec(
            (1, strip, block), lambda s, meta: (jnp.clip(s - first, 0, count - 1), 0, 0)
        )

    strip_specs = [
        strip_spec(sum(chunks[:i]), count) for i, count in enumerate(chunks) for _ in range(groups)
    ]
    return pl.pallas_call(
        functools.partial(statistics_kernel, groups, strip, chunks),
        grid_spec=pltpu.PrefetchScalarGridSpec(
            num_scalar_prefetch=1,
            grid=(slots,),
            in_specs=[stat] * 3 + strip_specs,
            out_specs=[stat] * 3,
            scratch_shapes=[pltpu.VMEM((block, block), jnp.bfloat16)],
        ),
        out_shape=[jax.ShapeDtypeStruct(left_stat.shape, jnp.float32)] * 3,
        compiler_params=pltpu.CompilerParams(vmem_limit_bytes=32 * MIB),
        cost_estimate=pl.CostEstimate(
            flops=4 * slots * block**3,
            bytes_accessed=26 * slots * block * block,
            transcendentals=0,
        ),
        name="statistics",
    )(meta, left_stat, right_stat, second, *[piece for chunk in grads for piece in chunk])


def regroup_kernel(groups, chunks, bands, halves, meta, *refs):
    inputs, outs, placed = refs[: groups * len(chunks)], refs[groups * len(chunks) : -1], refs[-1]
    block = inputs[0].shape[-1]
    position = meta[0]
    own_band = lax.div(position, halves)
    slots = sum(chunks)

    def place(first, pieces, s, carry):
        for k in range(groups):
            block_id = meta[2 + (position ^ k) * slots + first + s]
            row_band, col_band = lax.div(block_id, bands), lax.rem(block_id, bands)
            columns = pl.ds(pl.multiple_of(col_band * block, block), block)
            placed[row_band ^ own_band, :, columns] = pieces[k][s]
        return carry

    for i, count in enumerate(chunks):
        pieces = inputs[i * groups : (i + 1) * groups]
        lax.fori_loop(0, count, functools.partial(place, sum(chunks[:i]), pieces), 0)
    for k in range(len(outs)):
        outs[k][...] = placed[k]


def regroup(meta, pieces, bands, halves):
    groups, chunks = len(pieces[0]), [chunk[0].shape[0] for chunk in pieces]
    _, sub, block = pieces[0][0].shape
    row_bands = groups // halves
    return pl.pallas_call(
        functools.partial(regroup_kernel, groups, chunks, bands, halves),
        grid_spec=pltpu.PrefetchScalarGridSpec(
            num_scalar_prefetch=1,
            grid=(),
            in_specs=[pl.BlockSpec(memory_space=pltpu.VMEM)] * (groups * len(chunks)),
            out_specs=[pl.BlockSpec(memory_space=pltpu.VMEM)] * row_bands,
            scratch_shapes=[pltpu.VMEM((row_bands, sub, bands * block), jnp.bfloat16)],
        ),
        out_shape=[jax.ShapeDtypeStruct((sub, bands * block), jnp.bfloat16)] * row_bands,
        compiler_params=pltpu.CompilerParams(vmem_limit_bytes=32 * MIB),
        cost_estimate=pl.CostEstimate(
            flops=0,
            bytes_accessed=4 * row_bands * sub * bands * block,
            transcendentals=0,
        ),
        name="regroup",
    )(meta, *[piece for chunk in pieces for piece in chunk])


def stack_kernel(halves, meta, *refs):
    pieces, out = refs[:-1], refs[-1]
    sub = pieces[0].shape[0]
    own_band = lax.div(meta[0], halves)
    for k in range(len(pieces)):
        start = pl.multiple_of((own_band ^ k) * sub, sub)
        out[0, pl.ds(start, sub), :] = pieces[k][...]


def stack_rows(meta, pieces, halves):
    count = len(pieces)
    sub, width = pieces[0].shape
    part = width // count
    return pl.pallas_call(
        functools.partial(stack_kernel, halves),
        grid_spec=pltpu.PrefetchScalarGridSpec(
            num_scalar_prefetch=1,
            grid=(count,),
            in_specs=[pl.BlockSpec((sub, part), lambda c, meta: (0, c))] * count,
            out_specs=pl.BlockSpec((1, count * sub, part), lambda c, meta: (0, 0, c)),
        ),
        out_shape=jax.ShapeDtypeStruct((1, count * sub, width), jnp.bfloat16),
        compiler_params=pltpu.CompilerParams(vmem_limit_bytes=16 * MIB),
        cost_estimate=pl.CostEstimate(
            flops=0, bytes_accessed=4 * count * sub * width, transcendentals=0
        ),
        name="stack_rows",
    )(meta, *pieces)


def exchange(pieces, stride=1):
    return [pieces[0]] + [swap(pieces[k], "fsdp", k * stride) for k in range(1, len(pieces))]


def gather_relayed(value):
    groups = lax.axis_size("fsdp")
    found = [value] + [None] * (groups - 1)
    far = groups // 2
    found[far] = swap(value, "fsdp", far)
    step = 1
    while step < far:
        found[step] = swap(value, "fsdp", step)
        for k in range(1, step):
            found[step + k] = swap(found[step], "fsdp", k)
        step *= 2
    step = 1
    while step < far:
        for k in range(step):
            found[far + step + k] = swap(found[far + k], "fsdp", step)
        step *= 2
    return found


def strip_plan(
    context, cotangent, block_table, left_stat, right_stat, root_left, root_right, second_moment
):
    groups, ranks = lax.axis_size("fsdp"), lax.axis_size("tensor")
    band_rows = context.shape[1]
    block, slots = left_stat.shape[-1], left_stat.shape[1]
    bands = cotangent.shape[1] * ranks // block
    strip_rows = band_rows // groups
    place = jnp.stack([lax.axis_index("fsdp"), lax.axis_index("tensor")]).astype(jnp.int32)
    meta = jnp.concatenate([place, block_table[0]])

    strips = exchange(cot_strips(meta, cotangent, groups, block))
    ctxs = gather_relayed(context)
    tokens = context.shape[0]
    cots = [jnp.stack(strips).reshape(groups, -1, tokens)]
    offset = ranks // 2
    by_offset = {0: cots[0]}
    while offset:
        for known in list(by_offset):
            by_offset[known ^ offset] = swap(by_offset[known], "tensor", offset)
        offset //= 2
    cots = [by_offset[t] for t in range(ranks)]

    chunks = [slots - slots // 2, slots // 2]
    grads = [
        exchange(chunk) for chunk in gradient_strips(meta, cots, ctxs, chunks, bands, block)
    ]
    halves = block // strip_rows
    sub = strip_rows * halves // groups
    pieces = []
    for i, chunk in enumerate(grads):
        stale = (second_moment, root_left, root_right)
        pieces.append(exchange(directions(meta, chunk, sum(chunks[:i]), *stale, halves, sub)))
    left_new, right_new, second_new = statistics(
        meta, grads, left_stat, right_stat, second_moment
    )
    rows = exchange(regroup(meta, pieces, bands, halves), halves)
    return (left_new, right_new, second_new, stack_rows(meta, rows, halves))


def per_device(context, cotangent, block_table, left_stat, *rest):
    groups, ranks = lax.axis_size("fsdp"), lax.axis_size("tensor")
    block = left_stat.shape[-1]
    strip_rows = context.shape[1] // groups
    powers = groups & (groups - 1) == 0 and ranks & (ranks - 1) == 0
    whole = block % strip_rows == 0 and cotangent.shape[1] % block == 0
    even = block % (16 * groups) == 0
    plan = strip_plan if powers and even and whole else general_plan
    return plan(context, cotangent, block_table, left_stat, *rest)


def solution(mesh):
    return jax.shard_map(
        per_device,
        mesh=mesh,
        in_specs=(
            P("fsdp", "tensor"),
            P("fsdp", "tensor"),
            P("tensor", None),
            P("tensor", "fsdp", None, None),
            P("tensor", "fsdp", None, None),
            P("tensor", "fsdp", None, None),
            P("tensor", "fsdp", None, None),
            P("tensor", "fsdp", None, None),
        ),
        out_specs=(
            P("tensor", "fsdp", None, None),
            P("tensor", "fsdp", None, None),
            P("tensor", "fsdp", None, None),
            P("tensor", "fsdp", None),
        ),
        check_vma=False,
    )
```

```python
import functools

import jax
import jax.numpy as jnp
from jax import lax
from jax.experimental import pallas as pl
from jax.experimental.pallas import tpu as pltpu
from jax.sharding import PartitionSpec as P

decay_rate = 0.95
MIB = 1024 * 1024


def general_plan(
    context, cotangent, block_table, left_stat, right_stat, root_left, root_right, second_moment
):
    full_cot = lax.all_gather(cotangent, "tensor", axis=1, tiled=True)
    tokens_here, band_rows = context.shape
    model_width = full_cot.shape[1]
    block_size = left_stat.shape[-1]
    slot_count = left_stat.shape[1]
    groups = lax.axis_size("fsdp")
    position = lax.axis_index("fsdp")
    owner_table = block_table[0]
    col_bands = model_width // block_size
    strip_rows = band_rows // groups
    per_band = block_size // strip_rows
    my_blocks = lax.dynamic_slice_in_dim(owner_table, position * slot_count, slot_count)
    ctx_bands = context.reshape(tokens_here, band_rows // block_size, block_size)
    cot_bands = full_cot.reshape(tokens_here, col_bands, block_size)
    left_part = jnp.take(ctx_bands, owner_table // col_bands, axis=1)
    right_part = jnp.take(cot_bands, owner_table % col_bands, axis=1)
    blocks = jnp.einsum("tnb,tnc->nbc", left_part, right_part, preferred_element_type=jnp.float32)
    gradient = lax.psum_scatter(
        blocks.reshape(slot_count * block_size * lax.axis_size("fsdp"), block_size).astype(
            jnp.bfloat16
        ),
        "fsdp",
        scatter_dimension=0,
        tiled=True,
    ).astype(jnp.float32)
    gradient = gradient.reshape(slot_count, block_size, block_size)
    highest = lax.Precision.HIGHEST
    gram_left = jnp.einsum("sij,skj->sik", gradient, gradient, precision=highest)
    gram_right = jnp.einsum("sji,sjk->sik", gradient, gradient, precision=highest)
    left_new = decay_rate * left_stat[0] + (1.0 - decay_rate) * gram_left / block_size
    right_new = decay_rate * right_stat[0] + (1.0 - decay_rate) * gram_right / block_size
    second_new = decay_rate * second_moment[0] + (1.0 - decay_rate) * gradient * gradient
    adam_step = gradient / (jnp.sqrt(second_new) + 1e-08)
    shaped = jnp.einsum("sij,sjk->sik", root_left[0], gradient, precision=highest)
    shaped = jnp.einsum("sij,sjk->sik", shaped, root_right[0], precision=highest)
    graft_ratio = jnp.sqrt(jnp.sum(adam_step * adam_step, axis=(1, 2))) / jnp.sqrt(
        jnp.sum(shaped * shaped, axis=(1, 2)) + 1e-06
    )
    direction = (shaped * graft_ratio[:, None, None]).astype(jnp.bfloat16)
    by_strip = direction.reshape(slot_count, per_band, strip_rows, block_size)
    targets = jnp.arange(groups, dtype=jnp.int32)
    chosen = jnp.take(by_strip, targets % per_band, axis=1)
    keep_mask = ((my_blocks // col_bands)[:, None] == (targets // per_band)[None, :]).astype(
        jnp.bfloat16
    )
    outgoing_rows = jnp.swapaxes(chosen * keep_mask[:, :, None, None], 0, 1)
    returned = lax.all_to_all(outgoing_rows, "fsdp", split_axis=0, concat_axis=0, tiled=True)
    wanted = position // per_band * col_bands + jnp.arange(col_bands, dtype=jnp.int32)
    slot_ids = jnp.arange(owner_table.shape[0], dtype=jnp.int32)
    located = jnp.sum(
        jnp.where(owner_table[None, :] == wanted[:, None], slot_ids[None, :], 0), axis=1
    )
    flat_pieces = returned.reshape(groups * slot_count, strip_rows, block_size)
    pieces = jnp.take(flat_pieces, located, axis=0)
    result = jnp.swapaxes(pieces, 0, 1).reshape(strip_rows, model_width)
    return (left_new[None], right_new[None], second_new[None], result[None])


def swap(value, axis, offset):
    count = lax.axis_size(axis)
    return lax.ppermute(value, axis, [(i, i ^ offset) for i in range(count)])


def prepare_kernel(pairs, block, meta, cot_ref, context_ref, *refs):
    outs, (own, other, turned) = refs[:pairs], refs[pairs:]
    strip, half = block // pairs, block // 2
    pair, side = lax.div(meta[0], 2), lax.rem(meta[0], 2)
    turned[...] = cot_ref[...].T
    for k in range(pairs):
        start = pl.multiple_of((pair ^ k) * strip, strip)
        outs[k][0] = turned[pl.ds(start, strip), :]

    @pl.when(pl.program_id(0) == 0)
    def _():
        for out, place in ((own, side), (other, side ^ 1)):
            for r in range(out.shape[1] // half):
                start = pl.multiple_of(r * block + place * half, half)
                out[:, r * half : (r + 1) * half] = context_ref[:, pl.ds(start, half)]


def prepare(meta, cotangent, context, pairs, block):
    tokens, width = cotangent.shape
    band_rows = context.shape[1]
    bands, strip = width // block, block // pairs
    outs = pl.pallas_call(
        functools.partial(prepare_kernel, pairs, block),
        grid_spec=pltpu.PrefetchScalarGridSpec(
            num_scalar_prefetch=1,
            grid=(bands,),
            in_specs=[
                pl.BlockSpec((tokens, block), lambda c, meta: (0, c)),
                pl.BlockSpec((tokens, band_rows), lambda c, meta: (0, 0)),
            ],
            out_specs=[pl.BlockSpec((1, strip, tokens), lambda c, meta: (c, 0, 0))] * pairs
            + [pl.BlockSpec((tokens, band_rows // 2), lambda c, meta: (0, 0))] * 2,
            scratch_shapes=[pltpu.VMEM((block, tokens), jnp.bfloat16)],
        ),
        out_shape=[jax.ShapeDtypeStruct((bands, strip, tokens), jnp.bfloat16)] * pairs
        + [jax.ShapeDtypeStruct((tokens, band_rows // 2), jnp.bfloat16)] * 2,
        compiler_params=pltpu.CompilerParams(vmem_limit_bytes=16 * MIB),
        cost_estimate=pl.CostEstimate(
            flops=0, bytes_accessed=4 * tokens * (width + band_rows), transcendentals=0
        ),
        name="prepare",
    )(meta, cotangent, context)
    return outs[:pairs], outs[pairs], outs[pairs + 1]


def gradient_kernel(groups, ranks, sources, chunks, bands, meta, *refs):
    pairs = groups // 2
    count = 1 + max(source for source, _ in sources)
    cots, ctxs = refs[:count], refs[count : count + pairs]
    outs, strips = refs[count + pairs : -1], refs[-1]
    slots = sum(chunks)
    rows = cots[0].shape[1]
    strip, part = outs[0].shape[1:]
    position, rank = meta[0], meta[1]
    rhs = jnp.concatenate([ctxs[k // 2][k % 2] for k in range(groups)], axis=0)
    for t in range(ranks):
        found = sources[t * groups : (t + 1) * groups]
        lhs = jnp.concatenate([cots[source][place] for source, place in found], axis=1)
        strips[pl.ds(t * rows, rows), :] = jnp.dot(
            lhs, rhs, preferred_element_type=jnp.float32
        ).astype(jnp.bfloat16)
    own_bands = bands // ranks

    def place(first, pieces, s, carry):
        for k in range(groups):
            block_id = meta[2 + (position ^ k) * slots + first + s]
            row_band, col_band = lax.div(block_id, bands), lax.rem(block_id, bands)
            piece = lax.div(col_band, own_bands) ^ rank
            start = piece * rows + lax.rem(col_band, own_bands) * strip
            pieces[k][s] = strips[
                pl.ds(pl.multiple_of(start, strip), strip),
                pl.ds(pl.multiple_of(row_band * part, part), part),
            ]
        return carry

    for i, count in enumerate(chunks):
        pieces = outs[i * groups : (i + 1) * groups]
        lax.fori_loop(0, count, functools.partial(place, sum(chunks[:i]), pieces), 0)


def gradient_strips(meta, cots, ctxs, chunks, bands, block):
    ranks, pairs = len(cots), len(ctxs)
    groups = 2 * pairs
    sources, first = [], 0
    for own, *other in cots:
        places = [(first + 1 + i, n) for i, piece in enumerate(other) for n in range(piece.shape[0])]
        for pair in range(pairs):
            sources += [(first, pair), places[pair]]
        first += 1 + len(other)
    _, tokens, band_rows = ctxs[0].shape
    rows = cots[0][0].shape[1]
    strip, part = block // pairs, block // 2
    slots = sum(chunks)
    outs = pl.pallas_call(
        functools.partial(gradient_kernel, groups, ranks, sources, chunks, bands),
        grid_spec=pltpu.PrefetchScalarGridSpec(
            num_scalar_prefetch=1,
            grid=(),
            in_specs=[pl.BlockSpec(memory_space=pltpu.VMEM)] * (first + pairs),
            out_specs=[pl.BlockSpec(memory_space=pltpu.VMEM)] * (groups * len(chunks)),
            scratch_shapes=[pltpu.VMEM((ranks * rows, band_rows), jnp.bfloat16)],
        ),
        out_shape=[
            jax.ShapeDtypeStruct((count, strip, part), jnp.bfloat16)
            for count in chunks
            for _ in range(groups)
        ],
        compiler_params=pltpu.CompilerParams(vmem_limit_bytes=32 * MIB),
        cost_estimate=pl.CostEstimate(
            flops=2 * ranks * rows * groups * tokens * band_rows,
            bytes_accessed=2
            * groups
            * (ranks * rows * tokens + tokens * band_rows + slots * strip * part),
            transcendentals=0,
        ),
        name="gradient_strips",
    )(meta, *[piece for rank in cots for piece in rank], *ctxs)
    return [outs[i * groups : (i + 1) * groups] for i in range(len(chunks))]


def gather_block(position, grads, turned):
    for k, piece in enumerate(grads):
        _, strip, part = piece.shape
        middle = position ^ k
        rows = pl.ds(pl.multiple_of(lax.div(middle, 2) * strip, strip), strip)
        columns = pl.ds(pl.multiple_of(lax.rem(middle, 2) * part, part), part)
        turned[rows, columns] = piece[0]


def direction_kernel(groups, halves, meta, second_ref, left_ref, right_ref, *refs):
    grads, outs, turned, rows = refs[:groups], refs[groups : 2 * groups], refs[-2], refs[-1]
    position = meta[0]
    gather_block(position, grads, turned)
    grad_bf16 = turned[...].T
    grad = grad_bf16.astype(jnp.float32)
    second = decay_rate * second_ref[0, 0] + (1.0 - decay_rate) * grad * grad
    adam = grad / (jnp.sqrt(second) + 1e-08)
    half = jnp.dot(
        left_ref[0, 0].astype(jnp.bfloat16), grad_bf16, preferred_element_type=jnp.float32
    )
    shaped = jnp.dot(
        half.astype(jnp.bfloat16),
        right_ref[0, 0].astype(jnp.bfloat16),
        preferred_element_type=jnp.float32,
    )
    adam_sum = jnp.sum(adam * adam, keepdims=True)
    shaped_sum = jnp.sum(shaped * shaped, keepdims=True)
    ratio = jnp.sqrt(adam_sum) / jnp.sqrt(shaped_sum + 1e-06)
    rows[...] = (shaped * ratio).astype(jnp.bfloat16)
    sub = outs[0].shape[1]
    for k in range(groups):
        middle = position ^ k
        half, quarter = lax.rem(middle, halves), lax.div(middle, halves)
        start = (half * (groups // halves) + quarter) * sub
        outs[k][0] = rows[pl.ds(pl.multiple_of(start, sub), sub), :]


def directions(meta, grads, first, second, root_left, root_right, halves, sub):
    groups = len(grads)
    slots, strip, part = grads[0].shape
    block = second.shape[-1]
    stat = pl.BlockSpec((1, 1, block, block), lambda s, meta: (0, first + s, 0, 0))
    return pl.pallas_call(
        functools.partial(direction_kernel, groups, halves),
        grid_spec=pltpu.PrefetchScalarGridSpec(
            num_scalar_prefetch=1,
            grid=(slots,),
            in_specs=[stat] * 3
            + [pl.BlockSpec((1, strip, part), lambda s, meta: (s, 0, 0))] * groups,
            out_specs=[pl.BlockSpec((1, sub, block), lambda s, meta: (s, 0, 0))] * groups,
            scratch_shapes=[
                pltpu.VMEM((block, block), jnp.bfloat16),
                pltpu.VMEM((block, block), jnp.bfloat16),
            ],
        ),
        out_shape=[jax.ShapeDtypeStruct((slots, sub, block), jnp.bfloat16)] * groups,
        compiler_params=pltpu.CompilerParams(vmem_limit_bytes=32 * MIB),
        cost_estimate=pl.CostEstimate(
            flops=4 * slots * block**3,
            bytes_accessed=16 * slots * block * block,
            transcendentals=0,
        ),
        name="directions",
    )(meta, second, root_left, root_right, *grads)


def statistics_kernel(groups, chunks, meta, left_ref, right_ref, second_ref, *refs):
    grads = refs[: groups * len(chunks)]
    left_out, right_out, second_out, turned = refs[groups * len(chunks) :]
    slot = pl.program_id(0)
    for i, count in enumerate(chunks):
        first = sum(chunks[:i])

        @pl.when(jnp.logical_and(slot >= first, slot < first + count))
        def _():
            gather_block(meta[0], grads[i * groups : (i + 1) * groups], turned)

    block = turned.shape[0]
    grad_t = turned[...]
    grad_bf16 = grad_t.T
    grad = grad_bf16.astype(jnp.float32)
    gram_left = jnp.dot(grad_bf16, grad_t, preferred_element_type=jnp.float32)
    gram_right = jnp.dot(grad_t, grad_bf16, preferred_element_type=jnp.float32)
    left_out[0, 0] = decay_rate * left_ref[0, 0] + (1.0 - decay_rate) * gram_left / block
    right_out[0, 0] = decay_rate * right_ref[0, 0] + (1.0 - decay_rate) * gram_right / block
    second_out[0, 0] = decay_rate * second_ref[0, 0] + (1.0 - decay_rate) * grad * grad


def statistics(meta, grads, left_stat, right_stat, second):
    groups, chunks = len(grads[0]), [chunk[0].shape[0] for chunk in grads]
    _, strip, part = grads[0][0].shape
    block = second.shape[-1]
    slots = sum(chunks)
    stat = pl.BlockSpec((1, 1, block, block), lambda s, meta: (0, s, 0, 0))

    def strip_spec(first, count):
        return pl.BlockSpec(
            (1, strip, part), lambda s, meta: (jnp.clip(s - first, 0, count - 1), 0, 0)
        )

    strip_specs = [
        strip_spec(sum(chunks[:i]), count) for i, count in enumerate(chunks) for _ in range(groups)
    ]
    return pl.pallas_call(
        functools.partial(statistics_kernel, groups, chunks),
        grid_spec=pltpu.PrefetchScalarGridSpec(
            num_scalar_prefetch=1,
            grid=(slots,),
            in_specs=[stat] * 3 + strip_specs,
            out_specs=[stat] * 3,
            scratch_shapes=[pltpu.VMEM((block, block), jnp.bfloat16)],
        ),
        out_shape=[jax.ShapeDtypeStruct(left_stat.shape, jnp.float32)] * 3,
        compiler_params=pltpu.CompilerParams(vmem_limit_bytes=32 * MIB),
        cost_estimate=pl.CostEstimate(
            flops=4 * slots * block**3,
            bytes_accessed=26 * slots * block * block,
            transcendentals=0,
        ),
        name="statistics",
    )(meta, left_stat, right_stat, second, *[piece for chunk in grads for piece in chunk])


def regroup_kernel(groups, chunks, bands, halves, meta, *refs):
    inputs, outs, placed = refs[: groups * len(chunks)], refs[groups * len(chunks) : -1], refs[-1]
    block = inputs[0].shape[-1]
    position = meta[0]
    own_band = lax.div(position, halves)
    slots = sum(chunks)

    def place(first, pieces, s, carry):
        for k in range(groups):
            block_id = meta[2 + (position ^ k) * slots + first + s]
            row_band, col_band = lax.div(block_id, bands), lax.rem(block_id, bands)
            columns = pl.ds(pl.multiple_of(col_band * block, block), block)
            placed[row_band ^ own_band, :, columns] = pieces[k][s]
        return carry

    for i, count in enumerate(chunks):
        pieces = inputs[i * groups : (i + 1) * groups]
        lax.fori_loop(0, count, functools.partial(place, sum(chunks[:i]), pieces), 0)
    for k in range(len(outs)):
        outs[k][...] = placed[k]


def regroup(meta, pieces, bands, halves):
    groups, chunks = len(pieces[0]), [chunk[0].shape[0] for chunk in pieces]
    _, sub, block = pieces[0][0].shape
    row_bands = groups // halves
    return pl.pallas_call(
        functools.partial(regroup_kernel, groups, chunks, bands, halves),
        grid_spec=pltpu.PrefetchScalarGridSpec(
            num_scalar_prefetch=1,
            grid=(),
            in_specs=[pl.BlockSpec(memory_space=pltpu.VMEM)] * (groups * len(chunks)),
            out_specs=[pl.BlockSpec(memory_space=pltpu.VMEM)] * row_bands,
            scratch_shapes=[pltpu.VMEM((row_bands, sub, bands * block), jnp.bfloat16)],
        ),
        out_shape=[jax.ShapeDtypeStruct((sub, bands * block), jnp.bfloat16)] * row_bands,
        compiler_params=pltpu.CompilerParams(vmem_limit_bytes=32 * MIB),
        cost_estimate=pl.CostEstimate(
            flops=0,
            bytes_accessed=4 * row_bands * sub * bands * block,
            transcendentals=0,
        ),
        name="regroup",
    )(meta, *[piece for chunk in pieces for piece in chunk])


def stack_kernel(halves, meta, *refs):
    pieces, out = refs[:-1], refs[-1]
    sub = pieces[0].shape[0]
    own_band = lax.div(meta[0], halves)
    for k in range(len(pieces)):
        start = pl.multiple_of((own_band ^ k) * sub, sub)
        out[0, pl.ds(start, sub), :] = pieces[k][...]


def stack_rows(meta, pieces, halves):
    count = len(pieces)
    sub, width = pieces[0].shape
    part = width // count
    return pl.pallas_call(
        functools.partial(stack_kernel, halves),
        grid_spec=pltpu.PrefetchScalarGridSpec(
            num_scalar_prefetch=1,
            grid=(count,),
            in_specs=[pl.BlockSpec((sub, part), lambda c, meta: (0, c))] * count,
            out_specs=pl.BlockSpec((1, count * sub, part), lambda c, meta: (0, 0, c)),
        ),
        out_shape=jax.ShapeDtypeStruct((1, count * sub, width), jnp.bfloat16),
        compiler_params=pltpu.CompilerParams(vmem_limit_bytes=16 * MIB),
        cost_estimate=pl.CostEstimate(
            flops=0, bytes_accessed=4 * count * sub * width, transcendentals=0
        ),
        name="stack_rows",
    )(meta, *pieces)


def exchange(pieces, stride=1):
    return [pieces[0]] + [swap(pieces[k], "fsdp", k * stride) for k in range(1, len(pieces))]


def strip_plan(
    context, cotangent, block_table, left_stat, right_stat, root_left, root_right, second_moment
):
    groups, ranks = lax.axis_size("fsdp"), lax.axis_size("tensor")
    band_rows = context.shape[1]
    block, slots = left_stat.shape[-1], left_stat.shape[1]
    bands = cotangent.shape[1] * ranks // block
    strip_rows = band_rows // groups
    place = jnp.stack([lax.axis_index("fsdp"), lax.axis_index("tensor")]).astype(jnp.int32)
    meta = jnp.concatenate([place, block_table[0]])

    pairs, tokens = groups // 2, context.shape[0]
    pairs, tokens = groups // 2, context.shape[0]
    strips, own, other = prepare(meta, cotangent, context, pairs, block)
    strips = exchange(strips, 2)
    other = swap(other, "fsdp", 1)
    strips, other = lax.optimization_barrier((strips, other))
    strips = jnp.stack(strips).reshape(pairs, -1, tokens)
    ctxs = [jnp.stack([own, other])] + [None] * (pairs - 1)
    far = pairs // 2
    ctxs[far] = swap(ctxs[0], "fsdp", 2 * far)
    step = 1
    while step < far:
        for k in range(step):
            ctxs[step + k] = swap(ctxs[k], "fsdp", 2 * step)
            ctxs[far + step + k] = swap(ctxs[far + k], "fsdp", 2 * step)
        step *= 2
    by_pair = swap(strips, "fsdp", 1)
    cots = {0: [strips, by_pair]}
    offset = ranks // 2
    while offset:
        for known in list(cots):
            here = cots[known]
            if known == 0 and offset == ranks // 2:
                there = [swap(strips, "tensor", offset)]
                there.append(swap(by_pair[:far], "tensor", offset))
                there.append(swap(there[0][far:], "fsdp", 1))
            else:
                if known:
                    here[0], _ = lax.optimization_barrier((here[0], here[1]))
                there = [swap(piece, "tensor", offset) for piece in here]
            cots[known ^ offset] = there
        offset //= 2
    cots = [cots[t] for t in range(ranks)]

    chunks = [slots - slots // 2, slots // 2]
    grads = [
        exchange(chunk) for chunk in gradient_strips(meta, cots, ctxs, chunks, bands, block)
    ]
    halves = block // strip_rows
    sub = strip_rows * halves // groups
    pieces = []
    for i, chunk in enumerate(grads):
        stale = (second_moment, root_left, root_right)
        pieces.append(exchange(directions(meta, chunk, sum(chunks[:i]), *stale, halves, sub)))
    left_new, right_new, second_new = statistics(
        meta, grads, left_stat, right_stat, second_moment
    )
    rows = exchange(regroup(meta, pieces, bands, halves), halves)
    return (left_new, right_new, second_new, stack_rows(meta, rows, halves))


def per_device(context, cotangent, block_table, left_stat, *rest):
    groups, ranks = lax.axis_size("fsdp"), lax.axis_size("tensor")
    block = left_stat.shape[-1]
    strip_rows = context.shape[1] // groups
    powers = groups & (groups - 1) == 0 and ranks & (ranks - 1) == 0
    whole = block % strip_rows == 0 and cotangent.shape[1] % block == 0
    even = block % (16 * groups) == 0 and block == 2 * strip_rows and groups >= 8
    plan = strip_plan if powers and even and whole else general_plan
    return plan(context, cotangent, block_table, left_stat, *rest)


def solution(mesh):
    return jax.shard_map(
        per_device,
        mesh=mesh,
        in_specs=(
            P("fsdp", "tensor"),
            P("fsdp", "tensor"),
            P("tensor", None),
            P("tensor", "fsdp", None, None),
            P("tensor", "fsdp", None, None),
            P("tensor", "fsdp", None, None),
            P("tensor", "fsdp", None, None),
            P("tensor", "fsdp", None, None),
        ),
        out_specs=(
            P("tensor", "fsdp", None, None),
            P("tensor", "fsdp", None, None),
            P("tensor", "fsdp", None, None),
            P("tensor", "fsdp", None),
        ),
        check_vma=False,
    )
```

```python
import functools

import jax
import jax.numpy as jnp
from jax import lax
from jax.experimental import pallas as pl
from jax.experimental.pallas import tpu as pltpu
from jax.sharding import PartitionSpec as P

decay_rate = 0.95
MIB = 1024 * 1024


def general_plan(
    context, cotangent, block_table, left_stat, right_stat, root_left, root_right, second_moment
):
    full_cot = lax.all_gather(cotangent, "tensor", axis=1, tiled=True)
    tokens_here, band_rows = context.shape
    model_width = full_cot.shape[1]
    block_size = left_stat.shape[-1]
    slot_count = left_stat.shape[1]
    groups = lax.axis_size("fsdp")
    position = lax.axis_index("fsdp")
    owner_table = block_table[0]
    col_bands = model_width // block_size
    strip_rows = band_rows // groups
    per_band = block_size // strip_rows
    my_blocks = lax.dynamic_slice_in_dim(owner_table, position * slot_count, slot_count)
    ctx_bands = context.reshape(tokens_here, band_rows // block_size, block_size)
    cot_bands = full_cot.reshape(tokens_here, col_bands, block_size)
    left_part = jnp.take(ctx_bands, owner_table // col_bands, axis=1)
    right_part = jnp.take(cot_bands, owner_table % col_bands, axis=1)
    blocks = jnp.einsum("tnb,tnc->nbc", left_part, right_part, preferred_element_type=jnp.float32)
    gradient = lax.psum_scatter(
        blocks.reshape(slot_count * block_size * lax.axis_size("fsdp"), block_size).astype(
            jnp.bfloat16
        ),
        "fsdp",
        scatter_dimension=0,
        tiled=True,
    ).astype(jnp.float32)
    gradient = gradient.reshape(slot_count, block_size, block_size)
    highest = lax.Precision.HIGHEST
    gram_left = jnp.einsum("sij,skj->sik", gradient, gradient, precision=highest)
    gram_right = jnp.einsum("sji,sjk->sik", gradient, gradient, precision=highest)
    left_new = decay_rate * left_stat[0] + (1.0 - decay_rate) * gram_left / block_size
    right_new = decay_rate * right_stat[0] + (1.0 - decay_rate) * gram_right / block_size
    second_new = decay_rate * second_moment[0] + (1.0 - decay_rate) * gradient * gradient
    adam_step = gradient / (jnp.sqrt(second_new) + 1e-08)
    shaped = jnp.einsum("sij,sjk->sik", root_left[0], gradient, precision=highest)
    shaped = jnp.einsum("sij,sjk->sik", shaped, root_right[0], precision=highest)
    graft_ratio = jnp.sqrt(jnp.sum(adam_step * adam_step, axis=(1, 2))) / jnp.sqrt(
        jnp.sum(shaped * shaped, axis=(1, 2)) + 1e-06
    )
    direction = (shaped * graft_ratio[:, None, None]).astype(jnp.bfloat16)
    by_strip = direction.reshape(slot_count, per_band, strip_rows, block_size)
    targets = jnp.arange(groups, dtype=jnp.int32)
    chosen = jnp.take(by_strip, targets % per_band, axis=1)
    keep_mask = ((my_blocks // col_bands)[:, None] == (targets // per_band)[None, :]).astype(
        jnp.bfloat16
    )
    outgoing_rows = jnp.swapaxes(chosen * keep_mask[:, :, None, None], 0, 1)
    returned = lax.all_to_all(outgoing_rows, "fsdp", split_axis=0, concat_axis=0, tiled=True)
    wanted = position // per_band * col_bands + jnp.arange(col_bands, dtype=jnp.int32)
    slot_ids = jnp.arange(owner_table.shape[0], dtype=jnp.int32)
    located = jnp.sum(
        jnp.where(owner_table[None, :] == wanted[:, None], slot_ids[None, :], 0), axis=1
    )
    flat_pieces = returned.reshape(groups * slot_count, strip_rows, block_size)
    pieces = jnp.take(flat_pieces, located, axis=0)
    result = jnp.swapaxes(pieces, 0, 1).reshape(strip_rows, model_width)
    return (left_new[None], right_new[None], second_new[None], result[None])


def swap(value, axis, offset):
    count = lax.axis_size(axis)
    return lax.ppermute(value, axis, [(i, i ^ offset) for i in range(count)])


def prepare_kernel(pairs, block, meta, cot_ref, context_ref, *refs):
    outs, (own, other, turned) = refs[:pairs], refs[pairs:]
    strip, half = block // pairs, block // 2
    pair, side = lax.div(meta[0], 2), lax.rem(meta[0], 2)
    turned[...] = cot_ref[...].T
    for k in range(pairs):
        start = pl.multiple_of((pair ^ k) * strip, strip)
        outs[k][0] = turned[pl.ds(start, strip), :]

    @pl.when(pl.program_id(0) == 0)
    def _():
        for out, place in ((own, side), (other, side ^ 1)):
            for r in range(out.shape[1] // half):
                start = pl.multiple_of(r * block + place * half, half)
                out[:, r * half : (r + 1) * half] = context_ref[:, pl.ds(start, half)]


def prepare(meta, cotangent, context, pairs, block):
    tokens, width = cotangent.shape
    band_rows = context.shape[1]
    bands, strip = width // block, block // pairs
    outs = pl.pallas_call(
        functools.partial(prepare_kernel, pairs, block),
        grid_spec=pltpu.PrefetchScalarGridSpec(
            num_scalar_prefetch=1,
            grid=(bands,),
            in_specs=[
                pl.BlockSpec((tokens, block), lambda c, meta: (0, c)),
                pl.BlockSpec((tokens, band_rows), lambda c, meta: (0, 0)),
            ],
            out_specs=[pl.BlockSpec((1, strip, tokens), lambda c, meta: (c, 0, 0))] * pairs
            + [pl.BlockSpec((tokens, band_rows // 2), lambda c, meta: (0, 0))] * 2,
            scratch_shapes=[pltpu.VMEM((block, tokens), jnp.bfloat16)],
        ),
        out_shape=[jax.ShapeDtypeStruct((bands, strip, tokens), jnp.bfloat16)] * pairs
        + [jax.ShapeDtypeStruct((tokens, band_rows // 2), jnp.bfloat16)] * 2,
        compiler_params=pltpu.CompilerParams(vmem_limit_bytes=8 * MIB),
        cost_estimate=pl.CostEstimate(
            flops=0, bytes_accessed=4 * tokens * (width + band_rows), transcendentals=0
        ),
        name="prepare",
    )(meta, cotangent, context)
    return outs[:pairs], outs[pairs], outs[pairs + 1]


def gradient_kernel(groups, ranks, sources, chunks, bands, meta, *refs):
    pairs = groups // 2
    count = 1 + max(source for source, _ in sources)
    cots, ctxs = refs[:count], refs[count : count + pairs]
    outs, strips = refs[count + pairs : -1], refs[-1]
    slots = sum(chunks)
    rows = cots[0].shape[1]
    strip, part = outs[0].shape[1:]
    position, rank = meta[0], meta[1]
    rhs = jnp.concatenate([ctxs[k // 2][k % 2] for k in range(groups)], axis=0)
    for t in range(ranks):
        found = sources[t * groups : (t + 1) * groups]
        lhs = jnp.concatenate([cots[source][place] for source, place in found], axis=1)
        strips[pl.ds(t * rows, rows), :] = jnp.dot(
            lhs, rhs, preferred_element_type=jnp.float32
        ).astype(jnp.bfloat16)
    own_bands = bands // ranks

    def place(first, pieces, s, carry):
        for k in range(groups):
            block_id = meta[2 + (position ^ k) * slots + first + s]
            row_band, col_band = lax.div(block_id, bands), lax.rem(block_id, bands)
            piece = lax.div(col_band, own_bands) ^ rank
            start = piece * rows + lax.rem(col_band, own_bands) * strip
            pieces[k][s] = strips[
                pl.ds(pl.multiple_of(start, strip), strip),
                pl.ds(pl.multiple_of(row_band * part, part), part),
            ]
        return carry

    for i, count in enumerate(chunks):
        pieces = outs[i * groups : (i + 1) * groups]
        lax.fori_loop(0, count, functools.partial(place, sum(chunks[:i]), pieces), 0)


def gradient_strips(meta, cots, ctxs, chunks, bands, block):
    ranks, pairs = len(cots), len(ctxs)
    groups = 2 * pairs
    sources, first = [], 0
    for own, *other in cots:
        places = [(first + 1 + i, n) for i, piece in enumerate(other) for n in range(piece.shape[0])]
        for pair in range(pairs):
            sources += [(first, pair), places[pair]]
        first += 1 + len(other)
    _, tokens, band_rows = ctxs[0].shape
    rows = cots[0][0].shape[1]
    strip, part = block // pairs, block // 2
    slots = sum(chunks)
    outs = pl.pallas_call(
        functools.partial(gradient_kernel, groups, ranks, sources, chunks, bands),
        grid_spec=pltpu.PrefetchScalarGridSpec(
            num_scalar_prefetch=1,
            grid=(),
            in_specs=[pl.BlockSpec(memory_space=pltpu.VMEM)] * (first + pairs),
            out_specs=[pl.BlockSpec(memory_space=pltpu.VMEM)] * (groups * len(chunks)),
            scratch_shapes=[pltpu.VMEM((ranks * rows, band_rows), jnp.bfloat16)],
        ),
        out_shape=[
            jax.ShapeDtypeStruct((count, strip, part), jnp.bfloat16)
            for count in chunks
            for _ in range(groups)
        ],
        compiler_params=pltpu.CompilerParams(vmem_limit_bytes=16 * MIB),
        cost_estimate=pl.CostEstimate(
            flops=2 * ranks * rows * groups * tokens * band_rows,
            bytes_accessed=2
            * groups
            * (ranks * rows * tokens + tokens * band_rows + slots * strip * part),
            transcendentals=0,
        ),
        name="gradient_strips",
    )(meta, *[piece for rank in cots for piece in rank], *ctxs)
    return [outs[i * groups : (i + 1) * groups] for i in range(len(chunks))]


def gather_block(position, grads, turned):
    for k, piece in enumerate(grads):
        _, strip, part = piece.shape
        middle = position ^ k
        rows = pl.ds(pl.multiple_of(lax.div(middle, 2) * strip, strip), strip)
        columns = pl.ds(pl.multiple_of(lax.rem(middle, 2) * part, part), part)
        turned[rows, columns] = piece[0]


def direction_kernel(groups, halves, meta, second_ref, left_ref, right_ref, *refs):
    grads, outs, turned, rows = refs[:groups], refs[groups : 2 * groups], refs[-2], refs[-1]
    position = meta[0]
    gather_block(position, grads, turned)
    grad_bf16 = turned[...].T
    grad = grad_bf16.astype(jnp.float32)
    second = decay_rate * second_ref[0, 0] + (1.0 - decay_rate) * grad * grad
    adam = grad / (jnp.sqrt(second) + 1e-08)
    half = jnp.dot(
        left_ref[0, 0].astype(jnp.bfloat16), grad_bf16, preferred_element_type=jnp.float32
    )
    shaped = jnp.dot(
        half.astype(jnp.bfloat16),
        right_ref[0, 0].astype(jnp.bfloat16),
        preferred_element_type=jnp.float32,
    )
    adam_sum = jnp.sum(adam * adam, keepdims=True)
    shaped_sum = jnp.sum(shaped * shaped, keepdims=True)
    ratio = jnp.sqrt(adam_sum) / jnp.sqrt(shaped_sum + 1e-06)
    rows[...] = (shaped * ratio).astype(jnp.bfloat16)
    sub = outs[0].shape[1]
    for k in range(groups):
        middle = position ^ k
        half, quarter = lax.rem(middle, halves), lax.div(middle, halves)
        start = (half * (groups // halves) + quarter) * sub
        outs[k][0] = rows[pl.ds(pl.multiple_of(start, sub), sub), :]


def directions(meta, grads, first, second, root_left, root_right, halves, sub):
    groups = len(grads)
    slots, strip, part = grads[0].shape
    block = second.shape[-1]
    stat = pl.BlockSpec((1, 1, block, block), lambda s, meta: (0, first + s, 0, 0))
    return pl.pallas_call(
        functools.partial(direction_kernel, groups, halves),
        grid_spec=pltpu.PrefetchScalarGridSpec(
            num_scalar_prefetch=1,
            grid=(slots,),
            in_specs=[stat] * 3
            + [pl.BlockSpec((1, strip, part), lambda s, meta: (s, 0, 0))] * groups,
            out_specs=[pl.BlockSpec((1, sub, block), lambda s, meta: (s, 0, 0))] * groups,
            scratch_shapes=[
                pltpu.VMEM((block, block), jnp.bfloat16),
                pltpu.VMEM((block, block), jnp.bfloat16),
            ],
        ),
        out_shape=[jax.ShapeDtypeStruct((slots, sub, block), jnp.bfloat16)] * groups,
        compiler_params=pltpu.CompilerParams(vmem_limit_bytes=8 * MIB),
        cost_estimate=pl.CostEstimate(
            flops=4 * slots * block**3,
            bytes_accessed=16 * slots * block * block,
            transcendentals=0,
        ),
        name="directions",
    )(meta, second, root_left, root_right, *grads)


def statistics_kernel(groups, chunks, meta, left_ref, right_ref, second_ref, *refs):
    grads = refs[: groups * len(chunks)]
    left_out, right_out, second_out, turned = refs[groups * len(chunks) :]
    slot = pl.program_id(0)
    for i, count in enumerate(chunks):
        first = sum(chunks[:i])

        @pl.when(jnp.logical_and(slot >= first, slot < first + count))
        def _():
            gather_block(meta[0], grads[i * groups : (i + 1) * groups], turned)

    block = turned.shape[0]
    grad_t = turned[...]
    grad_bf16 = grad_t.T
    grad = grad_bf16.astype(jnp.float32)
    gram_left = jnp.dot(grad_bf16, grad_t, preferred_element_type=jnp.float32)
    gram_right = jnp.dot(grad_t, grad_bf16, preferred_element_type=jnp.float32)
    left_out[0, 0] = decay_rate * left_ref[0, 0] + (1.0 - decay_rate) * gram_left / block
    right_out[0, 0] = decay_rate * right_ref[0, 0] + (1.0 - decay_rate) * gram_right / block
    second_out[0, 0] = decay_rate * second_ref[0, 0] + (1.0 - decay_rate) * grad * grad


def statistics(meta, grads, left_stat, right_stat, second):
    groups, chunks = len(grads[0]), [chunk[0].shape[0] for chunk in grads]
    _, strip, part = grads[0][0].shape
    block = second.shape[-1]
    slots = sum(chunks)
    stat = pl.BlockSpec((1, 1, block, block), lambda s, meta: (0, s, 0, 0))

    def strip_spec(first, count):
        return pl.BlockSpec(
            (1, strip, part), lambda s, meta: (jnp.clip(s - first, 0, count - 1), 0, 0)
        )

    strip_specs = [
        strip_spec(sum(chunks[:i]), count) for i, count in enumerate(chunks) for _ in range(groups)
    ]
    return pl.pallas_call(
        functools.partial(statistics_kernel, groups, chunks),
        grid_spec=pltpu.PrefetchScalarGridSpec(
            num_scalar_prefetch=1,
            grid=(slots,),
            in_specs=[stat] * 3 + strip_specs,
            out_specs=[stat] * 3,
            scratch_shapes=[pltpu.VMEM((block, block), jnp.bfloat16)],
        ),
        out_shape=[jax.ShapeDtypeStruct(left_stat.shape, jnp.float32)] * 3,
        compiler_params=pltpu.CompilerParams(vmem_limit_bytes=8 * MIB),
        cost_estimate=pl.CostEstimate(
            flops=4 * slots * block**3,
            bytes_accessed=26 * slots * block * block,
            transcendentals=0,
        ),
        name="statistics",
    )(meta, left_stat, right_stat, second, *[piece for chunk in grads for piece in chunk])


def regroup_kernel(groups, chunks, bands, halves, meta, *refs):
    inputs, outs, placed = refs[: groups * len(chunks)], refs[groups * len(chunks) : -1], refs[-1]
    block = inputs[0].shape[-1]
    position = meta[0]
    own_band = lax.div(position, halves)
    slots = sum(chunks)

    def place(first, pieces, s, carry):
        for k in range(groups):
            block_id = meta[2 + (position ^ k) * slots + first + s]
            row_band, col_band = lax.div(block_id, bands), lax.rem(block_id, bands)
            columns = pl.ds(pl.multiple_of(col_band * block, block), block)
            placed[row_band ^ own_band, :, columns] = pieces[k][s]
        return carry

    for i, count in enumerate(chunks):
        pieces = inputs[i * groups : (i + 1) * groups]
        lax.fori_loop(0, count, functools.partial(place, sum(chunks[:i]), pieces), 0)
    for k in range(len(outs)):
        outs[k][...] = placed[k]


def regroup(meta, pieces, bands, halves):
    groups, chunks = len(pieces[0]), [chunk[0].shape[0] for chunk in pieces]
    _, sub, block = pieces[0][0].shape
    row_bands = groups // halves
    return pl.pallas_call(
        functools.partial(regroup_kernel, groups, chunks, bands, halves),
        grid_spec=pltpu.PrefetchScalarGridSpec(
            num_scalar_prefetch=1,
            grid=(),
            in_specs=[pl.BlockSpec(memory_space=pltpu.VMEM)] * (groups * len(chunks)),
            out_specs=[pl.BlockSpec(memory_space=pltpu.VMEM)] * row_bands,
            scratch_shapes=[pltpu.VMEM((row_bands, sub, bands * block), jnp.bfloat16)],
        ),
        out_shape=[jax.ShapeDtypeStruct((sub, bands * block), jnp.bfloat16)] * row_bands,
        compiler_params=pltpu.CompilerParams(vmem_limit_bytes=8 * MIB),
        cost_estimate=pl.CostEstimate(
            flops=0,
            bytes_accessed=4 * row_bands * sub * bands * block,
            transcendentals=0,
        ),
        name="regroup",
    )(meta, *[piece for chunk in pieces for piece in chunk])


def stack_kernel(halves, meta, *refs):
    pieces, out, sems = refs[:-2], refs[-2], refs[-1]
    sub = pieces[0].shape[0]
    own_band = lax.div(meta[0], halves)
    copies = []
    for k, piece in enumerate(pieces):
        start = pl.multiple_of((own_band ^ k) * sub, sub)
        copies.append(pltpu.make_async_copy(piece, out.at[0, pl.ds(start, sub), :], sems.at[k]))
    for copy in copies:
        copy.start()
    for copy in copies:
        copy.wait()


def stack_rows(meta, pieces, halves):
    count = len(pieces)
    sub, width = pieces[0].shape
    return pl.pallas_call(
        functools.partial(stack_kernel, halves),
        grid_spec=pltpu.PrefetchScalarGridSpec(
            num_scalar_prefetch=1,
            grid=(),
            in_specs=[pl.BlockSpec(memory_space=pltpu.VMEM)] * count,
            out_specs=pl.BlockSpec(memory_space=pl.ANY),
            scratch_shapes=[pltpu.SemaphoreType.DMA((count,))],
        ),
        out_shape=jax.ShapeDtypeStruct((1, count * sub, width), jnp.bfloat16),
        compiler_params=pltpu.CompilerParams(vmem_limit_bytes=4 * MIB),
        cost_estimate=pl.CostEstimate(
            flops=0, bytes_accessed=4 * count * sub * width, transcendentals=0
        ),
        name="stack_rows",
    )(meta, *pieces)


def exchange(pieces, stride=1):
    return [pieces[0]] + [swap(pieces[k], "fsdp", k * stride) for k in range(1, len(pieces))]


def strip_plan(
    context, cotangent, block_table, left_stat, right_stat, root_left, root_right, second_moment
):
    groups, ranks = lax.axis_size("fsdp"), lax.axis_size("tensor")
    band_rows = context.shape[1]
    block, slots = left_stat.shape[-1], left_stat.shape[1]
    bands = cotangent.shape[1] * ranks // block
    strip_rows = band_rows // groups
    place = jnp.stack([lax.axis_index("fsdp"), lax.axis_index("tensor")]).astype(jnp.int32)
    meta = jnp.concatenate([place, block_table[0]])

    pairs, tokens = groups // 2, context.shape[0]
    pairs, tokens = groups // 2, context.shape[0]
    strips, own, other = prepare(meta, cotangent, context, pairs, block)
    strips = exchange(strips, 2)
    other = swap(other, "fsdp", 1)
    strips, other = lax.optimization_barrier((strips, other))
    strips = jnp.stack(strips).reshape(pairs, -1, tokens)
    ctxs = [jnp.stack([own, other])] + [None] * (pairs - 1)
    far = pairs // 2
    ctxs[far] = swap(ctxs[0], "fsdp", 2 * far)
    step = 1
    while step < far:
        for k in range(step):
            ctxs[step + k] = swap(ctxs[k], "fsdp", 2 * step)
            ctxs[far + step + k] = swap(ctxs[far + k], "fsdp", 2 * step)
        step *= 2
    by_pair = swap(strips, "fsdp", 1)
    by_rank = swap(strips, "tensor", ranks // 2)
    to_rank, to_pair = by_pair[:far], by_rank[far:]
    to_rank, _ = lax.optimization_barrier((to_rank, ctxs[1]))
    across = [
        by_rank,
        swap(to_rank, "tensor", ranks // 2),
        swap(to_pair, "fsdp", 1),
    ]
    cots = {0: [strips, by_pair], ranks // 2: across}
    offset = ranks // 4
    while offset:
        for known in list(cots):
            here = list(cots[known])
            if known:
                here[0], _ = lax.optimization_barrier((here[0], here[1]))

            cots[known ^ offset] = [swap(piece, "tensor", offset) for piece in here]
        offset //= 2
    cots = [cots[t] for t in range(ranks)]

    chunks = [slots - slots // 2, slots // 2]
    grads = [
        exchange(chunk) for chunk in gradient_strips(meta, cots, ctxs, chunks, bands, block)
    ]
    halves = block // strip_rows
    sub = strip_rows * halves // groups
    pieces = []
    for i, chunk in enumerate(grads):
        stale = (second_moment, root_left, root_right)
        pieces.append(exchange(directions(meta, chunk, sum(chunks[:i]), *stale, halves, sub)))
    left_new, right_new, second_new = statistics(
        meta, grads, left_stat, right_stat, second_moment
    )
    rows = exchange(regroup(meta, pieces, bands, halves), halves)
    return (left_new, right_new, second_new, stack_rows(meta, rows, halves))


def per_device(context, cotangent, block_table, left_stat, *rest):
    groups, ranks = lax.axis_size("fsdp"), lax.axis_size("tensor")
    block = left_stat.shape[-1]
    strip_rows = context.shape[1] // groups
    powers = groups & (groups - 1) == 0 and ranks & (ranks - 1) == 0
    whole = block % strip_rows == 0 and cotangent.shape[1] % block == 0
    even = block % (16 * groups) == 0 and block == 2 * strip_rows and groups >= 8
    plan = strip_plan if powers and even and whole else general_plan
    return plan(context, cotangent, block_table, left_stat, *rest)


def solution(mesh):
    return jax.shard_map(
        per_device,
        mesh=mesh,
        in_specs=(
            P("fsdp", "tensor"),
            P("fsdp", "tensor"),
            P("tensor", None),
            P("tensor", "fsdp", None, None),
            P("tensor", "fsdp", None, None),
            P("tensor", "fsdp", None, None),
            P("tensor", "fsdp", None, None),
            P("tensor", "fsdp", None, None),
        ),
        out_specs=(
            P("tensor", "fsdp", None, None),
            P("tensor", "fsdp", None, None),
            P("tensor", "fsdp", None, None),
            P("tensor", "fsdp", None),
        ),
        check_vma=False,
    )
```

```python
import functools

import jax
import jax.numpy as jnp
from jax import lax
from jax.experimental import pallas as pl
from jax.experimental.pallas import tpu as pltpu
from jax.sharding import PartitionSpec as P

decay_rate = 0.95
MIB = 1024 * 1024


def general_plan(
    context, cotangent, block_table, left_stat, right_stat, root_left, root_right, second_moment
):
    full_cot = lax.all_gather(cotangent, "tensor", axis=1, tiled=True)
    tokens_here, band_rows = context.shape
    model_width = full_cot.shape[1]
    block_size = left_stat.shape[-1]
    slot_count = left_stat.shape[1]
    groups = lax.axis_size("fsdp")
    position = lax.axis_index("fsdp")
    owner_table = block_table[0]
    col_bands = model_width // block_size
    strip_rows = band_rows // groups
    per_band = block_size // strip_rows
    my_blocks = lax.dynamic_slice_in_dim(owner_table, position * slot_count, slot_count)
    ctx_bands = context.reshape(tokens_here, band_rows // block_size, block_size)
    cot_bands = full_cot.reshape(tokens_here, col_bands, block_size)
    left_part = jnp.take(ctx_bands, owner_table // col_bands, axis=1)
    right_part = jnp.take(cot_bands, owner_table % col_bands, axis=1)
    blocks = jnp.einsum("tnb,tnc->nbc", left_part, right_part, preferred_element_type=jnp.float32)
    gradient = lax.psum_scatter(
        blocks.reshape(slot_count * block_size * lax.axis_size("fsdp"), block_size).astype(
            jnp.bfloat16
        ),
        "fsdp",
        scatter_dimension=0,
        tiled=True,
    ).astype(jnp.float32)
    gradient = gradient.reshape(slot_count, block_size, block_size)
    highest = lax.Precision.HIGHEST
    gram_left = jnp.einsum("sij,skj->sik", gradient, gradient, precision=highest)
    gram_right = jnp.einsum("sji,sjk->sik", gradient, gradient, precision=highest)
    left_new = decay_rate * left_stat[0] + (1.0 - decay_rate) * gram_left / block_size
    right_new = decay_rate * right_stat[0] + (1.0 - decay_rate) * gram_right / block_size
    second_new = decay_rate * second_moment[0] + (1.0 - decay_rate) * gradient * gradient
    adam_step = gradient / (jnp.sqrt(second_new) + 1e-08)
    shaped = jnp.einsum("sij,sjk->sik", root_left[0], gradient, precision=highest)
    shaped = jnp.einsum("sij,sjk->sik", shaped, root_right[0], precision=highest)
    graft_ratio = jnp.sqrt(jnp.sum(adam_step * adam_step, axis=(1, 2))) / jnp.sqrt(
        jnp.sum(shaped * shaped, axis=(1, 2)) + 1e-06
    )
    direction = (shaped * graft_ratio[:, None, None]).astype(jnp.bfloat16)
    by_strip = direction.reshape(slot_count, per_band, strip_rows, block_size)
    targets = jnp.arange(groups, dtype=jnp.int32)
    chosen = jnp.take(by_strip, targets % per_band, axis=1)
    keep_mask = ((my_blocks // col_bands)[:, None] == (targets // per_band)[None, :]).astype(
        jnp.bfloat16
    )
    outgoing_rows = jnp.swapaxes(chosen * keep_mask[:, :, None, None], 0, 1)
    returned = lax.all_to_all(outgoing_rows, "fsdp", split_axis=0, concat_axis=0, tiled=True)
    wanted = position // per_band * col_bands + jnp.arange(col_bands, dtype=jnp.int32)
    slot_ids = jnp.arange(owner_table.shape[0], dtype=jnp.int32)
    located = jnp.sum(
        jnp.where(owner_table[None, :] == wanted[:, None], slot_ids[None, :], 0), axis=1
    )
    flat_pieces = returned.reshape(groups * slot_count, strip_rows, block_size)
    pieces = jnp.take(flat_pieces, located, axis=0)
    result = jnp.swapaxes(pieces, 0, 1).reshape(strip_rows, model_width)
    return (left_new[None], right_new[None], second_new[None], result[None])


def swap(value, axis, offset):
    count = lax.axis_size(axis)
    return lax.ppermute(value, axis, [(i, i ^ offset) for i in range(count)])


def offsets_of(groups):
    far, near = range(groups // 2, groups), range(1, groups // 2)
    order = [k for pair in zip(far, near) for k in pair]
    return [*order, groups - 1, 0]


def pair_order(pairs):
    return [pairs // 2, 0, *[k for k in range(1, pairs) if k != pairs // 2]]


def prepare_kernel(pairs, block, meta, cot_ref, context_ref, *refs):
    outs, (own, other, turned) = refs[:pairs], refs[pairs:]
    strip, half = block // pairs, block // 2
    pair, side = lax.div(meta[0], 2), lax.rem(meta[0], 2)
    turned[...] = cot_ref[...].T
    for k in range(pairs):
        start = pl.multiple_of((pair ^ k) * strip, strip)
        outs[k][0] = turned[pl.ds(start, strip), :]

    @pl.when(pl.program_id(0) == 0)
    def _():
        for out, place in ((own, side), (other, side ^ 1)):
            for r in range(out.shape[1] // half):
                start = pl.multiple_of(r * block + place * half, half)
                out[:, r * half : (r + 1) * half] = context_ref[:, pl.ds(start, half)]


def prepare(meta, cotangent, context, pairs, block):
    tokens, width = cotangent.shape
    band_rows = context.shape[1]
    bands, strip = width // block, block // pairs
    outs = pl.pallas_call(
        functools.partial(prepare_kernel, pairs, block),
        grid_spec=pltpu.PrefetchScalarGridSpec(
            num_scalar_prefetch=1,
            grid=(bands,),
            in_specs=[
                pl.BlockSpec((tokens, block), lambda c, meta: (0, c)),
                pl.BlockSpec((tokens, band_rows), lambda c, meta: (0, 0)),
            ],
            out_specs=[pl.BlockSpec((1, strip, tokens), lambda c, meta: (c, 0, 0))] * pairs
            + [pl.BlockSpec((tokens, band_rows // 2), lambda c, meta: (0, 0))] * 2,
            scratch_shapes=[pltpu.VMEM((block, tokens), jnp.bfloat16)],
        ),
        out_shape=[jax.ShapeDtypeStruct((bands, strip, tokens), jnp.bfloat16)] * pairs
        + [jax.ShapeDtypeStruct((tokens, band_rows // 2), jnp.bfloat16)] * 2,
        compiler_params=pltpu.CompilerParams(vmem_limit_bytes=8 * MIB),
        cost_estimate=pl.CostEstimate(
            flops=0, bytes_accessed=4 * tokens * (width + band_rows), transcendentals=0
        ),
        name="prepare",
    )(meta, cotangent, context)
    return outs[:pairs], outs[pairs], outs[pairs + 1]


def gradient_kernel(groups, ranks, sources, chunks, bands, meta, *refs):
    pairs = groups // 2
    count = 1 + max(source for source, _ in sources)
    order = pair_order(pairs)
    ctxs, cots = [refs[order.index(k)] for k in range(pairs)], refs[pairs : count + pairs]
    outs, strips = refs[count + pairs : -1], refs[-1]
    slots = sum(chunks)
    rows = cots[0].shape[1]
    strip, part = outs[0].shape[1:]
    position, rank = meta[0], meta[1]
    rhs = jnp.concatenate([ctxs[k // 2][k % 2] for k in range(groups)], axis=0)
    for t in range(ranks):
        found = sources[t * groups : (t + 1) * groups]
        lhs = jnp.concatenate([cots[source][place] for source, place in found], axis=1)
        strips[pl.ds(t * rows, rows), :] = jnp.dot(
            lhs, rhs, preferred_element_type=jnp.float32
        ).astype(jnp.bfloat16)
    own_bands = bands // ranks
    offsets = offsets_of(groups)

    def place(first, pieces, s, carry):
        for k in range(groups):
            block_id = meta[2 + (position ^ offsets[k]) * slots + first + s]
            row_band, col_band = lax.div(block_id, bands), lax.rem(block_id, bands)
            piece = lax.div(col_band, own_bands) ^ rank
            start = piece * rows + lax.rem(col_band, own_bands) * strip
            pieces[k][s] = strips[
                pl.ds(pl.multiple_of(start, strip), strip),
                pl.ds(pl.multiple_of(row_band * part, part), part),
            ]
        return carry

    for i, count in enumerate(chunks):
        pieces = outs[i * groups : (i + 1) * groups]
        lax.fori_loop(0, count, functools.partial(place, sum(chunks[:i]), pieces), 0)


def gradient_strips(meta, cots, ctxs, chunks, bands, block):
    ranks, pairs = len(cots), len(ctxs)
    groups = 2 * pairs
    sources, first = [], 0
    for own, *other in cots:
        places = [(first + 1 + i, n) for i, piece in enumerate(other) for n in range(piece.shape[0])]
        for pair in range(pairs):
            sources += [(first, pair), places[pair]]
        first += 1 + len(other)
    _, tokens, band_rows = ctxs[0].shape
    rows = cots[0][0].shape[1]
    strip, part = block // pairs, block // 2
    slots = sum(chunks)
    outs = pl.pallas_call(
        functools.partial(gradient_kernel, groups, ranks, sources, chunks, bands),
        grid_spec=pltpu.PrefetchScalarGridSpec(
            num_scalar_prefetch=1,
            grid=(),
            in_specs=[pl.BlockSpec(memory_space=pltpu.VMEM)] * (first + pairs),
            out_specs=[pl.BlockSpec(memory_space=pltpu.VMEM)] * (groups * len(chunks)),
            scratch_shapes=[pltpu.VMEM((ranks * rows, band_rows), jnp.bfloat16)],
        ),
        out_shape=[
            jax.ShapeDtypeStruct((count, strip, part), jnp.bfloat16)
            for count in chunks
            for _ in range(groups)
        ],
        compiler_params=pltpu.CompilerParams(vmem_limit_bytes=16 * MIB),
        cost_estimate=pl.CostEstimate(
            flops=2 * ranks * rows * groups * tokens * band_rows,
            bytes_accessed=2
            * groups
            * (ranks * rows * tokens + tokens * band_rows + slots * strip * part),
            transcendentals=0,
        ),
        name="gradient_strips",
    )(meta, *[ctxs[k] for k in pair_order(pairs)], *[piece for rank in cots for piece in rank])
    return [outs[i * groups : (i + 1) * groups] for i in range(len(chunks))]


def gather_block(position, grads, turned):
    for offset, piece in zip(offsets_of(len(grads)), grads):
        _, strip, part = piece.shape
        middle = position ^ offset
        rows = pl.ds(pl.multiple_of(lax.div(middle, 2) * strip, strip), strip)
        columns = pl.ds(pl.multiple_of(lax.rem(middle, 2) * part, part), part)
        turned[rows, columns] = piece[0]


def direction_kernel(groups, halves, meta, second_ref, left_ref, right_ref, *refs):
    grads, outs, turned, rows = refs[:groups], refs[groups : 2 * groups], refs[-2], refs[-1]
    position = meta[0]
    gather_block(position, grads, turned)
    grad_bf16 = turned[...].T
    grad = grad_bf16.astype(jnp.float32)
    second = decay_rate * second_ref[0, 0] + (1.0 - decay_rate) * grad * grad
    adam = grad / (jnp.sqrt(second) + 1e-08)
    half = jnp.dot(
        left_ref[0, 0].astype(jnp.bfloat16), grad_bf16, preferred_element_type=jnp.float32
    )
    shaped = jnp.dot(
        half.astype(jnp.bfloat16),
        right_ref[0, 0].astype(jnp.bfloat16),
        preferred_element_type=jnp.float32,
    )
    adam_sum = jnp.sum(adam * adam, keepdims=True)
    shaped_sum = jnp.sum(shaped * shaped, keepdims=True)
    ratio = jnp.sqrt(adam_sum) / jnp.sqrt(shaped_sum + 1e-06)
    rows[...] = (shaped * ratio).astype(jnp.bfloat16)
    sub = outs[0].shape[1]
    for k, offset in enumerate(offsets_of(groups)):
        middle = position ^ offset
        half, quarter = lax.rem(middle, halves), lax.div(middle, halves)
        start = (half * (groups // halves) + quarter) * sub
        outs[k][0] = rows[pl.ds(pl.multiple_of(start, sub), sub), :]


def directions(meta, grads, first, second, root_left, root_right, halves, sub):
    groups = len(grads)
    slots, strip, part = grads[0].shape
    block = second.shape[-1]
    stat = pl.BlockSpec((1, 1, block, block), lambda s, meta: (0, first + s, 0, 0))
    return pl.pallas_call(
        functools.partial(direction_kernel, groups, halves),
        grid_spec=pltpu.PrefetchScalarGridSpec(
            num_scalar_prefetch=1,
            grid=(slots,),
            in_specs=[stat] * 3
            + [pl.BlockSpec((1, strip, part), lambda s, meta: (s, 0, 0))] * groups,
            out_specs=[pl.BlockSpec((1, sub, block), lambda s, meta: (s, 0, 0))] * groups,
            scratch_shapes=[
                pltpu.VMEM((block, block), jnp.bfloat16),
                pltpu.VMEM((block, block), jnp.bfloat16),
            ],
        ),
        out_shape=[jax.ShapeDtypeStruct((slots, sub, block), jnp.bfloat16)] * groups,
        compiler_params=pltpu.CompilerParams(vmem_limit_bytes=8 * MIB),
        cost_estimate=pl.CostEstimate(
            flops=4 * slots * block**3,
            bytes_accessed=16 * slots * block * block,
            transcendentals=0,
        ),
        name="directions",
    )(meta, second, root_left, root_right, *grads)


def statistics_kernel(groups, chunks, meta, left_ref, right_ref, second_ref, *refs):
    grads = refs[: groups * len(chunks)]
    left_out, right_out, second_out, turned = refs[groups * len(chunks) :]
    slot = pl.program_id(0)
    for i, count in enumerate(chunks):
        first = sum(chunks[:i])

        @pl.when(jnp.logical_and(slot >= first, slot < first + count))
        def _():
            gather_block(meta[0], grads[i * groups : (i + 1) * groups], turned)

    block = turned.shape[0]
    grad_t = turned[...]
    grad_bf16 = grad_t.T
    grad = grad_bf16.astype(jnp.float32)
    gram_left = jnp.dot(grad_bf16, grad_t, preferred_element_type=jnp.float32)
    gram_right = jnp.dot(grad_t, grad_bf16, preferred_element_type=jnp.float32)
    left_out[0, 0] = decay_rate * left_ref[0, 0] + (1.0 - decay_rate) * gram_left / block
    right_out[0, 0] = decay_rate * right_ref[0, 0] + (1.0 - decay_rate) * gram_right / block
    second_out[0, 0] = decay_rate * second_ref[0, 0] + (1.0 - decay_rate) * grad * grad


def statistics(meta, grads, left_stat, right_stat, second):
    groups, chunks = len(grads[0]), [chunk[0].shape[0] for chunk in grads]
    _, strip, part = grads[0][0].shape
    block = second.shape[-1]
    slots = sum(chunks)
    stat = pl.BlockSpec((1, 1, block, block), lambda s, meta: (0, s, 0, 0))

    def strip_spec(first, count):
        return pl.BlockSpec(
            (1, strip, part), lambda s, meta: (jnp.clip(s - first, 0, count - 1), 0, 0)
        )

    strip_specs = [
        strip_spec(sum(chunks[:i]), count) for i, count in enumerate(chunks) for _ in range(groups)
    ]
    return pl.pallas_call(
        functools.partial(statistics_kernel, groups, chunks),
        grid_spec=pltpu.PrefetchScalarGridSpec(
            num_scalar_prefetch=1,
            grid=(slots,),
            in_specs=[stat] * 3 + strip_specs,
            out_specs=[stat] * 3,
            scratch_shapes=[pltpu.VMEM((block, block), jnp.bfloat16)],
        ),
        out_shape=[jax.ShapeDtypeStruct(left_stat.shape, jnp.float32)] * 3,
        compiler_params=pltpu.CompilerParams(vmem_limit_bytes=8 * MIB),
        cost_estimate=pl.CostEstimate(
            flops=4 * slots * block**3,
            bytes_accessed=26 * slots * block * block,
            transcendentals=0,
        ),
        name="statistics",
    )(meta, left_stat, right_stat, second, *[piece for chunk in grads for piece in chunk])


def regroup_kernel(groups, chunks, bands, halves, meta, *refs):
    inputs, outs, placed = refs[: groups * len(chunks)], refs[groups * len(chunks) : -1], refs[-1]
    block = inputs[0].shape[-1]
    position = meta[0]
    own_band = lax.div(position, halves)
    slots = sum(chunks)
    offsets = offsets_of(groups)

    def place(first, pieces, s, carry):
        for k in range(groups):
            block_id = meta[2 + (position ^ offsets[k]) * slots + first + s]
            row_band, col_band = lax.div(block_id, bands), lax.rem(block_id, bands)
            columns = pl.ds(pl.multiple_of(col_band * block, block), block)
            placed[row_band ^ own_band, :, columns] = pieces[k][s]
        return carry

    for i, count in enumerate(chunks):
        pieces = inputs[i * groups : (i + 1) * groups]
        lax.fori_loop(0, count, functools.partial(place, sum(chunks[:i]), pieces), 0)
    for k in range(len(outs)):
        outs[k][...] = placed[k]


def regroup(meta, pieces, bands, halves):
    groups, chunks = len(pieces[0]), [chunk[0].shape[0] for chunk in pieces]
    _, sub, block = pieces[0][0].shape
    row_bands = groups // halves
    return pl.pallas_call(
        functools.partial(regroup_kernel, groups, chunks, bands, halves),
        grid_spec=pltpu.PrefetchScalarGridSpec(
            num_scalar_prefetch=1,
            grid=(),
            in_specs=[pl.BlockSpec(memory_space=pltpu.VMEM)] * (groups * len(chunks)),
            out_specs=[pl.BlockSpec(memory_space=pltpu.VMEM)] * row_bands,
            scratch_shapes=[pltpu.VMEM((row_bands, sub, bands * block), jnp.bfloat16)],
        ),
        out_shape=[jax.ShapeDtypeStruct((sub, bands * block), jnp.bfloat16)] * row_bands,
        compiler_params=pltpu.CompilerParams(vmem_limit_bytes=8 * MIB),
        cost_estimate=pl.CostEstimate(
            flops=0,
            bytes_accessed=4 * row_bands * sub * bands * block,
            transcendentals=0,
        ),
        name="regroup",
    )(meta, *[piece for chunk in pieces for piece in chunk])


def stack_kernel(halves, meta, *refs):
    pieces, out, sems = refs[:-2], refs[-2], refs[-1]
    sub = pieces[0].shape[0]
    own_band = lax.div(meta[0], halves)
    copies = []
    for k, piece in enumerate(pieces):
        start = pl.multiple_of((own_band ^ k) * sub, sub)
        copies.append(pltpu.make_async_copy(piece, out.at[0, pl.ds(start, sub), :], sems.at[k]))
    for copy in copies:
        copy.start()
    for copy in copies:
        copy.wait()


def stack_rows(meta, pieces, halves):
    count = len(pieces)
    sub, width = pieces[0].shape
    return pl.pallas_call(
        functools.partial(stack_kernel, halves),
        grid_spec=pltpu.PrefetchScalarGridSpec(
            num_scalar_prefetch=1,
            grid=(),
            in_specs=[pl.BlockSpec(memory_space=pltpu.VMEM)] * count,
            out_specs=pl.BlockSpec(memory_space=pl.ANY),
            scratch_shapes=[pltpu.SemaphoreType.DMA((count,))],
        ),
        out_shape=jax.ShapeDtypeStruct((1, count * sub, width), jnp.bfloat16),
        compiler_params=pltpu.CompilerParams(vmem_limit_bytes=4 * MIB),
        cost_estimate=pl.CostEstimate(
            flops=0, bytes_accessed=4 * count * sub * width, transcendentals=0
        ),
        name="stack_rows",
    )(meta, *pieces)


def exchange(pieces, offsets):
    return [swap(piece, "fsdp", k) if k else piece for piece, k in zip(pieces, offsets)]


def strip_plan(
    context, cotangent, block_table, left_stat, right_stat, root_left, root_right, second_moment
):
    groups, ranks = lax.axis_size("fsdp"), lax.axis_size("tensor")
    band_rows = context.shape[1]
    block, slots = left_stat.shape[-1], left_stat.shape[1]
    bands = cotangent.shape[1] * ranks // block
    strip_rows = band_rows // groups
    place = jnp.stack([lax.axis_index("fsdp"), lax.axis_index("tensor")]).astype(jnp.int32)
    meta = jnp.concatenate([place, block_table[0]])

    pairs, tokens = groups // 2, context.shape[0]
    offsets = offsets_of(groups)
    strips, own, other = prepare(meta, cotangent, context, pairs, block)
    strips = exchange(strips, range(0, groups, 2))
    other = swap(other, "fsdp", 1)
    strips, other = lax.optimization_barrier((strips, other))
    strips = jnp.stack(strips).reshape(pairs, -1, tokens)
    ctxs = [jnp.stack([own, other])] + [None] * (pairs - 1)
    far = pairs // 2
    ctxs[far] = swap(ctxs[0], "fsdp", 2 * far)
    step = 1
    while step < far:
        for k in range(step):
            ctxs[step + k] = swap(ctxs[k], "fsdp", 2 * step)
            ctxs[far + step + k] = swap(ctxs[far + k], "fsdp", 2 * step)
        step *= 2
    by_pair = swap(strips, "fsdp", 1)
    by_rank = swap(strips, "tensor", ranks // 2)
    to_rank, to_pair = by_pair[:far], by_rank[far:]
    to_rank, _ = lax.optimization_barrier((to_rank, ctxs[1]))
    across = [
        by_rank,
        swap(to_rank, "tensor", ranks // 2),
        swap(to_pair, "fsdp", 1),
    ]
    cots = {0: [strips, by_pair], ranks // 2: across}
    offset = ranks // 4
    while offset:
        for known in list(cots):
            here = list(cots[known])
            if known:
                here[0], _ = lax.optimization_barrier((here[0], here[1]))
            cots[known ^ offset] = [swap(piece, "tensor", offset) for piece in here]
        offset //= 2
    cots = [cots[t] for t in range(ranks)]

    chunks = [slots - slots // 2, slots // 2]
    grads = [
        exchange(chunk, offsets) for chunk in gradient_strips(meta, cots, ctxs, chunks, bands, block)
    ]
    halves = block // strip_rows
    sub = strip_rows * halves // groups
    pieces = []
    for i, chunk in enumerate(grads):
        stale = (second_moment, root_left, root_right)
        parts = directions(meta, chunk, sum(chunks[:i]), *stale, halves, sub)
        pieces.append(exchange(parts, offsets))
    left_new, right_new, second_new = statistics(
        meta, grads, left_stat, right_stat, second_moment
    )
    rows = exchange(regroup(meta, pieces, bands, halves), range(0, groups, halves))
    return (left_new, right_new, second_new, stack_rows(meta, rows, halves))


def per_device(context, cotangent, block_table, left_stat, *rest):
    groups, ranks = lax.axis_size("fsdp"), lax.axis_size("tensor")
    block = left_stat.shape[-1]
    strip_rows = context.shape[1] // groups
    powers = groups & (groups - 1) == 0 and ranks & (ranks - 1) == 0
    whole = block % strip_rows == 0 and cotangent.shape[1] % block == 0
    even = block % (16 * groups) == 0 and block == 2 * strip_rows and groups >= 8
    plan = strip_plan if powers and even and whole else general_plan
    return plan(context, cotangent, block_table, left_stat, *rest)


def solution(mesh):
    return jax.shard_map(
        per_device,
        mesh=mesh,
        in_specs=(
            P("fsdp", "tensor"),
            P("fsdp", "tensor"),
            P("tensor", None),
            P("tensor", "fsdp", None, None),
            P("tensor", "fsdp", None, None),
            P("tensor", "fsdp", None, None),
            P("tensor", "fsdp", None, None),
            P("tensor", "fsdp", None, None),
        ),
        out_specs=(
            P("tensor", "fsdp", None, None),
            P("tensor", "fsdp", None, None),
            P("tensor", "fsdp", None, None),
            P("tensor", "fsdp", None),
        ),
        check_vma=False,
    )
```

```python
import functools

import jax
import jax.numpy as jnp
from jax import lax
from jax.experimental import pallas as pl
from jax.experimental.pallas import tpu as pltpu
from jax.sharding import PartitionSpec as P

decay_rate = 0.95
MIB = 1024 * 1024


def general_plan(
    context, cotangent, block_table, left_stat, right_stat, root_left, root_right, second_moment
):
    full_cot = lax.all_gather(cotangent, "tensor", axis=1, tiled=True)
    tokens_here, band_rows = context.shape
    model_width = full_cot.shape[1]
    block_size = left_stat.shape[-1]
    slot_count = left_stat.shape[1]
    groups = lax.axis_size("fsdp")
    position = lax.axis_index("fsdp")
    owner_table = block_table[0]
    col_bands = model_width // block_size
    strip_rows = band_rows // groups
    per_band = block_size // strip_rows
    my_blocks = lax.dynamic_slice_in_dim(owner_table, position * slot_count, slot_count)
    ctx_bands = context.reshape(tokens_here, band_rows // block_size, block_size)
    cot_bands = full_cot.reshape(tokens_here, col_bands, block_size)
    left_part = jnp.take(ctx_bands, owner_table // col_bands, axis=1)
    right_part = jnp.take(cot_bands, owner_table % col_bands, axis=1)
    blocks = jnp.einsum("tnb,tnc->nbc", left_part, right_part, preferred_element_type=jnp.float32)
    gradient = lax.psum_scatter(
        blocks.reshape(slot_count * block_size * lax.axis_size("fsdp"), block_size).astype(
            jnp.bfloat16
        ),
        "fsdp",
        scatter_dimension=0,
        tiled=True,
    ).astype(jnp.float32)
    gradient = gradient.reshape(slot_count, block_size, block_size)
    highest = lax.Precision.HIGHEST
    gram_left = jnp.einsum("sij,skj->sik", gradient, gradient, precision=highest)
    gram_right = jnp.einsum("sji,sjk->sik", gradient, gradient, precision=highest)
    left_new = decay_rate * left_stat[0] + (1.0 - decay_rate) * gram_left / block_size
    right_new = decay_rate * right_stat[0] + (1.0 - decay_rate) * gram_right / block_size
    second_new = decay_rate * second_moment[0] + (1.0 - decay_rate) * gradient * gradient
    adam_step = gradient / (jnp.sqrt(second_new) + 1e-08)
    shaped = jnp.einsum("sij,sjk->sik", root_left[0], gradient, precision=highest)
    shaped = jnp.einsum("sij,sjk->sik", shaped, root_right[0], precision=highest)
    graft_ratio = jnp.sqrt(jnp.sum(adam_step * adam_step, axis=(1, 2))) / jnp.sqrt(
        jnp.sum(shaped * shaped, axis=(1, 2)) + 1e-06
    )
    direction = (shaped * graft_ratio[:, None, None]).astype(jnp.bfloat16)
    by_strip = direction.reshape(slot_count, per_band, strip_rows, block_size)
    targets = jnp.arange(groups, dtype=jnp.int32)
    chosen = jnp.take(by_strip, targets % per_band, axis=1)
    keep_mask = ((my_blocks // col_bands)[:, None] == (targets // per_band)[None, :]).astype(
        jnp.bfloat16
    )
    outgoing_rows = jnp.swapaxes(chosen * keep_mask[:, :, None, None], 0, 1)
    returned = lax.all_to_all(outgoing_rows, "fsdp", split_axis=0, concat_axis=0, tiled=True)
    wanted = position // per_band * col_bands + jnp.arange(col_bands, dtype=jnp.int32)
    slot_ids = jnp.arange(owner_table.shape[0], dtype=jnp.int32)
    located = jnp.sum(
        jnp.where(owner_table[None, :] == wanted[:, None], slot_ids[None, :], 0), axis=1
    )
    flat_pieces = returned.reshape(groups * slot_count, strip_rows, block_size)
    pieces = jnp.take(flat_pieces, located, axis=0)
    result = jnp.swapaxes(pieces, 0, 1).reshape(strip_rows, model_width)
    return (left_new[None], right_new[None], second_new[None], result[None])


def swap(value, axis, offset):
    count = lax.axis_size(axis)
    return lax.ppermute(value, axis, [(i, i ^ offset) for i in range(count)])


def offsets_of(groups):
    far, near = range(groups // 2, groups), range(1, groups // 2)
    order = [k for pair in zip(far, near) for k in pair]
    return [*order, groups - 1, 0]


def pair_order(pairs):
    return [pairs // 2, 0, *[k for k in range(1, pairs) if k != pairs // 2]]


def strip_kernel(pairs, cot_ref, *refs):
    outs, turned = refs[:pairs], refs[pairs]
    strip = turned.shape[0] // pairs
    pair = lax.div(lax.axis_index("fsdp"), 2)
    turned[...] = cot_ref[...].T
    for k in range(pairs):
        start = pl.multiple_of((pair ^ k) * strip, strip)
        outs[k][0] = turned[pl.ds(start, strip), :]


def cot_strips(cotangent, pairs, block):
    tokens, width = cotangent.shape
    bands, strip = width // block, block // pairs
    return pl.pallas_call(
        functools.partial(strip_kernel, pairs),
        grid=(bands,),
        in_specs=[pl.BlockSpec((tokens, block), lambda c: (0, c))],
        out_specs=[pl.BlockSpec((1, strip, tokens), lambda c: (c, 0, 0))] * pairs,
        scratch_shapes=[pltpu.VMEM((block, tokens), jnp.bfloat16)],
        out_shape=[jax.ShapeDtypeStruct((bands, strip, tokens), jnp.bfloat16)] * pairs,
        compiler_params=pltpu.CompilerParams(vmem_limit_bytes=8 * MIB),
        cost_estimate=pl.CostEstimate(
            flops=0, bytes_accessed=4 * tokens * width, transcendentals=0
        ),
        name="cot_strips",
    )(cotangent)


def column_kernel(block, context_ref, own, other):
    half = block // 2
    side = lax.rem(lax.axis_index("fsdp"), 2)
    for out, place in ((own, side), (other, side ^ 1)):
        for r in range(out.shape[1] // half):
            start = pl.multiple_of(r * block + place * half, half)
            out[:, r * half : (r + 1) * half] = context_ref[:, pl.ds(start, half)]


def column_halves(context, block):
    tokens, width = context.shape
    return pl.pallas_call(
        functools.partial(column_kernel, block),
        in_specs=[pl.BlockSpec(memory_space=pltpu.VMEM)],
        out_specs=[pl.BlockSpec(memory_space=pltpu.VMEM)] * 2,
        out_shape=[jax.ShapeDtypeStruct((tokens, width // 2), jnp.bfloat16)] * 2,
        compiler_params=pltpu.CompilerParams(vmem_limit_bytes=8 * MIB),
        cost_estimate=pl.CostEstimate(
            flops=0, bytes_accessed=4 * tokens * width, transcendentals=0
        ),
        name="column_halves",
    )(context)


def gradient_kernel(groups, ranks, sources, chunks, bands, table, *refs):
    pairs = groups // 2
    count = 1 + max(source for source, _ in sources)
    order = pair_order(pairs)
    ctxs, cots = [refs[order.index(k)] for k in range(pairs)], refs[pairs : count + pairs]
    outs, strips = refs[count + pairs : -1], refs[-1]
    slots = sum(chunks)
    rows = cots[0].shape[1]
    strip, part = outs[0].shape[1:]
    position, rank = lax.axis_index("fsdp"), lax.axis_index("tensor")
    rhs = jnp.concatenate([ctxs[k // 2][k % 2] for k in range(groups)], axis=0)
    for t in range(ranks):
        found = sources[t * groups : (t + 1) * groups]
        lhs = jnp.concatenate([cots[source][place] for source, place in found], axis=1)
        strips[pl.ds(t * rows, rows), :] = jnp.dot(
            lhs, rhs, preferred_element_type=jnp.float32
        ).astype(jnp.bfloat16)
    own_bands = bands // ranks
    offsets = offsets_of(groups)

    def place(first, pieces, s, carry):
        for k in range(groups):
            block_id = table[(position ^ offsets[k]) * slots + first + s]
            row_band, col_band = lax.div(block_id, bands), lax.rem(block_id, bands)
            piece = lax.div(col_band, own_bands) ^ rank
            start = piece * rows + lax.rem(col_band, own_bands) * strip
            pieces[k][s] = strips[
                pl.ds(pl.multiple_of(start, strip), strip),
                pl.ds(pl.multiple_of(row_band * part, part), part),
            ]
        return carry

    for i, count in enumerate(chunks):
        pieces = outs[i * groups : (i + 1) * groups]
        lax.fori_loop(0, count, functools.partial(place, sum(chunks[:i]), pieces), 0)


def gradient_strips(table, cots, ctxs, chunks, bands, block):
    ranks, pairs = len(cots), len(ctxs)
    groups = 2 * pairs
    sources, first = [], 0
    for own, *other in cots:
        places = [(first + 1 + i, n) for i, piece in enumerate(other) for n in range(piece.shape[0])]
        for pair in range(pairs):
            sources += [(first, pair), places[pair]]
        first += 1 + len(other)
    _, tokens, band_rows = ctxs[0].shape
    rows = cots[0][0].shape[1]
    strip, part = block // pairs, block // 2
    slots = sum(chunks)
    outs = pl.pallas_call(
        functools.partial(gradient_kernel, groups, ranks, sources, chunks, bands),
        grid_spec=pltpu.PrefetchScalarGridSpec(
            num_scalar_prefetch=1,
            grid=(),
            in_specs=[pl.BlockSpec(memory_space=pltpu.VMEM)] * (first + pairs),
            out_specs=[pl.BlockSpec(memory_space=pltpu.VMEM)] * (groups * len(chunks)),
            scratch_shapes=[pltpu.VMEM((ranks * rows, band_rows), jnp.bfloat16)],
        ),
        out_shape=[
            jax.ShapeDtypeStruct((count, strip, part), jnp.bfloat16)
            for count in chunks
            for _ in range(groups)
        ],
        compiler_params=pltpu.CompilerParams(vmem_limit_bytes=16 * MIB),
        cost_estimate=pl.CostEstimate(
            flops=2 * ranks * rows * groups * tokens * band_rows,
            bytes_accessed=2
            * groups
            * (ranks * rows * tokens + tokens * band_rows + slots * strip * part),
            transcendentals=0,
        ),
        name="gradient_strips",
    )(table, *[ctxs[k] for k in pair_order(pairs)], *[piece for rank in cots for piece in rank])
    return [outs[i * groups : (i + 1) * groups] for i in range(len(chunks))]


def gather_block(position, grads, turned):
    for offset, piece in zip(offsets_of(len(grads)), grads):
        _, strip, part = piece.shape
        middle = position ^ offset
        rows = pl.ds(pl.multiple_of(lax.div(middle, 2) * strip, strip), strip)
        columns = pl.ds(pl.multiple_of(lax.rem(middle, 2) * part, part), part)
        turned[rows, columns] = piece[0]


def direction_kernel(groups, halves, table, second_ref, left_ref, right_ref, *refs):
    grads, outs, turned, rows = refs[:groups], refs[groups : 2 * groups], refs[-2], refs[-1]
    position = lax.axis_index("fsdp")
    gather_block(position, grads, turned)
    grad_bf16 = turned[...].T
    grad = grad_bf16.astype(jnp.float32)
    second = decay_rate * second_ref[0, 0] + (1.0 - decay_rate) * grad * grad
    adam = grad / (jnp.sqrt(second) + 1e-08)
    half = jnp.dot(
        left_ref[0, 0].astype(jnp.bfloat16), grad_bf16, preferred_element_type=jnp.float32
    )
    shaped = jnp.dot(
        half.astype(jnp.bfloat16),
        right_ref[0, 0].astype(jnp.bfloat16),
        preferred_element_type=jnp.float32,
    )
    adam_sum = jnp.sum(adam * adam, keepdims=True)
    shaped_sum = jnp.sum(shaped * shaped, keepdims=True)
    ratio = jnp.sqrt(adam_sum) / jnp.sqrt(shaped_sum + 1e-06)
    rows[...] = (shaped * ratio).astype(jnp.bfloat16)
    sub = outs[0].shape[1]
    for k, offset in enumerate(offsets_of(groups)):
        middle = position ^ offset
        half, quarter = lax.rem(middle, halves), lax.div(middle, halves)
        start = (half * (groups // halves) + quarter) * sub
        outs[k][0] = rows[pl.ds(pl.multiple_of(start, sub), sub), :]


def directions(table, grads, first, second, root_left, root_right, halves, sub):
    groups = len(grads)
    slots, strip, part = grads[0].shape
    block = second.shape[-1]
    stat = pl.BlockSpec((1, 1, block, block), lambda s, table: (0, first + s, 0, 0))
    return pl.pallas_call(
        functools.partial(direction_kernel, groups, halves),
        grid_spec=pltpu.PrefetchScalarGridSpec(
            num_scalar_prefetch=1,
            grid=(slots,),
            in_specs=[stat] * 3
            + [pl.BlockSpec((1, strip, part), lambda s, table: (s, 0, 0))] * groups,
            out_specs=[pl.BlockSpec((1, sub, block), lambda s, table: (s, 0, 0))] * groups,
            scratch_shapes=[
                pltpu.VMEM((block, block), jnp.bfloat16),
                pltpu.VMEM((block, block), jnp.bfloat16),
            ],
        ),
        out_shape=[jax.ShapeDtypeStruct((slots, sub, block), jnp.bfloat16)] * groups,
        compiler_params=pltpu.CompilerParams(vmem_limit_bytes=8 * MIB),
        cost_estimate=pl.CostEstimate(
            flops=4 * slots * block**3,
            bytes_accessed=16 * slots * block * block,
            transcendentals=0,
        ),
        name="directions",
    )(table, second, root_left, root_right, *grads)


def statistics_kernel(groups, chunks, table, left_ref, right_ref, second_ref, *refs):
    grads = refs[: groups * len(chunks)]
    left_out, right_out, second_out, turned = refs[groups * len(chunks) :]
    slot = pl.program_id(0)
    for i, count in enumerate(chunks):
        first = sum(chunks[:i])

        @pl.when(jnp.logical_and(slot >= first, slot < first + count))
        def _():
            gather_block(lax.axis_index("fsdp"), grads[i * groups : (i + 1) * groups], turned)

    block = turned.shape[0]
    grad_t = turned[...]
    grad_bf16 = grad_t.T
    grad = grad_bf16.astype(jnp.float32)
    gram_left = jnp.dot(grad_bf16, grad_t, preferred_element_type=jnp.float32)
    gram_right = jnp.dot(grad_t, grad_bf16, preferred_element_type=jnp.float32)
    left_out[0, 0] = decay_rate * left_ref[0, 0] + (1.0 - decay_rate) * gram_left / block
    right_out[0, 0] = decay_rate * right_ref[0, 0] + (1.0 - decay_rate) * gram_right / block
    second_out[0, 0] = decay_rate * second_ref[0, 0] + (1.0 - decay_rate) * grad * grad


def statistics(table, grads, left_stat, right_stat, second):
    groups, chunks = len(grads[0]), [chunk[0].shape[0] for chunk in grads]
    _, strip, part = grads[0][0].shape
    block = second.shape[-1]
    slots = sum(chunks)
    stat = pl.BlockSpec((1, 1, block, block), lambda s, table: (0, s, 0, 0))

    def strip_spec(first, count):
        return pl.BlockSpec(
            (1, strip, part), lambda s, table: (jnp.clip(s - first, 0, count - 1), 0, 0)
        )

    strip_specs = [
        strip_spec(sum(chunks[:i]), count) for i, count in enumerate(chunks) for _ in range(groups)
    ]
    return pl.pallas_call(
        functools.partial(statistics_kernel, groups, chunks),
        grid_spec=pltpu.PrefetchScalarGridSpec(
            num_scalar_prefetch=1,
            grid=(slots,),
            in_specs=[stat] * 3 + strip_specs,
            out_specs=[stat] * 3,
            scratch_shapes=[pltpu.VMEM((block, block), jnp.bfloat16)],
        ),
        out_shape=[jax.ShapeDtypeStruct(left_stat.shape, jnp.float32)] * 3,
        compiler_params=pltpu.CompilerParams(vmem_limit_bytes=8 * MIB),
        cost_estimate=pl.CostEstimate(
            flops=4 * slots * block**3,
            bytes_accessed=26 * slots * block * block,
            transcendentals=0,
        ),
        name="statistics",
    )(table, left_stat, right_stat, second, *[piece for chunk in grads for piece in chunk])


def regroup_kernel(groups, chunks, bands, halves, table, *refs):
    inputs, outs, placed = refs[: groups * len(chunks)], refs[groups * len(chunks) : -1], refs[-1]
    block = inputs[0].shape[-1]
    position = lax.axis_index("fsdp")
    own_band = lax.div(position, halves)
    slots = sum(chunks)
    offsets = offsets_of(groups)

    def place(first, pieces, s, carry):
        for k in range(groups):
            block_id = table[(position ^ offsets[k]) * slots + first + s]
            row_band, col_band = lax.div(block_id, bands), lax.rem(block_id, bands)
            columns = pl.ds(pl.multiple_of(col_band * block, block), block)
            placed[row_band ^ own_band, :, columns] = pieces[k][s]
        return carry

    for i, count in enumerate(chunks):
        pieces = inputs[i * groups : (i + 1) * groups]
        lax.fori_loop(0, count, functools.partial(place, sum(chunks[:i]), pieces), 0)
    for k in range(len(outs)):
        outs[k][...] = placed[k]


def regroup(table, pieces, bands, halves):
    groups, chunks = len(pieces[0]), [chunk[0].shape[0] for chunk in pieces]
    _, sub, block = pieces[0][0].shape
    row_bands = groups // halves
    return pl.pallas_call(
        functools.partial(regroup_kernel, groups, chunks, bands, halves),
        grid_spec=pltpu.PrefetchScalarGridSpec(
            num_scalar_prefetch=1,
            grid=(),
            in_specs=[pl.BlockSpec(memory_space=pltpu.VMEM)] * (groups * len(chunks)),
            out_specs=[pl.BlockSpec(memory_space=pltpu.VMEM)] * row_bands,
            scratch_shapes=[pltpu.VMEM((row_bands, sub, bands * block), jnp.bfloat16)],
        ),
        out_shape=[jax.ShapeDtypeStruct((sub, bands * block), jnp.bfloat16)] * row_bands,
        compiler_params=pltpu.CompilerParams(vmem_limit_bytes=8 * MIB),
        cost_estimate=pl.CostEstimate(
            flops=0,
            bytes_accessed=4 * row_bands * sub * bands * block,
            transcendentals=0,
        ),
        name="regroup",
    )(table, *[piece for chunk in pieces for piece in chunk])


def stack_kernel(halves, table, *refs):
    pieces, out, sems = refs[:-2], refs[-2], refs[-1]
    sub = pieces[0].shape[0]
    own_band = lax.div(lax.axis_index("fsdp"), halves)
    copies = []
    for k, piece in enumerate(pieces):
        start = pl.multiple_of((own_band ^ k) * sub, sub)
        copies.append(pltpu.make_async_copy(piece, out.at[0, pl.ds(start, sub), :], sems.at[k]))
    for copy in copies:
        copy.start()
    for copy in copies:
        copy.wait()


def stack_rows(table, pieces, halves):
    count = len(pieces)
    sub, width = pieces[0].shape
    return pl.pallas_call(
        functools.partial(stack_kernel, halves),
        grid_spec=pltpu.PrefetchScalarGridSpec(
            num_scalar_prefetch=1,
            grid=(),
            in_specs=[pl.BlockSpec(memory_space=pltpu.VMEM)] * count,
            out_specs=pl.BlockSpec(memory_space=pl.ANY),
            scratch_shapes=[pltpu.SemaphoreType.DMA((count,))],
        ),
        out_shape=jax.ShapeDtypeStruct((1, count * sub, width), jnp.bfloat16),
        compiler_params=pltpu.CompilerParams(vmem_limit_bytes=4 * MIB),
        cost_estimate=pl.CostEstimate(
            flops=0, bytes_accessed=4 * count * sub * width, transcendentals=0
        ),
        name="stack_rows",
    )(table, *pieces)


def exchange(pieces, offsets):
    return [swap(piece, "fsdp", k) if k else piece for piece, k in zip(pieces, offsets)]


def strip_plan(
    context, cotangent, block_table, left_stat, right_stat, root_left, root_right, second_moment
):
    groups, ranks = lax.axis_size("fsdp"), lax.axis_size("tensor")
    band_rows = context.shape[1]
    block, slots = left_stat.shape[-1], left_stat.shape[1]
    bands = cotangent.shape[1] * ranks // block
    strip_rows = band_rows // groups
    table = block_table[0]

    pairs, tokens = groups // 2, context.shape[0]
    offsets = offsets_of(groups)
    strips = cot_strips(cotangent, pairs, block)
    context, _ = lax.optimization_barrier((context, strips[0]))
    own, other = column_halves(context, block)
    strips = exchange(strips, range(0, groups, 2))
    other = swap(other, "fsdp", 1)
    strips, other = lax.optimization_barrier((strips, other))
    strips = jnp.stack(strips).reshape(pairs, -1, tokens)
    ctxs = [jnp.stack([own, other])] + [None] * (pairs - 1)
    far = pairs // 2
    ctxs[far] = swap(ctxs[0], "fsdp", 2 * far)
    step = 1
    while step < far:
        for k in range(step):
            ctxs[step + k] = swap(ctxs[k], "fsdp", 2 * step)
            ctxs[far + step + k] = swap(ctxs[far + k], "fsdp", 2 * step)
        step *= 2
    by_pair = swap(strips, "fsdp", 1)
    by_rank = swap(strips, "tensor", ranks // 2)
    to_rank, to_pair = by_pair[:far], by_rank[far:]
    to_rank, _ = lax.optimization_barrier((to_rank, ctxs[1]))
    across = [
        by_rank,
        swap(to_rank, "tensor", ranks // 2),
        swap(to_pair, "fsdp", 1),
    ]
    cots = {0: [strips, by_pair], ranks // 2: across}
    offset = ranks // 4
    while offset:
        for known in list(cots):
            here = list(cots[known])
            if known:
                here[0], _ = lax.optimization_barrier((here[0], here[1]))
            cots[known ^ offset] = [swap(piece, "tensor", offset) for piece in here]
        offset //= 2
    cots = [cots[t] for t in range(ranks)]

    chunks = [slots - slots // 2, slots // 2]
    grads = [
        exchange(chunk, offsets) for chunk in gradient_strips(table, cots, ctxs, chunks, bands, block)
    ]
    halves = block // strip_rows
    sub = strip_rows * halves // groups
    pieces = []
    for i, chunk in enumerate(grads):
        stale = (second_moment, root_left, root_right)
        parts = directions(table, chunk, sum(chunks[:i]), *stale, halves, sub)
        pieces.append(exchange(parts, offsets))
    left_new, right_new, second_new = statistics(
        table, grads, left_stat, right_stat, second_moment
    )
    rows = exchange(regroup(table, pieces, bands, halves), range(0, groups, halves))
    return (left_new, right_new, second_new, stack_rows(table, rows, halves))


def per_device(context, cotangent, block_table, left_stat, *rest):
    groups, ranks = lax.axis_size("fsdp"), lax.axis_size("tensor")
    block = left_stat.shape[-1]
    strip_rows = context.shape[1] // groups
    powers = groups & (groups - 1) == 0 and ranks & (ranks - 1) == 0
    whole = block % strip_rows == 0 and cotangent.shape[1] % block == 0
    even = block % (16 * groups) == 0 and block == 2 * strip_rows and groups >= 8
    plan = strip_plan if powers and even and whole else general_plan
    return plan(context, cotangent, block_table, left_stat, *rest)


def solution(mesh):
    return jax.shard_map(
        per_device,
        mesh=mesh,
        in_specs=(
            P("fsdp", "tensor"),
            P("fsdp", "tensor"),
            P("tensor", None),
            P("tensor", "fsdp", None, None),
            P("tensor", "fsdp", None, None),
            P("tensor", "fsdp", None, None),
            P("tensor", "fsdp", None, None),
            P("tensor", "fsdp", None, None),
        ),
        out_specs=(
            P("tensor", "fsdp", None, None),
            P("tensor", "fsdp", None, None),
            P("tensor", "fsdp", None, None),
            P("tensor", "fsdp", None),
        ),
        check_vma=False,
    )
```

```python
import functools

import jax
import jax.numpy as jnp
from jax import lax
from jax.experimental import pallas as pl
from jax.experimental.pallas import tpu as pltpu
from jax.sharding import PartitionSpec as P

decay_rate = 0.95
MIB = 1024 * 1024
TOGETHER = 4


def general_plan(
    context, cotangent, block_table, left_stat, right_stat, root_left, root_right, second_moment
):
    full_cot = lax.all_gather(cotangent, "tensor", axis=1, tiled=True)
    tokens_here, band_rows = context.shape
    model_width = full_cot.shape[1]
    block_size = left_stat.shape[-1]
    slot_count = left_stat.shape[1]
    groups = lax.axis_size("fsdp")
    position = lax.axis_index("fsdp")
    owner_table = block_table[0]
    col_bands = model_width // block_size
    strip_rows = band_rows // groups
    per_band = block_size // strip_rows
    my_blocks = lax.dynamic_slice_in_dim(owner_table, position * slot_count, slot_count)
    ctx_bands = context.reshape(tokens_here, band_rows // block_size, block_size)
    cot_bands = full_cot.reshape(tokens_here, col_bands, block_size)
    left_part = jnp.take(ctx_bands, owner_table // col_bands, axis=1)
    right_part = jnp.take(cot_bands, owner_table % col_bands, axis=1)
    blocks = jnp.einsum("tnb,tnc->nbc", left_part, right_part, preferred_element_type=jnp.float32)
    gradient = lax.psum_scatter(
        blocks.reshape(slot_count * block_size * lax.axis_size("fsdp"), block_size).astype(
            jnp.bfloat16
        ),
        "fsdp",
        scatter_dimension=0,
        tiled=True,
    ).astype(jnp.float32)
    gradient = gradient.reshape(slot_count, block_size, block_size)
    highest = lax.Precision.HIGHEST
    gram_left = jnp.einsum("sij,skj->sik", gradient, gradient, precision=highest)
    gram_right = jnp.einsum("sji,sjk->sik", gradient, gradient, precision=highest)
    left_new = decay_rate * left_stat[0] + (1.0 - decay_rate) * gram_left / block_size
    right_new = decay_rate * right_stat[0] + (1.0 - decay_rate) * gram_right / block_size
    second_new = decay_rate * second_moment[0] + (1.0 - decay_rate) * gradient * gradient
    adam_step = gradient / (jnp.sqrt(second_new) + 1e-08)
    shaped = jnp.einsum("sij,sjk->sik", root_left[0], gradient, precision=highest)
    shaped = jnp.einsum("sij,sjk->sik", shaped, root_right[0], precision=highest)
    graft_ratio = jnp.sqrt(jnp.sum(adam_step * adam_step, axis=(1, 2))) / jnp.sqrt(
        jnp.sum(shaped * shaped, axis=(1, 2)) + 1e-06
    )
    direction = (shaped * graft_ratio[:, None, None]).astype(jnp.bfloat16)
    by_strip = direction.reshape(slot_count, per_band, strip_rows, block_size)
    targets = jnp.arange(groups, dtype=jnp.int32)
    chosen = jnp.take(by_strip, targets % per_band, axis=1)
    keep_mask = ((my_blocks // col_bands)[:, None] == (targets // per_band)[None, :]).astype(
        jnp.bfloat16
    )
    outgoing_rows = jnp.swapaxes(chosen * keep_mask[:, :, None, None], 0, 1)
    returned = lax.all_to_all(outgoing_rows, "fsdp", split_axis=0, concat_axis=0, tiled=True)
    wanted = position // per_band * col_bands + jnp.arange(col_bands, dtype=jnp.int32)
    slot_ids = jnp.arange(owner_table.shape[0], dtype=jnp.int32)
    located = jnp.sum(
        jnp.where(owner_table[None, :] == wanted[:, None], slot_ids[None, :], 0), axis=1
    )
    flat_pieces = returned.reshape(groups * slot_count, strip_rows, block_size)
    pieces = jnp.take(flat_pieces, located, axis=0)
    result = jnp.swapaxes(pieces, 0, 1).reshape(strip_rows, model_width)
    return (left_new[None], right_new[None], second_new[None], result[None])


def swap(value, axis, offset):
    count = lax.axis_size(axis)
    return lax.ppermute(value, axis, [(i, i ^ offset) for i in range(count)])


def offsets_of(groups):
    far, near = range(groups // 2, groups), range(1, groups // 2)
    order = [k for pair in zip(far, near) for k in pair]
    return [*order, groups - 1, 0]


def pair_order(pairs):
    return [pairs // 2, 0, *[k for k in range(1, pairs) if k != pairs // 2]]


def strip_kernel(pairs, cot_ref, *refs):
    outs, turned = refs[:pairs], refs[pairs]
    strip = turned.shape[0] // pairs
    pair = lax.div(lax.axis_index("fsdp"), 2)
    turned[...] = cot_ref[...].T
    for k in range(pairs):
        start = pl.multiple_of((pair ^ k) * strip, strip)
        outs[k][0] = turned[pl.ds(start, strip), :]


def cot_strips(cotangent, pairs, block):
    tokens, width = cotangent.shape
    bands, strip = width // block, block // pairs
    return pl.pallas_call(
        functools.partial(strip_kernel, pairs),
        grid=(bands,),
        in_specs=[pl.BlockSpec((tokens, block), lambda c: (0, c))],
        out_specs=[pl.BlockSpec((1, strip, tokens), lambda c: (c, 0, 0))] * pairs,
        scratch_shapes=[pltpu.VMEM((block, tokens), jnp.bfloat16)],
        out_shape=[jax.ShapeDtypeStruct((bands, strip, tokens), jnp.bfloat16)] * pairs,
        compiler_params=pltpu.CompilerParams(vmem_limit_bytes=8 * MIB),
        cost_estimate=pl.CostEstimate(
            flops=0, bytes_accessed=4 * tokens * width, transcendentals=0
        ),
        name="cot_strips",
    )(cotangent)


def column_kernel(block, context_ref, own, other):
    half = block // 2
    side = lax.rem(lax.axis_index("fsdp"), 2)
    for out, place in ((own, side), (other, side ^ 1)):
        for r in range(out.shape[1] // half):
            start = pl.multiple_of(r * block + place * half, half)
            out[:, r * half : (r + 1) * half] = context_ref[:, pl.ds(start, half)]


def column_halves(context, block):
    tokens, width = context.shape
    return pl.pallas_call(
        functools.partial(column_kernel, block),
        in_specs=[pl.BlockSpec(memory_space=pltpu.VMEM)],
        out_specs=[pl.BlockSpec(memory_space=pltpu.VMEM)] * 2,
        out_shape=[jax.ShapeDtypeStruct((tokens, width // 2), jnp.bfloat16)] * 2,
        compiler_params=pltpu.CompilerParams(vmem_limit_bytes=8 * MIB),
        cost_estimate=pl.CostEstimate(
            flops=0, bytes_accessed=4 * tokens * width, transcendentals=0
        ),
        name="column_halves",
    )(context)


def gradient_kernel(groups, ranks, sources, chunks, bands, table, *refs):
    pairs = groups // 2
    count = 1 + max(source for source, _ in sources)
    order = pair_order(pairs)
    ctxs, cots = [refs[order.index(k)] for k in range(pairs)], refs[pairs : count + pairs]
    outs, strips = refs[count + pairs : -1], refs[-1]
    slots = sum(chunks)
    rows = cots[0].shape[1]
    strip, part = outs[0].shape[1:]
    position, rank = lax.axis_index("fsdp"), lax.axis_index("tensor")
    rhs = jnp.concatenate([ctxs[k // 2][k % 2] for k in range(groups)], axis=0)
    for t in range(ranks):
        found = sources[t * groups : (t + 1) * groups]
        lhs = jnp.concatenate([cots[source][place] for source, place in found], axis=1)
        strips[pl.ds(t * rows, rows), :] = jnp.dot(
            lhs, rhs, preferred_element_type=jnp.float32
        ).astype(jnp.bfloat16)
    own_bands = bands // ranks
    offsets = offsets_of(groups)

    def place(first, pieces, s, carry):
        for k in range(groups):
            block_id = table[(position ^ offsets[k]) * slots + first + s]
            row_band, col_band = lax.div(block_id, bands), lax.rem(block_id, bands)
            piece = lax.div(col_band, own_bands) ^ rank
            start = piece * rows + lax.rem(col_band, own_bands) * strip
            pieces[k][s] = strips[
                pl.ds(pl.multiple_of(start, strip), strip),
                pl.ds(pl.multiple_of(row_band * part, part), part),
            ]
        return carry

    for i, count in enumerate(chunks):
        pieces = outs[i * groups : (i + 1) * groups]
        lax.fori_loop(0, count, functools.partial(place, sum(chunks[:i]), pieces), 0, unroll=4)


def gradient_strips(table, cots, ctxs, chunks, bands, block):
    ranks, pairs = len(cots), len(ctxs)
    groups = 2 * pairs
    sources, first = [], 0
    for own, *other in cots:
        places = [(first + 1 + i, n) for i, piece in enumerate(other) for n in range(piece.shape[0])]
        for pair in range(pairs):
            sources += [(first, pair), places[pair]]
        first += 1 + len(other)
    _, tokens, band_rows = ctxs[0].shape
    rows = cots[0][0].shape[1]
    strip, part = block // pairs, block // 2
    slots = sum(chunks)
    outs = pl.pallas_call(
        functools.partial(gradient_kernel, groups, ranks, sources, chunks, bands),
        grid_spec=pltpu.PrefetchScalarGridSpec(
            num_scalar_prefetch=1,
            grid=(),
            in_specs=[pl.BlockSpec(memory_space=pltpu.VMEM)] * (first + pairs),
            out_specs=[pl.BlockSpec(memory_space=pltpu.VMEM)] * (groups * len(chunks)),
            scratch_shapes=[pltpu.VMEM((ranks * rows, band_rows), jnp.bfloat16)],
        ),
        out_shape=[
            jax.ShapeDtypeStruct((count, strip, part), jnp.bfloat16)
            for count in chunks
            for _ in range(groups)
        ],
        compiler_params=pltpu.CompilerParams(vmem_limit_bytes=16 * MIB),
        cost_estimate=pl.CostEstimate(
            flops=2 * ranks * rows * groups * tokens * band_rows,
            bytes_accessed=2
            * groups
            * (ranks * rows * tokens + tokens * band_rows + slots * strip * part),
            transcendentals=0,
        ),
        name="gradient_strips",
    )(table, *[ctxs[k] for k in pair_order(pairs)], *[piece for rank in cots for piece in rank])
    return [outs[i * groups : (i + 1) * groups] for i in range(len(chunks))]


def gather_block(position, grads, slot, turned):
    for offset, piece in zip(offsets_of(len(grads)), grads):
        _, strip, part = piece.shape
        middle = position ^ offset
        rows = pl.ds(pl.multiple_of(lax.div(middle, 2) * strip, strip), strip)
        columns = pl.ds(pl.multiple_of(lax.rem(middle, 2) * part, part), part)
        turned[rows, columns] = piece[slot]


def direction_kernel(groups, halves, together, table, second_ref, left_ref, right_ref, *refs):
    grads, outs, turned, rows = refs[:groups], refs[groups : 2 * groups], refs[-2], refs[-1]
    position = lax.axis_index("fsdp")
    sub = outs[0].shape[1]
    for u in range(together):
        slot = pl.program_id(0) * together + u
        gather_block(position, grads, slot, turned.at[u])
        grad_bf16 = turned[u].T
        grad = grad_bf16.astype(jnp.float32)
        second = decay_rate * second_ref[0, u] + (1.0 - decay_rate) * grad * grad
        adam = grad / (jnp.sqrt(second) + 1e-08)
        half = jnp.dot(
            left_ref[0, u].astype(jnp.bfloat16), grad_bf16, preferred_element_type=jnp.float32
        )
        shaped = jnp.dot(
            half.astype(jnp.bfloat16),
            right_ref[0, u].astype(jnp.bfloat16),
            preferred_element_type=jnp.float32,
        )
        adam_sum = jnp.sum(adam * adam, keepdims=True)
        shaped_sum = jnp.sum(shaped * shaped, keepdims=True)
        ratio = jnp.sqrt(adam_sum) / jnp.sqrt(shaped_sum + 1e-06)
        rows[u] = (shaped * ratio).astype(jnp.bfloat16)
        for k, offset in enumerate(offsets_of(groups)):
            middle = position ^ offset
            side, quarter = lax.rem(middle, halves), lax.div(middle, halves)
            start = (side * (groups // halves) + quarter) * sub
            outs[k][slot] = rows[u, pl.ds(pl.multiple_of(start, sub), sub), :]


def directions(table, grads, first, second, root_left, root_right, halves, sub):
    groups = len(grads)
    slots = grads[0].shape[0]
    block = second.shape[-1]
    together = TOGETHER if slots % TOGETHER == 0 and first % TOGETHER == 0 else 1
    stat = pl.BlockSpec(
        (1, together, block, block), lambda s, table: (0, first // together + s, 0, 0)
    )
    whole = pl.BlockSpec(memory_space=pltpu.VMEM)
    return pl.pallas_call(
        functools.partial(direction_kernel, groups, halves, together),
        grid_spec=pltpu.PrefetchScalarGridSpec(
            num_scalar_prefetch=1,
            grid=(slots // together,),
            in_specs=[stat] * 3 + [whole] * groups,
            out_specs=[whole] * groups,
            scratch_shapes=[pltpu.VMEM((together, block, block), jnp.bfloat16)] * 2,
        ),
        out_shape=[jax.ShapeDtypeStruct((slots, sub, block), jnp.bfloat16)] * groups,
        compiler_params=pltpu.CompilerParams(vmem_limit_bytes=16 * MIB),
        cost_estimate=pl.CostEstimate(
            flops=4 * slots * block**3,
            bytes_accessed=16 * slots * block * block,
            transcendentals=0,
        ),
        name="directions",
    )(table, second, root_left, root_right, *grads)


def statistics_kernel(groups, chunks, table, left_ref, right_ref, second_ref, *refs):
    grads = refs[: groups * len(chunks)]
    left_out, right_out, second_out, turned = refs[groups * len(chunks) :]
    slot = pl.program_id(0)
    for i, count in enumerate(chunks):
        first = sum(chunks[:i])

        @pl.when(jnp.logical_and(slot >= first, slot < first + count))
        def _():
            pieces = grads[i * groups : (i + 1) * groups]
            gather_block(lax.axis_index("fsdp"), pieces, 0, turned)

    block = turned.shape[0]
    grad_t = turned[...]
    grad_bf16 = grad_t.T
    grad = grad_bf16.astype(jnp.float32)
    gram_left = jnp.dot(grad_bf16, grad_t, preferred_element_type=jnp.float32)
    gram_right = jnp.dot(grad_t, grad_bf16, preferred_element_type=jnp.float32)
    left_out[0, 0] = decay_rate * left_ref[0, 0] + (1.0 - decay_rate) * gram_left / block
    right_out[0, 0] = decay_rate * right_ref[0, 0] + (1.0 - decay_rate) * gram_right / block
    second_out[0, 0] = decay_rate * second_ref[0, 0] + (1.0 - decay_rate) * grad * grad


def statistics(table, grads, left_stat, right_stat, second):
    groups, chunks = len(grads[0]), [chunk[0].shape[0] for chunk in grads]
    _, strip, part = grads[0][0].shape
    block = second.shape[-1]
    slots = sum(chunks)
    stat = pl.BlockSpec((1, 1, block, block), lambda s, table: (0, s, 0, 0))

    def strip_spec(first, count):
        return pl.BlockSpec(
            (1, strip, part), lambda s, table: (jnp.clip(s - first, 0, count - 1), 0, 0)
        )

    strip_specs = [
        strip_spec(sum(chunks[:i]), count) for i, count in enumerate(chunks) for _ in range(groups)
    ]
    return pl.pallas_call(
        functools.partial(statistics_kernel, groups, chunks),
        grid_spec=pltpu.PrefetchScalarGridSpec(
            num_scalar_prefetch=1,
            grid=(slots,),
            in_specs=[stat] * 3 + strip_specs,
            out_specs=[stat] * 3,
            scratch_shapes=[pltpu.VMEM((block, block), jnp.bfloat16)],
        ),
        out_shape=[jax.ShapeDtypeStruct(left_stat.shape, jnp.float32)] * 3,
        compiler_params=pltpu.CompilerParams(vmem_limit_bytes=8 * MIB),
        cost_estimate=pl.CostEstimate(
            flops=4 * slots * block**3,
            bytes_accessed=26 * slots * block * block,
            transcendentals=0,
        ),
        name="statistics",
    )(table, left_stat, right_stat, second, *[piece for chunk in grads for piece in chunk])


def row_order(pairs):
    return [*reversed(range(pairs))]


def regroup_kernel(groups, chunks, bands, halves, table, *refs):
    inputs, outs, placed = refs[: groups * len(chunks)], refs[groups * len(chunks) : -1], refs[-1]
    block = inputs[0].shape[-1]
    position = lax.axis_index("fsdp")
    own_band = lax.div(position, halves)
    slots = sum(chunks)
    offsets = offsets_of(groups)

    def place(first, pieces, s, carry):
        for k in range(groups):
            block_id = table[(position ^ offsets[k]) * slots + first + s]
            row_band, col_band = lax.div(block_id, bands), lax.rem(block_id, bands)
            columns = pl.ds(pl.multiple_of(col_band * block, block), block)
            placed[row_band ^ own_band, :, columns] = pieces[k][s]
        return carry

    for i, count in enumerate(chunks):
        pieces = inputs[i * groups : (i + 1) * groups]
        lax.fori_loop(0, count, functools.partial(place, sum(chunks[:i]), pieces), 0, unroll=4)
    for k, out in zip(row_order(len(outs)), outs):
        out[...] = placed[k]


def regroup(table, pieces, bands, halves):
    groups, chunks = len(pieces[0]), [chunk[0].shape[0] for chunk in pieces]
    _, sub, block = pieces[0][0].shape
    row_bands = groups // halves
    return pl.pallas_call(
        functools.partial(regroup_kernel, groups, chunks, bands, halves),
        grid_spec=pltpu.PrefetchScalarGridSpec(
            num_scalar_prefetch=1,
            grid=(),
            in_specs=[pl.BlockSpec(memory_space=pltpu.VMEM)] * (groups * len(chunks)),
            out_specs=[pl.BlockSpec(memory_space=pltpu.VMEM)] * row_bands,
            scratch_shapes=[pltpu.VMEM((row_bands, sub, bands * block), jnp.bfloat16)],
        ),
        out_shape=[jax.ShapeDtypeStruct((sub, bands * block), jnp.bfloat16)] * row_bands,
        compiler_params=pltpu.CompilerParams(vmem_limit_bytes=8 * MIB),
        cost_estimate=pl.CostEstimate(
            flops=0,
            bytes_accessed=4 * row_bands * sub * bands * block,
            transcendentals=0,
        ),
        name="regroup",
    )(table, *[piece for chunk in pieces for piece in chunk])


def stack_kernel(halves, offsets, table, *refs):
    pieces, out, sems = refs[: len(offsets)], refs[-2], refs[-1]
    sub = pieces[0].shape[0]
    own_band = lax.div(lax.axis_index("fsdp"), halves)
    copies = []
    for i, (piece, k) in enumerate(zip(pieces, offsets)):
        start = pl.multiple_of((own_band ^ k) * sub, sub)
        copies.append(pltpu.make_async_copy(piece, out.at[0, pl.ds(start, sub), :], sems.at[i]))
    for copy in copies:
        copy.start()
    for copy in copies:
        copy.wait()


def stack_rows(table, pieces, offsets, halves, count, known=None):
    sub, width = pieces[0].shape
    anywhere = pl.BlockSpec(memory_space=pl.ANY)
    before = [] if known is None else [known]
    return pl.pallas_call(
        functools.partial(stack_kernel, halves, offsets),
        grid_spec=pltpu.PrefetchScalarGridSpec(
            num_scalar_prefetch=1,
            grid=(),
            in_specs=[pl.BlockSpec(memory_space=pltpu.VMEM)] * len(pieces)
            + [anywhere] * len(before),
            out_specs=anywhere,
            scratch_shapes=[pltpu.SemaphoreType.DMA((len(pieces),))],
        ),
        out_shape=jax.ShapeDtypeStruct((1, count * sub, width), jnp.bfloat16),
        input_output_aliases={len(pieces) + 1: 0} if before else {},
        compiler_params=pltpu.CompilerParams(vmem_limit_bytes=4 * MIB),
        cost_estimate=pl.CostEstimate(
            flops=0, bytes_accessed=4 * len(pieces) * sub * width, transcendentals=0
        ),
        name="stack_rows",
    )(table, *pieces, *before)


def exchange(pieces, offsets):
    return [swap(piece, "fsdp", k) if k else piece for piece, k in zip(pieces, offsets)]


def strip_plan(
    context, cotangent, block_table, left_stat, right_stat, root_left, root_right, second_moment
):
    groups, ranks = lax.axis_size("fsdp"), lax.axis_size("tensor")
    band_rows = context.shape[1]
    block, slots = left_stat.shape[-1], left_stat.shape[1]
    bands = cotangent.shape[1] * ranks // block
    strip_rows = band_rows // groups
    table = block_table[0]

    pairs, tokens = groups // 2, context.shape[0]
    offsets = offsets_of(groups)
    strips = cot_strips(cotangent, pairs, block)
    context, _ = lax.optimization_barrier((context, strips[0]))
    own, other = column_halves(context, block)
    strips = exchange(strips, range(0, groups, 2))
    other = swap(other, "fsdp", 1)
    strips, other = lax.optimization_barrier((strips, other))
    strips = jnp.stack(strips).reshape(pairs, -1, tokens)
    ctxs = [jnp.stack([own, other])] + [None] * (pairs - 1)
    far = pairs // 2
    ctxs[far] = swap(ctxs[0], "fsdp", 2 * far)
    step = 1
    while step < far:
        for k in range(step):
            ctxs[step + k] = swap(ctxs[k], "fsdp", 2 * step)
            ctxs[far + step + k] = swap(ctxs[far + k], "fsdp", 2 * step)
        step *= 2
    by_pair = swap(strips, "fsdp", 1)
    by_rank = swap(strips, "tensor", ranks // 2)
    to_rank, to_pair = by_pair[:far], by_rank[far:]
    to_rank, _ = lax.optimization_barrier((to_rank, ctxs[1]))
    across = [
        by_rank,
        swap(to_rank, "tensor", ranks // 2),
        swap(to_pair, "fsdp", 1),
    ]
    cots = {0: [strips, by_pair], ranks // 2: across}
    offset = ranks // 4
    while offset:
        for known in list(cots):
            here = list(cots[known])
            if known:
                here[0], _ = lax.optimization_barrier((here[0], here[1]))
            cots[known ^ offset] = [swap(piece, "tensor", offset) for piece in here]
        offset //= 2
    cots = [cots[t] for t in range(ranks)]

    chunks = [slots - slots // 2, slots // 2]
    grads = [
        exchange(chunk, offsets) for chunk in gradient_strips(table, cots, ctxs, chunks, bands, block)
    ]
    halves = block // strip_rows
    sub = strip_rows * halves // groups
    pieces = []
    for i, chunk in enumerate(grads):
        stale = (second_moment, root_left, root_right)
        parts = directions(table, chunk, sum(chunks[:i]), *stale, halves, sub)
        pieces.append(exchange(parts, offsets))
    left_new, right_new, second_new = statistics(
        table, grads, left_stat, right_stat, second_moment
    )
    order = row_order(pairs)
    rows = exchange(regroup(table, pieces, bands, halves), [k * halves for k in order])
    found = stack_rows(table, rows[1:], order[1:], halves, pairs)
    found = stack_rows(table, rows[:1], order[:1], halves, pairs, found)
    return (left_new, right_new, second_new, found)


def per_device(context, cotangent, block_table, left_stat, *rest):
    groups, ranks = lax.axis_size("fsdp"), lax.axis_size("tensor")
    block = left_stat.shape[-1]
    strip_rows = context.shape[1] // groups
    powers = groups & (groups - 1) == 0 and ranks & (ranks - 1) == 0
    whole = block % strip_rows == 0 and cotangent.shape[1] % block == 0
    even = block % (16 * groups) == 0 and block == 2 * strip_rows and groups >= 8
    plan = strip_plan if powers and even and whole else general_plan
    return plan(context, cotangent, block_table, left_stat, *rest)


def solution(mesh):
    return jax.shard_map(
        per_device,
        mesh=mesh,
        in_specs=(
            P("fsdp", "tensor"),
            P("fsdp", "tensor"),
            P("tensor", None),
            P("tensor", "fsdp", None, None),
            P("tensor", "fsdp", None, None),
            P("tensor", "fsdp", None, None),
            P("tensor", "fsdp", None, None),
            P("tensor", "fsdp", None, None),
        ),
        out_specs=(
            P("tensor", "fsdp", None, None),
            P("tensor", "fsdp", None, None),
            P("tensor", "fsdp", None, None),
            P("tensor", "fsdp", None),
        ),
        check_vma=False,
    )
```

```python
import functools

import jax
import jax.numpy as jnp
from jax import lax
from jax.experimental import pallas as pl
from jax.experimental.pallas import tpu as pltpu
from jax.sharding import PartitionSpec as P

decay_rate = 0.95
MIB = 1024 * 1024
TOGETHER = 4


def general_plan(
    context, cotangent, block_table, left_stat, right_stat, root_left, root_right, second_moment
):
    full_cot = lax.all_gather(cotangent, "tensor", axis=1, tiled=True)
    tokens_here, band_rows = context.shape
    model_width = full_cot.shape[1]
    block_size = left_stat.shape[-1]
    slot_count = left_stat.shape[1]
    groups = lax.axis_size("fsdp")
    position = lax.axis_index("fsdp")
    owner_table = block_table[0]
    col_bands = model_width // block_size
    strip_rows = band_rows // groups
    per_band = block_size // strip_rows
    my_blocks = lax.dynamic_slice_in_dim(owner_table, position * slot_count, slot_count)
    ctx_bands = context.reshape(tokens_here, band_rows // block_size, block_size)
    cot_bands = full_cot.reshape(tokens_here, col_bands, block_size)
    left_part = jnp.take(ctx_bands, owner_table // col_bands, axis=1)
    right_part = jnp.take(cot_bands, owner_table % col_bands, axis=1)
    blocks = jnp.einsum("tnb,tnc->nbc", left_part, right_part, preferred_element_type=jnp.float32)
    gradient = lax.psum_scatter(
        blocks.reshape(slot_count * block_size * lax.axis_size("fsdp"), block_size).astype(
            jnp.bfloat16
        ),
        "fsdp",
        scatter_dimension=0,
        tiled=True,
    ).astype(jnp.float32)
    gradient = gradient.reshape(slot_count, block_size, block_size)
    highest = lax.Precision.HIGHEST
    gram_left = jnp.einsum("sij,skj->sik", gradient, gradient, precision=highest)
    gram_right = jnp.einsum("sji,sjk->sik", gradient, gradient, precision=highest)
    left_new = decay_rate * left_stat[0] + (1.0 - decay_rate) * gram_left / block_size
    right_new = decay_rate * right_stat[0] + (1.0 - decay_rate) * gram_right / block_size
    second_new = decay_rate * second_moment[0] + (1.0 - decay_rate) * gradient * gradient
    adam_step = gradient / (jnp.sqrt(second_new) + 1e-08)
    shaped = jnp.einsum("sij,sjk->sik", root_left[0], gradient, precision=highest)
    shaped = jnp.einsum("sij,sjk->sik", shaped, root_right[0], precision=highest)
    graft_ratio = jnp.sqrt(jnp.sum(adam_step * adam_step, axis=(1, 2))) / jnp.sqrt(
        jnp.sum(shaped * shaped, axis=(1, 2)) + 1e-06
    )
    direction = (shaped * graft_ratio[:, None, None]).astype(jnp.bfloat16)
    by_strip = direction.reshape(slot_count, per_band, strip_rows, block_size)
    targets = jnp.arange(groups, dtype=jnp.int32)
    chosen = jnp.take(by_strip, targets % per_band, axis=1)
    keep_mask = ((my_blocks // col_bands)[:, None] == (targets // per_band)[None, :]).astype(
        jnp.bfloat16
    )
    outgoing_rows = jnp.swapaxes(chosen * keep_mask[:, :, None, None], 0, 1)
    returned = lax.all_to_all(outgoing_rows, "fsdp", split_axis=0, concat_axis=0, tiled=True)
    wanted = position // per_band * col_bands + jnp.arange(col_bands, dtype=jnp.int32)
    slot_ids = jnp.arange(owner_table.shape[0], dtype=jnp.int32)
    located = jnp.sum(
        jnp.where(owner_table[None, :] == wanted[:, None], slot_ids[None, :], 0), axis=1
    )
    flat_pieces = returned.reshape(groups * slot_count, strip_rows, block_size)
    pieces = jnp.take(flat_pieces, located, axis=0)
    result = jnp.swapaxes(pieces, 0, 1).reshape(strip_rows, model_width)
    return (left_new[None], right_new[None], second_new[None], result[None])


def swap(value, axis, offset):
    count = lax.axis_size(axis)
    return lax.ppermute(value, axis, [(i, i ^ offset) for i in range(count)])


def offsets_of(groups):
    far, near = range(groups // 2, groups), range(1, groups // 2)
    order = [k for pair in zip(far, near) for k in pair]
    return [*order, groups - 1, 0]


def pair_order(pairs):
    return [pairs // 2, 0, *[k for k in range(1, pairs) if k != pairs // 2]]


def strip_kernel(pairs, cot_ref, *refs):
    outs, turned = refs[:pairs], refs[pairs]
    strip = turned.shape[0] // pairs
    pair = lax.div(lax.axis_index("fsdp"), 2)
    turned[...] = cot_ref[...].T
    for k, out in zip(row_order(pairs), outs):
        start = pl.multiple_of((pair ^ k) * strip, strip)
        out[0] = turned[pl.ds(start, strip), :]


def cot_strips(cotangent, pairs, block):
    tokens, width = cotangent.shape
    bands, strip = width // block, block // pairs
    return pl.pallas_call(
        functools.partial(strip_kernel, pairs),
        grid=(bands,),
        in_specs=[pl.BlockSpec((tokens, block), lambda c: (0, c))],
        out_specs=[pl.BlockSpec((1, strip, tokens), lambda c: (c, 0, 0))] * pairs,
        scratch_shapes=[pltpu.VMEM((block, tokens), jnp.bfloat16)],
        out_shape=[jax.ShapeDtypeStruct((bands, strip, tokens), jnp.bfloat16)] * pairs,
        compiler_params=pltpu.CompilerParams(vmem_limit_bytes=8 * MIB),
        cost_estimate=pl.CostEstimate(
            flops=0, bytes_accessed=4 * tokens * width, transcendentals=0
        ),
        name="cot_strips",
    )(cotangent)


def column_kernel(block, context_ref, own, other):
    half = block // 2
    side = lax.rem(lax.axis_index("fsdp"), 2)
    for out, place in ((own, side), (other, side ^ 1)):
        for r in range(out.shape[1] // half):
            start = pl.multiple_of(r * block + place * half, half)
            out[:, r * half : (r + 1) * half] = context_ref[:, pl.ds(start, half)]


def column_halves(context, block):
    tokens, width = context.shape
    return pl.pallas_call(
        functools.partial(column_kernel, block),
        in_specs=[pl.BlockSpec(memory_space=pltpu.VMEM)],
        out_specs=[pl.BlockSpec(memory_space=pltpu.VMEM)] * 2,
        out_shape=[jax.ShapeDtypeStruct((tokens, width // 2), jnp.bfloat16)] * 2,
        compiler_params=pltpu.CompilerParams(vmem_limit_bytes=8 * MIB),
        cost_estimate=pl.CostEstimate(
            flops=0, bytes_accessed=4 * tokens * width, transcendentals=0
        ),
        name="column_halves",
    )(context)


def gradient_kernel(groups, ranks, sources, chunks, bands, table, *refs):
    pairs = groups // 2
    count = 1 + max(source for source, _ in sources)
    order = pair_order(pairs)
    ctxs, cots = [refs[order.index(k)] for k in range(pairs)], refs[pairs : count + pairs]
    outs, strips = refs[count + pairs : -1], refs[-1]
    slots = sum(chunks)
    rows = cots[0].shape[1]
    strip, part = outs[0].shape[1:]
    position, rank = lax.axis_index("fsdp"), lax.axis_index("tensor")
    rhs = jnp.concatenate([ctxs[k // 2][k % 2] for k in range(groups)], axis=0)
    for t in range(ranks):
        found = sources[t * groups : (t + 1) * groups]
        lhs = jnp.concatenate([cots[source][place] for source, place in found], axis=1)
        strips[pl.ds(t * rows, rows), :] = jnp.dot(
            lhs, rhs, preferred_element_type=jnp.float32
        ).astype(jnp.bfloat16)
    own_bands = bands // ranks
    offsets = offsets_of(groups)

    def place(first, pieces, s, carry):
        for k in range(groups):
            block_id = table[(position ^ offsets[k]) * slots + first + s]
            row_band, col_band = lax.div(block_id, bands), lax.rem(block_id, bands)
            piece = lax.div(col_band, own_bands) ^ rank
            start = piece * rows + lax.rem(col_band, own_bands) * strip
            pieces[k][s] = strips[
                pl.ds(pl.multiple_of(start, strip), strip),
                pl.ds(pl.multiple_of(row_band * part, part), part),
            ]
        return carry

    for i, count in enumerate(chunks):
        pieces = outs[i * groups : (i + 1) * groups]
        lax.fori_loop(0, count, functools.partial(place, sum(chunks[:i]), pieces), 0, unroll=4)


def gradient_strips(table, cots, ctxs, chunks, bands, block):
    ranks, pairs = len(cots), len(ctxs)
    groups = 2 * pairs
    sources, first = [], 0
    for own, *other in cots:
        places = [(first + 1 + i, n) for i, piece in enumerate(other) for n in range(piece.shape[0])]
        for pair in range(pairs):
            sources += [(first, pair), places[pair]]
        first += 1 + len(other)
    _, tokens, band_rows = ctxs[0].shape
    rows = cots[0][0].shape[1]
    strip, part = block // pairs, block // 2
    slots = sum(chunks)
    outs = pl.pallas_call(
        functools.partial(gradient_kernel, groups, ranks, sources, chunks, bands),
        grid_spec=pltpu.PrefetchScalarGridSpec(
            num_scalar_prefetch=1,
            grid=(),
            in_specs=[pl.BlockSpec(memory_space=pltpu.VMEM)] * (first + pairs),
            out_specs=[pl.BlockSpec(memory_space=pltpu.VMEM)] * (groups * len(chunks)),
            scratch_shapes=[pltpu.VMEM((ranks * rows, band_rows), jnp.bfloat16)],
        ),
        out_shape=[
            jax.ShapeDtypeStruct((count, strip, part), jnp.bfloat16)
            for count in chunks
            for _ in range(groups)
        ],
        compiler_params=pltpu.CompilerParams(vmem_limit_bytes=16 * MIB),
        cost_estimate=pl.CostEstimate(
            flops=2 * ranks * rows * groups * tokens * band_rows,
            bytes_accessed=2
            * groups
            * (ranks * rows * tokens + tokens * band_rows + slots * strip * part),
            transcendentals=0,
        ),
        name="gradient_strips",
    )(table, *[ctxs[k] for k in pair_order(pairs)], *[piece for rank in cots for piece in rank])
    return [outs[i * groups : (i + 1) * groups] for i in range(len(chunks))]


def gather_block(position, grads, slot, turned):
    for offset, piece in zip(offsets_of(len(grads)), grads):
        _, strip, part = piece.shape
        middle = position ^ offset
        rows = pl.ds(pl.multiple_of(lax.div(middle, 2) * strip, strip), strip)
        columns = pl.ds(pl.multiple_of(lax.rem(middle, 2) * part, part), part)
        turned[rows, columns] = piece[slot]


def direction_kernel(groups, halves, together, table, second_ref, left_ref, right_ref, *refs):
    grads, outs, turned, rows = refs[:groups], refs[groups : 2 * groups], refs[-2], refs[-1]
    position = lax.axis_index("fsdp")
    sub = outs[0].shape[1]
    for u in range(together):
        slot = pl.program_id(0) * together + u
        gather_block(position, grads, slot, turned.at[u])
        grad_bf16 = turned[u].T
        grad = grad_bf16.astype(jnp.float32)
        second = decay_rate * second_ref[0, u] + (1.0 - decay_rate) * grad * grad
        adam = grad / (jnp.sqrt(second) + 1e-08)
        half = jnp.dot(
            left_ref[0, u].astype(jnp.bfloat16), grad_bf16, preferred_element_type=jnp.float32
        )
        shaped = jnp.dot(
            half.astype(jnp.bfloat16),
            right_ref[0, u].astype(jnp.bfloat16),
            preferred_element_type=jnp.float32,
        )
        adam_sum = jnp.sum(adam * adam, keepdims=True)
        shaped_sum = jnp.sum(shaped * shaped, keepdims=True)
        ratio = jnp.sqrt(adam_sum) / jnp.sqrt(shaped_sum + 1e-06)
        rows[u] = (shaped * ratio).astype(jnp.bfloat16)
        for k, offset in enumerate(offsets_of(groups)):
            middle = position ^ offset
            side, quarter = lax.rem(middle, halves), lax.div(middle, halves)
            start = (side * (groups // halves) + quarter) * sub
            outs[k][slot] = rows[u, pl.ds(pl.multiple_of(start, sub), sub), :]


def directions(table, grads, first, second, root_left, root_right, halves, sub):
    groups = len(grads)
    slots = grads[0].shape[0]
    block = second.shape[-1]
    together = TOGETHER if slots % TOGETHER == 0 and first % TOGETHER == 0 else 1
    stat = pl.BlockSpec(
        (1, together, block, block), lambda s, table: (0, first // together + s, 0, 0)
    )
    whole = pl.BlockSpec(memory_space=pltpu.VMEM)
    return pl.pallas_call(
        functools.partial(direction_kernel, groups, halves, together),
        grid_spec=pltpu.PrefetchScalarGridSpec(
            num_scalar_prefetch=1,
            grid=(slots // together,),
            in_specs=[stat] * 3 + [whole] * groups,
            out_specs=[whole] * groups,
            scratch_shapes=[pltpu.VMEM((together, block, block), jnp.bfloat16)] * 2,
        ),
        out_shape=[jax.ShapeDtypeStruct((slots, sub, block), jnp.bfloat16)] * groups,
        compiler_params=pltpu.CompilerParams(vmem_limit_bytes=16 * MIB),
        cost_estimate=pl.CostEstimate(
            flops=4 * slots * block**3,
            bytes_accessed=16 * slots * block * block,
            transcendentals=0,
        ),
        name="directions",
    )(table, second, root_left, root_right, *grads)


def statistics_kernel(groups, chunks, table, left_ref, right_ref, second_ref, *refs):
    grads = refs[: groups * len(chunks)]
    left_out, right_out, second_out, turned = refs[groups * len(chunks) :]
    slot = pl.program_id(0)
    for i, count in enumerate(chunks):
        first = sum(chunks[:i])

        @pl.when(jnp.logical_and(slot >= first, slot < first + count))
        def _():
            pieces = grads[i * groups : (i + 1) * groups]
            gather_block(lax.axis_index("fsdp"), pieces, 0, turned)

    block = turned.shape[0]
    grad_t = turned[...]
    grad_bf16 = grad_t.T
    grad = grad_bf16.astype(jnp.float32)
    gram_left = jnp.dot(grad_bf16, grad_t, preferred_element_type=jnp.float32)
    gram_right = jnp.dot(grad_t, grad_bf16, preferred_element_type=jnp.float32)
    left_out[0, 0] = decay_rate * left_ref[0, 0] + (1.0 - decay_rate) * gram_left / block
    right_out[0, 0] = decay_rate * right_ref[0, 0] + (1.0 - decay_rate) * gram_right / block
    second_out[0, 0] = decay_rate * second_ref[0, 0] + (1.0 - decay_rate) * grad * grad


def statistics(table, grads, left_stat, right_stat, second):
    groups, chunks = len(grads[0]), [chunk[0].shape[0] for chunk in grads]
    _, strip, part = grads[0][0].shape
    block = second.shape[-1]
    slots = sum(chunks)
    stat = pl.BlockSpec((1, 1, block, block), lambda s, table: (0, s, 0, 0))

    def strip_spec(first, count):
        return pl.BlockSpec(
            (1, strip, part), lambda s, table: (jnp.clip(s - first, 0, count - 1), 0, 0)
        )

    strip_specs = [
        strip_spec(sum(chunks[:i]), count) for i, count in enumerate(chunks) for _ in range(groups)
    ]
    return pl.pallas_call(
        functools.partial(statistics_kernel, groups, chunks),
        grid_spec=pltpu.PrefetchScalarGridSpec(
            num_scalar_prefetch=1,
            grid=(slots,),
            in_specs=[stat] * 3 + strip_specs,
            out_specs=[stat] * 3,
            scratch_shapes=[pltpu.VMEM((block, block), jnp.bfloat16)],
        ),
        out_shape=[jax.ShapeDtypeStruct(left_stat.shape, jnp.float32)] * 3,
        compiler_params=pltpu.CompilerParams(vmem_limit_bytes=8 * MIB),
        cost_estimate=pl.CostEstimate(
            flops=4 * slots * block**3,
            bytes_accessed=26 * slots * block * block,
            transcendentals=0,
        ),
        name="statistics",
    )(table, left_stat, right_stat, second, *[piece for chunk in grads for piece in chunk])


def row_order(pairs):
    return [*reversed(range(pairs))]


def regroup_kernel(groups, chunks, bands, halves, table, *refs):
    inputs, outs, placed = refs[: groups * len(chunks)], refs[groups * len(chunks) : -1], refs[-1]
    block = inputs[0].shape[-1]
    position = lax.axis_index("fsdp")
    own_band = lax.div(position, halves)
    slots = sum(chunks)
    offsets = offsets_of(groups)

    def place(first, pieces, s, carry):
        for k in range(groups):
            block_id = table[(position ^ offsets[k]) * slots + first + s]
            row_band, col_band = lax.div(block_id, bands), lax.rem(block_id, bands)
            columns = pl.ds(pl.multiple_of(col_band * block, block), block)
            placed[row_band ^ own_band, :, columns] = pieces[k][s]
        return carry

    for i, count in enumerate(chunks):
        pieces = inputs[i * groups : (i + 1) * groups]
        lax.fori_loop(0, count, functools.partial(place, sum(chunks[:i]), pieces), 0, unroll=4)
    for k, out in zip(row_order(len(outs)), outs):
        out[...] = placed[k]


def regroup(table, pieces, bands, halves):
    groups, chunks = len(pieces[0]), [chunk[0].shape[0] for chunk in pieces]
    _, sub, block = pieces[0][0].shape
    row_bands = groups // halves
    return pl.pallas_call(
        functools.partial(regroup_kernel, groups, chunks, bands, halves),
        grid_spec=pltpu.PrefetchScalarGridSpec(
            num_scalar_prefetch=1,
            grid=(),
            in_specs=[pl.BlockSpec(memory_space=pltpu.VMEM)] * (groups * len(chunks)),
            out_specs=[pl.BlockSpec(memory_space=pltpu.VMEM)] * row_bands,
            scratch_shapes=[pltpu.VMEM((row_bands, sub, bands * block), jnp.bfloat16)],
        ),
        out_shape=[jax.ShapeDtypeStruct((sub, bands * block), jnp.bfloat16)] * row_bands,
        compiler_params=pltpu.CompilerParams(vmem_limit_bytes=8 * MIB),
        cost_estimate=pl.CostEstimate(
            flops=0,
            bytes_accessed=4 * row_bands * sub * bands * block,
            transcendentals=0,
        ),
        name="regroup",
    )(table, *[piece for chunk in pieces for piece in chunk])


def stack_kernel(halves, offsets, table, *refs):
    pieces, out, sems = refs[: len(offsets)], refs[-2], refs[-1]
    sub = pieces[0].shape[0]
    own_band = lax.div(lax.axis_index("fsdp"), halves)
    copies = []
    for i, (piece, k) in enumerate(zip(pieces, offsets)):
        start = pl.multiple_of((own_band ^ k) * sub, sub)
        copies.append(pltpu.make_async_copy(piece, out.at[0, pl.ds(start, sub), :], sems.at[i]))
    for copy in copies:
        copy.start()
    for copy in copies:
        copy.wait()


def stack_rows(table, pieces, offsets, halves, count, known=None):
    sub, width = pieces[0].shape
    anywhere = pl.BlockSpec(memory_space=pl.ANY)
    before = [] if known is None else [known]
    return pl.pallas_call(
        functools.partial(stack_kernel, halves, offsets),
        grid_spec=pltpu.PrefetchScalarGridSpec(
            num_scalar_prefetch=1,
            grid=(),
            in_specs=[pl.BlockSpec(memory_space=pltpu.VMEM)] * len(pieces)
            + [anywhere] * len(before),
            out_specs=anywhere,
            scratch_shapes=[pltpu.SemaphoreType.DMA((len(pieces),))],
        ),
        out_shape=jax.ShapeDtypeStruct((1, count * sub, width), jnp.bfloat16),
        input_output_aliases={len(pieces) + 1: 0} if before else {},
        compiler_params=pltpu.CompilerParams(vmem_limit_bytes=4 * MIB),
        cost_estimate=pl.CostEstimate(
            flops=0, bytes_accessed=4 * len(pieces) * sub * width, transcendentals=0
        ),
        name="stack_rows",
    )(table, *pieces, *before)


def exchange(pieces, offsets):
    return [swap(piece, "fsdp", k) if k else piece for piece, k in zip(pieces, offsets)]


def strip_plan(
    context, cotangent, block_table, left_stat, right_stat, root_left, root_right, second_moment
):
    groups, ranks = lax.axis_size("fsdp"), lax.axis_size("tensor")
    band_rows = context.shape[1]
    block, slots = left_stat.shape[-1], left_stat.shape[1]
    bands = cotangent.shape[1] * ranks // block
    strip_rows = band_rows // groups
    table = block_table[0]

    pairs, tokens = groups // 2, context.shape[0]
    offsets = offsets_of(groups)
    strips = cot_strips(cotangent, pairs, block)
    context, _ = lax.optimization_barrier((context, strips[0]))
    own, other = column_halves(context, block)
    strips = exchange(strips, [2 * k for k in row_order(pairs)])[::-1]
    other = swap(other, "fsdp", 1)
    strips, other = lax.optimization_barrier((strips, other))
    strips = jnp.stack(strips).reshape(pairs, -1, tokens)
    ctxs = [jnp.stack([own, other])] + [None] * (pairs - 1)
    far = pairs // 2
    ctxs[far] = swap(ctxs[0], "fsdp", 2 * far)
    step = 1
    while step < far:
        for k in range(step):
            ctxs[step + k] = swap(ctxs[k], "fsdp", 2 * step)
            ctxs[far + step + k] = swap(ctxs[far + k], "fsdp", 2 * step)
        step *= 2
    by_pair = swap(strips, "fsdp", 1)
    by_rank = swap(strips, "tensor", ranks // 2)
    to_rank, to_pair = by_pair[:far], by_rank[far:]
    to_rank, _ = lax.optimization_barrier((to_rank, ctxs[1]))
    across = [
        by_rank,
        swap(to_rank, "tensor", ranks // 2),
        swap(to_pair, "fsdp", 1),
    ]
    cots = {0: [strips, by_pair], ranks // 2: across}
    offset = ranks // 4
    while offset:
        for known in list(cots):
            here = list(cots[known])
            if known:
                here[0], _ = lax.optimization_barrier((here[0], here[1]))
            cots[known ^ offset] = [swap(piece, "tensor", offset) for piece in here]
        offset //= 2
    cots = [cots[t] for t in range(ranks)]

    chunks = [slots - slots // 2, slots // 2]
    grads = [
        exchange(chunk, offsets) for chunk in gradient_strips(table, cots, ctxs, chunks, bands, block)
    ]
    halves = block // strip_rows
    sub = strip_rows * halves // groups
    pieces = []
    for i, chunk in enumerate(grads):
        stale = (second_moment, root_left, root_right)
        parts = directions(table, chunk, sum(chunks[:i]), *stale, halves, sub)
        pieces.append(exchange(parts, offsets))
    left_new, right_new, second_new = statistics(
        table, grads, left_stat, right_stat, second_moment
    )
    order = row_order(pairs)
    rows = exchange(regroup(table, pieces, bands, halves), [k * halves for k in order])
    found = stack_rows(table, rows[1:], order[1:], halves, pairs)
    found = stack_rows(table, rows[:1], order[:1], halves, pairs, found)
    return (left_new, right_new, second_new, found)


def per_device(context, cotangent, block_table, left_stat, *rest):
    groups, ranks = lax.axis_size("fsdp"), lax.axis_size("tensor")
    block = left_stat.shape[-1]
    strip_rows = context.shape[1] // groups
    powers = groups & (groups - 1) == 0 and ranks & (ranks - 1) == 0
    whole = block % strip_rows == 0 and cotangent.shape[1] % block == 0
    even = block % (16 * groups) == 0 and block == 2 * strip_rows and groups >= 8
    plan = strip_plan if powers and even and whole else general_plan
    return plan(context, cotangent, block_table, left_stat, *rest)


def solution(mesh):
    return jax.shard_map(
        per_device,
        mesh=mesh,
        in_specs=(
            P("fsdp", "tensor"),
            P("fsdp", "tensor"),
            P("tensor", None),
            P("tensor", "fsdp", None, None),
            P("tensor", "fsdp", None, None),
            P("tensor", "fsdp", None, None),
            P("tensor", "fsdp", None, None),
            P("tensor", "fsdp", None, None),
        ),
        out_specs=(
            P("tensor", "fsdp", None, None),
            P("tensor", "fsdp", None, None),
            P("tensor", "fsdp", None, None),
            P("tensor", "fsdp", None),
        ),
        check_vma=False,
    )
```
